128 devices in a mesh: ty: 16 (over x, y), tx: 8 (over z, core).
Axes of the slice: x: 4, y: 4, z: 4, core: 2. Of those that a mesh axis runs over, the one named last changes fastest.
Arguments:
- tracers: float32 [3, 60, 256, 2048], P(None, None, 'ty', 'tx'), may hold values from -6 to 6
- courant: float32 [2, 60, 256, 2048], P(None, None, 'ty', 'tx'), may hold values from -0.5 to 0.5
- depth_levels: int32 [256, 2048], P('ty', 'tx'), may hold values from 0 to 60
- mix_inverse: bfloat16 [4, 15, 15, 256, 2048], P(None, None, None, 'ty', 'tx'), may hold values from 0 to 1
- to_ocean: bfloat16 [5, 128, 256, 2048], P(None, None, 'ty', 'tx'), may hold values from -0.3125 to 0.3125
- to_atmos: bfloat16 [5, 128, 256, 2048], P(None, None, 'ty', 'tx'), may hold values from -0.09375 to 0.09375
- atm_flux: bfloat16 [3, 64, 1024], P(None, 'ty', 'tx'), may hold values from -6 to 6
- peer_list: int32 [16, 8, 5], P('ty', 'tx'), may hold values from 0 to 127, as said below
- peer_count: int32 [16, 8, 5], P('ty', 'tx'), may hold values from 1 to 128, as said below
- send_count: int32 [16, 8, 128], P('ty', 'tx'), may hold values from 0 to 128, as said below
- slot_cell: int32 [16, 8, 128, 128], P('ty', 'tx'), may hold values from 0 to 511, as said below
Outputs:
- tracers_out: float32 [3, 60, 256, 2048], P(None, None, 'ty', 'tx')
- surface_temp: float32 [64, 1024], P('ty', 'tx')
The draws below stay inside these ranges and needn't reach their ends.
Inputs may be any that keep to these rules, and one draw needn't show every extreme that they name: `peer_list`: entry 0 of device d is d itself; entries 1 and 2 are the devices of the same ty index whose tx index is one more and one less, modulo 8; entry 3 is a device of the next ty index and entry 4 one of the previous ty index, both modulo 16, whose tx index differs from d's by 1 or 0 modulo 8. `peer_count`: the largest value, 128, occurs in every draw. send_count[e, d] equals peer_count[d, p] where peer_list[d, p] = e, and 0 where e is not among d's peers. `slot_cell`: slots at or beyond the count hold arbitrary valid cells; a cell may appear in several slots.
All inputs are finite; a program needn't handle non-finite values.
Results may differ from the reference program's by a relative error of at most 0.014.
Values may be sent and summed in bfloat16 or wider, within the bound.
A program may use at most 256 MiB of HBM per device.

```python
import jax
import jax.numpy as jnp
from jax import lax

NTR = 3
NB = 4
ZB = 15
LEVELS = 60
OY = 16
OX = 256
AYD = 4
AXD = 128
P_SIZE = 5
S = 128
SUBSTEPS = 2
NY = 256
NX = 2048
AY = 64
AX = 1024
N_TY = 16
N_TX = 8
DEVICES = 128


def peer_graph(key):
    offset_key = jax.random.fold_in(key, 55)
    lower_key = jax.random.fold_in(key, 56)
    device_ids = jnp.arange(DEVICES, dtype=jnp.int32)
    row_ids = device_ids // N_TX
    col_ids = device_ids % N_TX
    east_ids = row_ids * N_TX + (col_ids + 1) % N_TX
    west_ids = row_ids * N_TX + (col_ids + N_TX - 1) % N_TX
    upper_rows = (row_ids + 1) % N_TY
    lower_rows = (row_ids + N_TY - 1) % N_TY
    upper_offsets = jax.random.randint(offset_key, (DEVICES,), -1, 2, dtype=jnp.int32)
    lower_offsets = jax.random.randint(lower_key, (DEVICES,), -1, 2, dtype=jnp.int32)
    upper_ids = upper_rows * N_TX + (col_ids + upper_offsets + N_TX) % N_TX
    lower_ids = lower_rows * N_TX + (col_ids + lower_offsets + N_TX) % N_TX
    peer_ids = jnp.stack([device_ids, east_ids, west_ids, upper_ids, lower_ids], axis=1).astype(jnp.int32)
    count_key = jax.random.fold_in(key, 101)
    counts = jax.random.randint(count_key, (DEVICES, P_SIZE), 1, S + 1, dtype=jnp.int32)
    dest_ids = device_ids[:, None]
    column = jnp.arange(P_SIZE, dtype=jnp.int32)[None, :]
    counts = jnp.where((dest_ids % 5 == 0) & (column == 0), jnp.int32(S), counts)
    return (peer_ids, counts)


def draw_peer_list(key, part):
    peer_ids, counts = peer_graph(key)
    return peer_ids.reshape(N_TY, N_TX, P_SIZE)


def draw_peer_count(key, part):
    peer_ids, counts = peer_graph(key)
    return counts.reshape(N_TY, N_TX, P_SIZE)


def draw_send_count(key, part):
    peer_ids, counts = peer_graph(key)
    source_ids = jnp.arange(DEVICES, dtype=jnp.int32)
    matches = (peer_ids[:, :, None] == source_ids[None, None, :]).astype(jnp.int32)
    totals = jnp.sum(matches * counts[:, :, None], axis=1)
    return totals.T.reshape(N_TY, N_TX, DEVICES)


def draw_slot_cell(key, part):
    key = jax.random.fold_in(key, 4)
    return jax.random.randint(key, (N_TY, N_TX, DEVICES, S), 0, AYD * AXD, dtype=jnp.int32)


def draw_mix_inverse(key, part):
    key = jax.random.fold_in(key, 7)
    first_key, second_key = jax.random.split(key)
    spread = 0.8
    shape = (NB, ZB, ZB, NY, NX)
    offdiag = jax.random.uniform(first_key, shape, jnp.float32, 0.0, spread / ZB)
    diagonal = jax.random.uniform(second_key, (NB, ZB, NY, NX), jnp.float32, 0.6, 1.0)
    identity = (jnp.arange(ZB)[:, None] == jnp.arange(ZB)[None, :]).astype(jnp.float32)[None, :, :, None, None]
    return (offdiag * (1.0 - identity) + identity * diagonal[:, :, None]).astype(jnp.bfloat16)


def plant(values, stream_key, smallest, largest):
    extent = values.shape
    place = [jax.random.randint(jax.random.fold_in(stream_key, axis), (), 0, extent[axis]) for axis in range(len(extent))]
    values = values.at[tuple(place)].set(smallest)
    longest = extent.index(max(extent))
    place[longest] = (place[longest] + 1) % extent[longest]
    return values.at[tuple(place)].set(largest)


def steps_of(stream_key, extent, cuts, low, high):
    def one(axis_at, shards_of):
        steps = jax.random.uniform(jax.random.fold_in(jax.random.fold_in(stream_key, 6), axis_at), (shards_of,), jnp.float32, low / len(cuts), high / len(cuts))
        return jnp.repeat(jnp.exp(steps), extent[axis_at] // shards_of).reshape((-1,) + (1,) * (len(extent) - axis_at - 1))

    factor_of = one(*cuts[0])
    for cut in cuts[1:]:
        factor_of = factor_of * one(*cut)
    return factor_of


def normal_values(stream_key, dims, scale, most, cuts=(), kind=jnp.bfloat16):
    drawn = jax.random.normal(stream_key, dims, jnp.float32) * scale
    if len(cuts) > 0:
        drawn = steps_of(stream_key, dims, cuts, -0.22, 0.18) * drawn
    return jnp.clip(drawn, min=-most, max=most).astype(kind)


def setup_inputs(seed: int = 0) -> dict:
    key_of = jax.random.split(jax.random.key(seed), 12)
    return {
        "tracers": normal_values(key_of[0], (NTR, LEVELS, NY, NX), 1.0, 6.0, ((2, 16), (3, 8)), jnp.float32),
        "courant": jnp.clip(jax.random.uniform(key_of[1], (2, LEVELS, NY, NX), jnp.float32, -0.5, 0.5) * steps_of(key_of[1], (2, LEVELS, NY, NX), ((2, 16), (3, 8)), -0.4, 0.0), -0.5, 0.5),
        "depth_levels": plant(jax.random.randint(key_of[2], (NY, NX), 0, LEVELS + 1), jax.random.fold_in(key_of[2], 1), 0, LEVELS).astype(jnp.int32),
        "mix_inverse": draw_mix_inverse(jax.random.fold_in(key_of[11], 71), 0),
        "to_ocean": normal_values(key_of[4], (P_SIZE, S, NY, NX), (P_SIZE * S // 2) ** -0.5, 0.3125, ((2, 16), (3, 8))),
        "to_atmos": normal_values(key_of[5], (P_SIZE, S, NY, NX), (OY * OX) ** -0.5, 0.09375, ((2, 16), (3, 8))),
        "atm_flux": normal_values(key_of[6], (NTR, AY, AX), 1.0, 6.0, ((1, 16), (2, 8))),
        "peer_list": draw_peer_list(jax.random.fold_in(key_of[11], 71), 0),
        "peer_count": draw_peer_count(jax.random.fold_in(key_of[11], 71), 0),
        "send_count": draw_send_count(jax.random.fold_in(key_of[11], 71), 0),
        "slot_cell": draw_slot_cell(jax.random.fold_in(key_of[11], 71), 0),
    }


def wet_levels(depth_levels, levels):
    level_index = jnp.arange(levels, dtype=jnp.int32)[:, None, None]
    return (level_index < depth_levels[None, :, :]).astype(jnp.float32)


def advect(padded_tracers, padded_flow):
    row_count = padded_tracers.shape[2] - 4
    col_count = padded_tracers.shape[3] - 4
    east_courant = padded_flow[0]
    north_courant = padded_flow[1]
    wet_mask = padded_flow[2]
    middle_rows = padded_tracers[:, :, 2:row_count + 2, :]
    open_east = wet_mask[:, 2:row_count + 2, 1:col_count + 2] * wet_mask[:, 2:row_count + 2, 2:col_count + 3]
    face_east = 0.5 * (east_courant[:, 2:row_count + 2, 1:col_count + 2] + east_courant[:, 2:row_count + 2, 2:col_count + 3]) * open_east
    flux_east = face_east * (7.0 * (middle_rows[..., 1:col_count + 2] + middle_rows[..., 2:col_count + 3]) - (middle_rows[..., 0:col_count + 1] + middle_rows[..., 3:col_count + 4])) / 12.0
    middle_cols = padded_tracers[:, :, :, 2:col_count + 2]
    open_north = wet_mask[:, 1:row_count + 2, 2:col_count + 2] * wet_mask[:, 2:row_count + 3, 2:col_count + 2]
    face_north = 0.5 * (north_courant[:, 1:row_count + 2, 2:col_count + 2] + north_courant[:, 2:row_count + 3, 2:col_count + 2]) * open_north
    flux_north = face_north * (7.0 * (middle_cols[:, :, 1:row_count + 2] + middle_cols[:, :, 2:row_count + 3]) - (middle_cols[:, :, 0:row_count + 1] + middle_cols[:, :, 3:row_count + 4])) / 12.0
    centre = padded_tracers[:, :, 2:row_count + 2, 2:col_count + 2]
    return centre - (flux_east[..., 1:] - flux_east[..., :-1]) - (flux_north[:, :, 1:] - flux_north[:, :, :-1])


def mix_columns(fields, mix_inverse):
    tracer_count, levels, row_count, col_count = fields.shape
    blocks = mix_inverse.shape[0]
    block_width = mix_inverse.shape[1]
    stacked = fields.reshape(tracer_count, blocks, block_width, row_count, col_count)
    running = jnp.zeros((tracer_count, blocks, block_width, row_count, col_count), jnp.float32)
    for column_index in range(block_width):
        running = running + mix_inverse[:, :, column_index].astype(jnp.float32)[None] * stacked[:, :, column_index][:, :, None]
    return running.reshape(tracer_count, levels, row_count, col_count)


def substep(padded_tracers, padded_flow, forcing, wet_mask, mix_inverse):
    advected = advect(padded_tracers, padded_flow)
    advected = advected.at[:, 0].add(forcing)
    advected = advected * wet_mask[None]
    return mix_columns(advected, mix_inverse) * wet_mask[None]


def reference(tracers, courant, depth_levels, mix_inverse, to_ocean, to_atmos, atm_flux, peer_list, peer_count, send_count, slot_cell):
    wet_mask = wet_levels(depth_levels, LEVELS)
    flow_fields = jnp.concatenate([courant, wet_mask[None]], axis=0)
    padded_flow = jnp.pad(flow_fields, ((0, 0), (0, 0), (2, 2), (2, 2)))
    atm_cells = AYD * AXD
    atm_flat = atm_flux.reshape(NTR, N_TY, AYD, N_TX, AXD).transpose(1, 3, 0, 2, 4).reshape(DEVICES, NTR, atm_cells)
    peer_ids = peer_list.reshape(DEVICES, P_SIZE)
    counts = peer_count.reshape(DEVICES, P_SIZE)
    cell_ids = slot_cell.reshape(DEVICES, DEVICES, S)
    dest_ids = jnp.arange(DEVICES, dtype=jnp.int32)[:, None]
    chosen = cell_ids[peer_ids, dest_ids]
    picked = atm_flat[peer_ids[:, :, None], :, chosen]
    slot_index = jnp.arange(S, dtype=jnp.int32)
    live_slots = slot_index[None, None, :] < counts[:, :, None]
    picked = jnp.where(live_slots[..., None], picked, jnp.zeros((), picked.dtype))
    picked = picked.reshape(N_TY, N_TX, P_SIZE, S, NTR).astype(jnp.float32)
    forcing = jnp.zeros((NTR, N_TY, OY, N_TX, OX), jnp.float32)
    for peer_index in range(P_SIZE):
        weights = to_ocean[peer_index].reshape(S, N_TY, OY, N_TX, OX).astype(jnp.float32)
        forcing = forcing + jnp.einsum('ijsc,siyjx->ciyjx', picked[:, :, peer_index], weights, precision=lax.Precision.HIGHEST)
    forcing = forcing.reshape(NTR, NY, NX)
    tracer_state = tracers
    for repeat_index in range(SUBSTEPS):
        padded = jnp.pad(tracer_state, ((0, 0), (0, 0), (2, 2), (2, 2)))
        tracer_state = substep(padded, padded_flow, forcing, wet_mask, mix_inverse)
    surface = lax.optimization_barrier(tracer_state[0, 0].astype(jnp.bfloat16)).astype(jnp.float32)
    surface = surface.reshape(N_TY, OY, N_TX, OX)
    pieces = []
    for peer_index in range(P_SIZE):
        weights = to_atmos[peer_index].reshape(S, N_TY, OY, N_TX, OX).astype(jnp.float32)
        pieces.append(jnp.einsum('siyjx,iyjx->ijs', weights, surface, precision=lax.Precision.HIGHEST))
    returned = jnp.stack(pieces, axis=2).reshape(DEVICES, P_SIZE, S)
    sent_count = send_count.reshape(DEVICES, DEVICES)[peer_ids, dest_ids]
    kept = slot_index[None, None, :] < sent_count[:, :, None]
    returned = jnp.where(kept, returned, jnp.zeros((), returned.dtype))
    targets = (peer_ids[:, :, None] * atm_cells + chosen).reshape(-1)
    surface_atm = jnp.zeros((DEVICES * atm_cells,), jnp.float32).at[targets].add(returned.reshape(-1))
    surface_atm = surface_atm.reshape(N_TY, N_TX, AYD, AXD).transpose(0, 2, 1, 3).reshape(AY, AX)
    return (tracer_state, surface_atm)
```

```python
import functools

import jax
import jax.numpy as jnp
from jax import lax
from jax.experimental import pallas as pl
from jax.experimental.pallas import tpu as pltpu
from jax.sharding import PartitionSpec as P

MESH = pl.DeviceIdType.MESH
F32 = jnp.float32
BF16 = jnp.bfloat16
I32 = jnp.int32
SUBSTEPS = 2
LANES = 128
RIM = 32
ROWS = 256
RGROUP = 5
NEAR = tuple((di, dj) for di in (-1, 0, 1) for dj in (-1, 0, 1))


def iota(shape, dim):
    return lax.broadcasted_iota(I32, shape, dim)


def stencil(d):
    return jnp.where((d == 0) | (d == 1), 7.0, jnp.where((d == -1) | (d == 2), -1.0, 0.0))


def nn(a, b):
    return jnp.dot(a, b, preferred_element_type=F32)


def nt(a, b):
    return lax.dot_general(a, b, (((1,), (1,)), ((), ())), preferred_element_type=F32)


def tn(a, b):
    return lax.dot_general(a, b, (((0,), (0,)), ((), ())), preferred_element_type=F32)


def kernel(
    nty,
    ntx,
    tracers,
    courant,
    mix,
    to_ocean,
    to_atmos,
    depth,
    atm,
    slot_cell,
    peer_list,
    peer_count,
    send_count,
    out,
    surf_out,
    q,
    cour,
    mixv,
    toc,
    toa,
    fld,
    sr,
    hr,
    sc,
    hc,
    coef,
    ux,
    uy,
    mv,
    forc,
    depx,
    dr,
    dc,
    c_x,
    c_xh,
    c_xs,
    c_xsh,
    c_y,
    c_yh,
    c_ys,
    c_ysh,
    c_sel,
    c_selc,
    c_e,
    oh,
    flat,
    pk_s,
    pk_r,
    rt_s,
    rt_r,
    s_tr,
    s_co,
    s_mix,
    s_toc,
    s_toa,
    s_out,
    row_ss,
    row_rs,
    col_ss,
    col_rs,
    dep_ss,
    dep_rs,
    pk_ss,
    pk_rs,
    rt_ss,
    rt_rs,
):
    ntr, nb, zb, oy, ox = q.shape
    peers, slots = to_ocean.shape[0], to_ocean.shape[1]
    i = lax.axis_index("ty")
    j = lax.axis_index("tx")

    def device(di, dj):
        return (lax.rem(i + di + nty, nty), lax.rem(j + dj + ntx, ntx))

    barrier = pltpu.get_barrier_semaphore()
    for di, dj in NEAR:
        if (di, dj) != (0, 0):
            pl.semaphore_signal(barrier, inc=1, device_id=device(di, dj), device_id_type=MESH)

    order = tuple((n + 1) % nb for n in range(nb))
    loads = {}
    for b in order:
        loads["tr", b] = pltpu.make_async_copy(
            tracers.at[:, pl.ds(b * zb, zb)], q.at[:, b], s_tr.at[b]
        )
        loads["co", b] = pltpu.make_async_copy(
            courant.at[:, pl.ds(b * zb, zb)], cour.at[:, b], s_co.at[b]
        )
        loads["tr", b].start()
        loads["co", b].start()
    for b in order[:-1]:
        pltpu.make_async_copy(mix.at[b], mixv.at[b], s_mix.at[b]).start()
    pltpu.make_async_copy(to_ocean, toc, s_toc).start()
    pltpu.make_async_copy(mix.at[order[-1]], mixv.at[order[-1]], s_mix.at[order[-1]]).start()
    pltpu.make_async_copy(to_atmos, toa, s_toa).start()

    g = iota((ox, 2 * ox), 0)
    n = iota((ox, 2 * ox), 1)
    d = g - jnp.where(n < ox, n, n - ox - 1)
    c_x[...] = stencil(d).astype(BF16)
    c_xs[...] = jnp.where(d == jnp.where(n < ox, 1, 0), 1.0, 0.0).astype(BF16)
    r = iota((16, 2 * ox), 0)
    n = iota((16, 2 * ox), 1)
    x = jnp.where(n < ox, n, n - ox - 1)
    for f in range(4):
        at = jnp.where(r < 8, -2 + r - 2 * f, ox + r - 8 - 2 * f)
        mine = ((r & 7) >> 1) == f
        if f < 3:
            c_xh[f] = jnp.where(mine, stencil(at - x), 0.0).astype(BF16)
        else:
            hit = mine & (at - x == jnp.where(n < ox, 1, 0))
            c_xsh[...] = jnp.where(hit, 1.0, 0.0).astype(BF16)
    m = iota((2 * ROWS, ROWS), 0)
    n = iota((2 * ROWS, ROWS), 1)
    mm = jnp.where(m < ROWS, m, m - ROWS)
    y = jnp.where(m < ROWS, mm & 15, (mm & 15) - 1)
    d = (n & 15) - y
    same = (mm >> 4) == (n >> 4)
    c_y[...] = jnp.where(same, stencil(d), 0.0).astype(BF16)
    hit = same & (d == jnp.where(m < ROWS, 1, 0))
    c_ys[...] = jnp.where(hit, 1.0, 0.0).astype(BF16)
    m = iota((2 * ROWS, 2 * RIM), 0)
    n = iota((2 * ROWS, 2 * RIM), 1)
    mm = jnp.where(m < ROWS, m, m - ROWS)
    y = jnp.where(m < ROWS, mm & 15, (mm & 15) - 1)
    nn_ = jnp.where(n < RIM, n, n - RIM)
    d = jnp.where(n < RIM, -2 + (nn_ & 1), oy + (nn_ & 1)) - y
    same = (mm >> 4) == (nn_ >> 1)
    c_yh[...] = jnp.where(same, stencil(d), 0.0).astype(BF16)
    hit = same & (d == jnp.where(m < ROWS, 1, 0))
    c_ysh[...] = jnp.where(hit, 1.0, 0.0).astype(BF16)
    m = iota((2 * RIM, ROWS), 0)
    n = iota((2 * RIM, ROWS), 1)
    mm = jnp.where(m < RIM, m, m - RIM)
    y = jnp.where(m < RIM, oy - 2 + (mm & 1), mm & 1)
    open_down = jnp.where(i == nty - 1, 0.0, 1.0)
    open_up = jnp.where(i == 0, 0.0, 1.0)
    hit = ((mm >> 1) == (n >> 4)) & ((n & 15) == y)
    c_sel[...] = jnp.where(hit, jnp.where(m < RIM, open_down, open_up), 0.0).astype(BF16)
    r = iota((16, ox), 0)
    n = iota((16, ox), 1)
    open_right = jnp.where(j == ntx - 1, 0.0, 1.0)
    open_left = jnp.where(j == 0, 0.0, 1.0)
    for f in range(4):
        at = jnp.where(r < 8, ox - 2 + r - 2 * f, r - 8 - 2 * f)
        mine = ((r & 7) >> 1) == f
        hit = mine & (at == n)
        c_selc[f] = jnp.where(hit, jnp.where(r < 8, open_right, open_left), 0.0).astype(BF16)
    r = iota((slots, slots * oy), 0)
    n = iota((slots, slots * oy), 1)
    c_e[...] = jnp.where((n >> 4) == r, 1.0, 0.0).astype(BF16)

    cells = iota((oh.shape[0], slots), 0)
    for k, (di, dj) in enumerate(NEAR):
        ti, tj = device(di, dj)
        row = slot_cell[0, 0, pl.ds(ti * ntx + tj, 1), :]
        oh[:, k * slots : (k + 1) * slots] = jnp.where(cells == row, 1.0, 0.0).astype(BF16)
    flux = atm[...].astype(F32)
    flat[...] = jnp.zeros_like(flat)
    for c in range(flux.shape[0]):
        for r in range(flux.shape[1]):
            flat[c : c + 1, r * LANES : (r + 1) * LANES] = flux[c, r : r + 1, :]
    picks = nn(flat[...].astype(BF16), oh[...])
    for k in range(len(NEAR)):
        pk_s[k] = picks[:, k * slots : (k + 1) * slots]

    pl.semaphore_wait(barrier, len(NEAR) - 1)

    def depth_copies():
        return (
            pltpu.make_async_remote_copy(
                depth.at[pl.ds(oy - 8, 8)], dr.at[0], dep_ss.at[0], dep_rs.at[0],
                device_id=device(1, 0), device_id_type=MESH,
            ),
            pltpu.make_async_remote_copy(
                depth.at[pl.ds(0, 8)], dr.at[1], dep_ss.at[1], dep_rs.at[1],
                device_id=device(-1, 0), device_id_type=MESH,
            ),
            pltpu.make_async_remote_copy(
                depth.at[:, pl.ds(ox - LANES, LANES)], dc.at[0], dep_ss.at[2], dep_rs.at[2],
                device_id=device(0, 1), device_id_type=MESH,
            ),
            pltpu.make_async_remote_copy(
                depth.at[:, pl.ds(0, LANES)], dc.at[1], dep_ss.at[3], dep_rs.at[3],
                device_id=device(0, -1), device_id_type=MESH,
            ),
        )

    def near_copies(source, target, ss, rs, of):
        made = []
        for k, (di, dj) in enumerate(NEAR):
            if (di, dj) != (0, 0):
                made.append(
                    pltpu.make_async_remote_copy(
                        source.at[of(k, di, dj)], target.at[len(NEAR) - 1 - k], ss.at[k],
                        rs.at[len(NEAR) - 1 - k], device_id=device(di, dj), device_id_type=MESH,
                    )
                )
        return made

    def rim_copies(step, b, fields):
        rows = [
            pltpu.make_async_remote_copy(
                sr.at[step, b, pl.ds(0, fields), pl.ds(s * RIM, RIM)],
                hr.at[step, b, pl.ds(0, fields), pl.ds(s * RIM, RIM)],
                row_ss.at[step, s, b], row_rs.at[step, s, b],
                device_id=device(1 - 2 * s, 0), device_id_type=MESH,
            )
            for s in range(2)
        ]
        cols = [
            pltpu.make_async_remote_copy(
                sc.at[step, b, pl.ds(s * 8, 8)],
                hc.at[step, b, pl.ds(s * 8, 8)],
                col_ss.at[step, s, b], col_rs.at[step, s, b],
                device_id=device(0, 1 - 2 * s), device_id_type=MESH,
            )
            for s in range(2)
        ]
        return rows + cols

    for copy in depth_copies():
        copy.start()
    for copy in near_copies(pk_s, pk_r, pk_ss, pk_rs, lambda k, di, dj: k):
        copy.start()

    dep = depth[...]

    def pack(step, b, row_fields, col_fields):
        for f, source in enumerate(row_fields):
            sr[step, b, f] = nn(c_sel[...], fld[source, b]).astype(BF16)
        cols = nt(c_selc[0], fld[col_fields[0], b])
        for f in range(1, len(col_fields)):
            cols = cols + nt(c_selc[f], fld[col_fields[f], b])
        sc[step, b] = cols
        for copy in rim_copies(step, b, len(row_fields)):
            copy.start()

    def fill(idx, carry):
        b = lax.rem(idx + 1, nb)
        pltpu.make_async_copy(tracers.at[:, pl.ds(0, zb)], q.at[:, b], s_tr.at[b]).wait()
        pltpu.make_async_copy(courant.at[:, pl.ds(0, zb)], cour.at[:, b], s_co.at[b]).wait()

        def level(k, carry):
            rows = pl.ds(pl.multiple_of(k * oy, oy), oy)
            for t in range(ntr):
                fld[t, b, rows, :] = q[t, b, k].astype(BF16)
            wet = (b * zb + k) < dep
            for a in range(2):
                fld[ntr + a, b, rows, :] = jnp.where(wet, cour[a, b, k], 0.0).astype(BF16)
            return carry

        lax.fori_loop(0, zb, level, 0)
        for f in range(ntr + 2):
            fld[f, b, zb * oy :, :] = jnp.zeros((ROWS - zb * oy, ox), BF16)
        pack(0, b, (0, 1, 2, 4), (0, 1, 2, 3))
        return carry

    lax.fori_loop(0, nb, fill, 0)

    for copy in depth_copies():
        copy.wait()
    south = jnp.where(i == 0, 0, dr[0])
    north = jnp.where(i == nty - 1, 0, dr[1])
    west = jnp.where(j == 0, 0, dc[0])
    east = jnp.where(j == ntx - 1, 0, dc[1])
    wide = jnp.concatenate([dep, east], axis=1)
    depx[0] = pltpu.roll(wide, ox + LANES - 1, 1)[:, :ox]
    wide = jnp.concatenate([west, dep], axis=1)
    depx[1] = pltpu.roll(wide, 1, 1)[:, LANES:]
    tall = jnp.concatenate([dep, north], axis=0)
    depx[2] = pltpu.roll(tall, oy + 7, 0)[:oy]
    tall = jnp.concatenate([south, dep], axis=0)
    depx[3] = pltpu.roll(tall, 1, 0)[8:]

    def wait_rims(step, b, fields):
        for copy in rim_copies(step, b, fields):
            copy.wait()

    def faces(b):
        ux[0] = nn(fld[ntr, b], c_xs[...]) + tn(hc[0, b].astype(BF16), c_xsh[...])
        uy[0] = nn(c_ys[...], fld[ntr + 1, b]) + nn(c_ysh[...], hr[0, b, ntr])

        def level(k, carry):
            rows = pl.ds(pl.multiple_of(k * oy, oy), oy)
            later = pl.ds(pl.multiple_of(ROWS + k * oy, oy), oy)
            at = b * zb + k
            wet = at < dep
            own = jnp.where(wet, cour[0, b, k] * (1.0 / 24.0), 0.0)
            coef[0, b, k] = jnp.where(at < depx[0], own, 0.0) + jnp.where(
                wet, ux[0, rows, 0:ox] * (1.0 / 24.0), 0.0
            )
            coef[1, b, k] = jnp.where(at < depx[1], own, 0.0) + jnp.where(
                wet, ux[0, rows, ox : 2 * ox] * (1.0 / 24.0), 0.0
            )
            own = jnp.where(wet, cour[1, b, k] * (1.0 / 24.0), 0.0)
            coef[2, b, k] = jnp.where(at < depx[2], own, 0.0) + jnp.where(
                wet, uy[0, rows, :] * (1.0 / 24.0), 0.0
            )
            coef[3, b, k] = jnp.where(at < depx[3], own, 0.0) + jnp.where(
                wet, uy[0, later, :] * (1.0 / 24.0), 0.0
            )
            return carry

        lax.fori_loop(0, zb, level, 0)

    def advect(step, b):
        halo = hc[step, b].astype(BF16)
        for t in range(ntr):
            ux[t] = nn(fld[t, b], c_x[...]) + tn(halo, c_xh[t])
            uy[t] = nn(c_y[...], fld[t, b]) + nn(c_yh[...], hr[step, b, t])

        def level(k, carry):
            rows = pl.ds(pl.multiple_of(k * oy, oy), oy)
            later = pl.ds(pl.multiple_of(ROWS + k * oy, oy), oy)
            wet = (b * zb + k) < dep
            c0, c1, c2, c3 = (coef[a, b, k] for a in range(4))
            for t in range(ntr):
                moved = jnp.where(wet, q[t, b, k], 0.0)
                moved = moved - (c0 * ux[t, rows, 0:ox] - c1 * ux[t, rows, ox : 2 * ox])
                mv[t, k] = moved - (c2 * uy[t, rows, :] - c3 * uy[t, later, :])
            return carry

        lax.fori_loop(0, zb, level, 0)

        @pl.when(b == 0)
        def _():
            for t in range(ntr):
                mv[t, 0] = mv[t, 0] + jnp.where(dep > 0, forc[t], 0.0)

    def mixing(b, keep):
        groups = zb // RGROUP

        def part(idx, carry):
            lanes = pl.ds(pl.multiple_of((idx // groups) * LANES, LANES), LANES)
            first = lax.rem(idx, groups) * RGROUP
            acc = [[None] * ntr for _ in range(RGROUP)]
            for c in range(zb):
                moved = [mv[t, c, :, lanes] for t in range(ntr)]
                for r in range(RGROUP):
                    weight = mixv[b, first + r, c, :, lanes].astype(F32)
                    for t in range(ntr):
                        term = weight * moved[t]
                        acc[r][t] = term if c == 0 else acc[r][t] + term
            for r in range(RGROUP):
                k = first + r
                wet = (b * zb + k) < depth[:, lanes]
                for t in range(ntr):
                    value = jnp.where(wet, acc[r][t], 0.0)
                    q[t, b, k, :, lanes] = value
                    if keep:
                        fld[t, b, pl.ds(pl.multiple_of(k * oy, oy), oy), lanes] = value.astype(BF16)
            return carry

        lax.fori_loop(0, groups * (ox // LANES), part, 0)

    def force():
        for copy in near_copies(pk_s, pk_r, pk_ss, pk_rs, lambda k, di, dj: k):
            copy.wait()
        pltpu.make_async_copy(to_ocean, toc, s_toc).wait()
        mine = pk_s[4]
        chosen = [mine, pk_r[5], pk_r[3]]
        for p, di in ((3, 1), (4, -1)):
            ids = [device(di, dj) for dj in (-1, 0, 1)]
            ids = [a * ntx + b for a, b in ids]
            base = (di + 1) * 3
            e = peer_list[0, 0, p]
            got = jnp.where(e == ids[0], pk_r[base], pk_r[base + 1])
            chosen.append(jnp.where(e == ids[2], pk_r[base + 2], got))
        slot = iota((8, slots), 1)
        y = iota((oy, slots * oy), 0)
        x = iota((oy, slots * oy), 1)
        diagonal = (x & 15) == y
        total = jnp.zeros((ntr * oy, ox), F32)
        for p in range(peers):
            live = jnp.where(slot < peer_count[0, 0, p], chosen[p], 0.0).astype(BF16)
            spread = nn(live, c_e[...])
            left = jnp.concatenate(
                [jnp.where(diagonal, spread[c : c + 1, :], 0.0).astype(BF16) for c in range(ntr)],
                axis=0,
            )
            total = total + nn(left, toc[p].reshape(slots * oy, ox))
        for t in range(ntr):
            forc[t] = total[t * oy : (t + 1) * oy]

    def ret_copies():
        of = lambda k, di, dj: {1: 3, -1: 4}[di] if di != 0 else {1: 1, -1: 2}[dj]
        return near_copies(rt_s, rt_r, rt_ss, rt_rs, of)

    def give_back():
        pltpu.make_async_copy(to_atmos, toa, s_toa).wait()
        surface = q[0, 0, 0].astype(BF16)
        y = iota((oy, slots * oy), 0)
        x = iota((oy, slots * oy), 1)
        diagonal = (x & 15) == y
        for p in range(peers):
            sums = nt(surface, toa[p].reshape(slots * oy, ox))
            sums = jnp.where(diagonal, sums, 0.0)
            high = sums.astype(BF16)
            low = (sums - high.astype(F32)).astype(BF16)
            both = nt(high, c_e[...]) + nt(low, c_e[...])
            rt_s[p] = jnp.broadcast_to(jnp.sum(both, axis=0, keepdims=True), (8, slots))
        for copy in ret_copies():
            copy.start()

    def first_step(idx, carry):
        b = lax.rem(idx + 1, nb)
        wait_rims(0, b, 4)
        faces(b)

        @pl.when(b == 0)
        def _():
            force()

        advect(0, b)
        pltpu.make_async_copy(mix.at[0], mixv.at[b], s_mix.at[b]).wait()
        mixing(b, True)
        pack(1, b, (0, 1, 2), (0, 1, 2))
        return carry

    lax.fori_loop(0, nb, first_step, 0)

    def second_step(idx, carry):
        b = jnp.where(idx < 2, 1 - idx, idx)
        wait_rims(1, b, 3)
        advect(1, b)
        mixing(b, False)
        pltpu.make_async_copy(q.at[:, b], out.at[:, pl.ds(b * zb, zb)], s_out.at[b]).start()

        @pl.when(b == 0)
        def _():
            give_back()

        return carry

    lax.fori_loop(0, nb, second_step, 0)

    for copy in ret_copies():
        copy.wait()
    slot = iota((1, slots), 1)
    parts = []
    for k, (di, dj) in enumerate(NEAR):
        ti, tj = device(di, dj)
        value = rt_s[0] if (di, dj) == (0, 0) else rt_r[k]
        kept = slot < send_count[0, 0, ti * ntx + tj]
        parts.append(jnp.where(kept, value, 0.0))
    values = jnp.concatenate(parts, axis=1)
    high = values.astype(BF16)
    low = (values - high.astype(F32)).astype(BF16)
    landed = nt(high, oh[...]) + nt(low, oh[...])
    for r in range(surf_out.shape[0]):
        surf_out[r : r + 1, :] = landed[0:1, r * LANES : (r + 1) * LANES]
    for b in range(nb):
        pltpu.make_async_copy(q.at[:, b], out.at[:, pl.ds(b * zb, zb)], s_out.at[b]).wait()


def body(
    nty,
    ntx,
    tracers,
    courant,
    depth_levels,
    mix_inverse,
    to_ocean,
    to_atmos,
    atm_flux,
    peer_list,
    peer_count,
    send_count,
    slot_cell,
):
    ntr, levels, oy, ox = tracers.shape
    nb, zb = mix_inverse.shape[:2]
    peers, slots = to_ocean.shape[:2]
    cells = atm_flux.shape[1] * atm_flux.shape[2]
    near = len(NEAR)
    anywhere = pl.BlockSpec(memory_space=pl.ANY)
    vmem = pl.BlockSpec(memory_space=pltpu.VMEM)
    smem = pl.BlockSpec(memory_space=pltpu.SMEM)
    dma = pltpu.SemaphoreType.DMA
    scratch = [
        pltpu.VMEM((ntr, nb, zb, oy, ox), F32),
        pltpu.VMEM((2, nb, zb, oy, ox), F32),
        pltpu.VMEM(mix_inverse.shape, BF16),
        pltpu.VMEM(to_ocean.shape, BF16),
        pltpu.VMEM(to_atmos.shape, BF16),
        pltpu.VMEM((ntr + 2, nb, ROWS, ox), BF16),
        pltpu.VMEM((SUBSTEPS, nb, 4, 2 * RIM, ox), BF16),
        pltpu.VMEM((SUBSTEPS, nb, 4, 2 * RIM, ox), BF16),
        pltpu.VMEM((SUBSTEPS, nb, 16, ox), F32),
        pltpu.VMEM((SUBSTEPS, nb, 16, ox), F32),
        pltpu.VMEM((4, nb, zb, oy, ox), F32),
        pltpu.VMEM((ntr, ROWS, 2 * ox), F32),
        pltpu.VMEM((ntr, 2 * ROWS, ox), F32),
        pltpu.VMEM((ntr, zb, oy, ox), F32),
        pltpu.VMEM((ntr, oy, ox), F32),
        pltpu.VMEM((4, oy, ox), I32),
        pltpu.VMEM((2, 8, ox), I32),
        pltpu.VMEM((2, oy, LANES), I32),
        pltpu.VMEM((ox, 2 * ox), BF16),
        pltpu.VMEM((3, 16, 2 * ox), BF16),
        pltpu.VMEM((ox, 2 * ox), BF16),
        pltpu.VMEM((16, 2 * ox), BF16),
        pltpu.VMEM((2 * ROWS, ROWS), BF16),
        pltpu.VMEM((2 * ROWS, 2 * RIM), BF16),
        pltpu.VMEM((2 * ROWS, ROWS), BF16),
        pltpu.VMEM((2 * ROWS, 2 * RIM), BF16),
        pltpu.VMEM((2 * RIM, ROWS), BF16),
        pltpu.VMEM((4, 16, ox), BF16),
        pltpu.VMEM((slots, slots * oy), BF16),
        pltpu.VMEM((cells, near * slots), BF16),
        pltpu.VMEM((8, cells), F32),
        pltpu.VMEM((near, 8, slots), F32),
        pltpu.VMEM((near, 8, slots), F32),
        pltpu.VMEM((peers, 8, slots), F32),
        pltpu.VMEM((near, 8, slots), F32),
        dma((nb,)),
        dma((nb,)),
        dma((nb,)),
        dma,
        dma,
        dma((nb,)),
        dma((SUBSTEPS, 2, nb)),
        dma((SUBSTEPS, 2, nb)),
        dma((SUBSTEPS, 2, nb)),
        dma((SUBSTEPS, 2, nb)),
        dma((4,)),
        dma((4,)),
        dma((near,)),
        dma((near,)),
        dma((near,)),
        dma((near,)),
    ]
    return pl.pallas_call(
        functools.partial(kernel, nty, ntx),
        out_shape=(
            jax.ShapeDtypeStruct(tracers.shape, F32),
            jax.ShapeDtypeStruct(atm_flux.shape[1:], F32),
        ),
        in_specs=[anywhere] * 5 + [vmem] * 3 + [smem] * 3,
        out_specs=(anywhere, vmem),
        scratch_shapes=scratch,
        compiler_params=pltpu.CompilerParams(
            collective_id=0, has_side_effects=True, vmem_limit_bytes=56 * 1024 * 1024
        ),
        cost_estimate=pl.CostEstimate(flops=10**9, bytes_accessed=26 * 10**6, transcendentals=0),
        name="interval",
    )(
        tracers,
        courant,
        mix_inverse,
        to_ocean,
        to_atmos,
        depth_levels,
        atm_flux,
        slot_cell,
        peer_list,
        peer_count,
        send_count,
    )


def solution(mesh):
    in_specs = (
        P(None, None, "ty", "tx"),
        P(None, None, "ty", "tx"),
        P("ty", "tx"),
        P(None, None, None, "ty", "tx"),
        P(None, None, "ty", "tx"),
        P(None, None, "ty", "tx"),
        P(None, "ty", "tx"),
        P("ty", "tx", None),
        P("ty", "tx", None),
        P("ty", "tx", None),
        P("ty", "tx", None, None),
    )
    out_specs = (P(None, None, "ty", "tx"), P("ty", "tx"))
    part = functools.partial(body, mesh.shape["ty"], mesh.shape["tx"])
    return jax.shard_map(part, mesh=mesh, in_specs=in_specs, out_specs=out_specs, check_vma=False)
```

```python
import functools

import jax
import jax.numpy as jnp
from jax import lax
from jax.experimental import pallas as pl
from jax.experimental.pallas import tpu as pltpu
from jax.sharding import PartitionSpec as P

MESH = pl.DeviceIdType.MESH
F32 = jnp.float32
BF16 = jnp.bfloat16
I32 = jnp.int32
SUBSTEPS = 2
LANES = 128
RIM = 32
ROWS = 256
RGROUP = 5
CGROUP = 5
NEAR = tuple((di, dj) for di in (-1, 0, 1) for dj in (-1, 0, 1))


def iota(shape, dim):
    return lax.broadcasted_iota(I32, shape, dim)


def stencil(d):
    return jnp.where((d == 0) | (d == 1), 7.0, jnp.where((d == -1) | (d == 2), -1.0, 0.0))


def nn(a, b):
    return jnp.dot(a, b, preferred_element_type=F32)


def nt(a, b):
    return lax.dot_general(a, b, (((1,), (1,)), ((), ())), preferred_element_type=F32)


def tn(a, b):
    return lax.dot_general(a, b, (((0,), (0,)), ((), ())), preferred_element_type=F32)


def kernel(
    nty,
    ntx,
    tracers,
    courant,
    mix,
    to_ocean,
    to_atmos,
    depth_in,
    atm_in,
    slot_cell_in,
    peer_list_in,
    peer_count_in,
    send_count_in,
    out,
    surf_out,
    q,
    cour,
    mixv,
    toc,
    toa,
    fld,
    sr,
    hr,
    sc,
    hc,
    coef,
    ux,
    uy,
    mv,
    forc,
    depx,
    dr,
    dc,
    c_x,
    c_xh,
    c_xs,
    c_xsh,
    c_y,
    c_yh,
    c_ys,
    c_ysh,
    c_sel,
    c_selc,
    c_e,
    oh,
    flat,
    pk_s,
    pk_r,
    rt_s,
    rt_r,
    depth,
    atm,
    slot_cell,
    peer_list,
    peer_count,
    send_count,
    s_in,
    s_tr,
    s_co,
    s_mix,
    s_toc,
    s_toa,
    row_ss,
    row_rs,
    col_ss,
    col_rs,
    dep_ss,
    dep_rs,
    pk_ss,
    pk_rs,
    rt_ss,
    rt_rs,
):
    ntr, nb, zb, oy, ox = q.shape
    peers, slots = to_ocean.shape[0], to_ocean.shape[1]
    i = lax.axis_index("ty")
    j = lax.axis_index("tx")

    def device(di, dj):
        return (lax.rem(i + di + nty, nty), lax.rem(j + dj + ntx, ntx))

    barrier = pltpu.get_barrier_semaphore()
    for di, dj in NEAR:
        if (di, dj) != (0, 0):
            pl.semaphore_signal(barrier, inc=1, device_id=device(di, dj), device_id_type=MESH)

    small = [
        pltpu.make_async_copy(source, target, s_in.at[k])
        for k, (source, target) in enumerate(
            (
                (depth_in, depth),
                (slot_cell_in, slot_cell),
                (atm_in, atm),
                (peer_list_in, peer_list),
                (peer_count_in, peer_count),
                (send_count_in, send_count),
            )
        )
    ]
    small[0].start()
    order = tuple((n + 1) % nb for n in range(nb))
    loads = {}
    for b in order:
        loads["tr", b] = pltpu.make_async_copy(
            tracers.at[:, pl.ds(b * zb, zb)], q.at[:, b], s_tr.at[b]
        )
        loads["co", b] = pltpu.make_async_copy(
            courant.at[:, pl.ds(b * zb, zb)], cour.at[:, b], s_co.at[b]
        )
        loads["tr", b].start()
        loads["co", b].start()
    for copy in small[1:]:
        copy.start()
    for b in order[:-1]:
        pltpu.make_async_copy(mix.at[b], mixv.at[b], s_mix.at[b]).start()
    pltpu.make_async_copy(to_ocean, toc, s_toc).start()
    pltpu.make_async_copy(mix.at[order[-1]], mixv.at[order[-1]], s_mix.at[order[-1]]).start()
    pltpu.make_async_copy(to_atmos, toa, s_toa).start()

    m = iota((2 * RIM, ROWS), 0)
    n = iota((2 * RIM, ROWS), 1)
    mm = jnp.where(m < RIM, m, m - RIM)
    y = jnp.where(m < RIM, oy - 2 + (mm & 1), mm & 1)
    open_down = jnp.where(i == nty - 1, 0.0, 1.0)
    open_up = jnp.where(i == 0, 0.0, 1.0)
    hit = ((mm >> 1) == (n >> 4)) & ((n & 15) == y)
    c_sel[...] = jnp.where(hit, jnp.where(m < RIM, open_down, open_up), 0.0).astype(BF16)
    r = iota((16, ox), 0)
    n = iota((16, ox), 1)
    open_right = jnp.where(j == ntx - 1, 0.0, 1.0)
    open_left = jnp.where(j == 0, 0.0, 1.0)
    for f in range(4):
        at = jnp.where(r < 8, ox - 2 + r - 2 * f, r - 8 - 2 * f)
        mine = ((r & 7) >> 1) == f
        hit = mine & (at == n)
        c_selc[f] = jnp.where(hit, jnp.where(r < 8, open_right, open_left), 0.0).astype(BF16)
    def depth_copies():
        return (
            pltpu.make_async_remote_copy(
                depth.at[pl.ds(oy - 8, 8)], dr.at[0], dep_ss.at[0], dep_rs.at[0],
                device_id=device(1, 0), device_id_type=MESH,
            ),
            pltpu.make_async_remote_copy(
                depth.at[pl.ds(0, 8)], dr.at[1], dep_ss.at[1], dep_rs.at[1],
                device_id=device(-1, 0), device_id_type=MESH,
            ),
            pltpu.make_async_remote_copy(
                depth.at[:, pl.ds(ox - LANES, LANES)], dc.at[0], dep_ss.at[2], dep_rs.at[2],
                device_id=device(0, 1), device_id_type=MESH,
            ),
            pltpu.make_async_remote_copy(
                depth.at[:, pl.ds(0, LANES)], dc.at[1], dep_ss.at[3], dep_rs.at[3],
                device_id=device(0, -1), device_id_type=MESH,
            ),
        )

    def near_copies(source, target, ss, rs, of):
        made = []
        for k, (di, dj) in enumerate(NEAR):
            if (di, dj) != (0, 0):
                made.append(
                    pltpu.make_async_remote_copy(
                        source.at[of(k, di, dj)], target.at[len(NEAR) - 1 - k], ss.at[k],
                        rs.at[len(NEAR) - 1 - k], device_id=device(di, dj), device_id_type=MESH,
                    )
                )
        return made

    def rim_copies(step, b, fields):
        rows = [
            pltpu.make_async_remote_copy(
                sr.at[step, b, pl.ds(0, fields), pl.ds(s * RIM, RIM)],
                hr.at[step, b, pl.ds(0, fields), pl.ds(s * RIM, RIM)],
                row_ss.at[step, s, b], row_rs.at[step, s, b],
                device_id=device(1 - 2 * s, 0), device_id_type=MESH,
            )
            for s in range(2)
        ]
        cols = [
            pltpu.make_async_remote_copy(
                sc.at[step, b, pl.ds(s * 8, 8)],
                hc.at[step, b, pl.ds(s * 8, 8)],
                col_ss.at[step, s, b], col_rs.at[step, s, b],
                device_id=device(0, 1 - 2 * s), device_id_type=MESH,
            )
            for s in range(2)
        ]
        return rows + cols

    small[0].wait()
    dep = depth[...]

    def pack(step, b, row_fields, col_fields):
        for f, source in enumerate(row_fields):
            sr[step, b, f] = nn(c_sel[...], fld[source, b]).astype(BF16)
        cols = nt(c_selc[0], fld[col_fields[0], b])
        for f in range(1, len(col_fields)):
            cols = cols + nt(c_selc[f], fld[col_fields[f], b])
        sc[step, b] = cols

    def send(step, b, fields):
        for copy in rim_copies(step, b, fields):
            copy.start()

    def fill(b):
        pltpu.make_async_copy(tracers.at[:, pl.ds(0, zb)], q.at[:, b], s_tr.at[b]).wait()
        pltpu.make_async_copy(courant.at[:, pl.ds(0, zb)], cour.at[:, b], s_co.at[b]).wait()

        def level(k, carry):
            rows = pl.ds(pl.multiple_of(k * oy, oy), oy)
            for t in range(ntr):
                fld[t, b, rows, :] = q[t, b, k].astype(BF16)
            wet = (b * zb + k) < dep
            for a in range(2):
                fld[ntr + a, b, rows, :] = jnp.where(wet, cour[a, b, k], 0.0).astype(BF16)
            return carry

        lax.fori_loop(0, zb, level, 0)
        for f in range(ntr + 2):
            fld[f, b, zb * oy :, :] = jnp.zeros((ROWS - zb * oy, ox), BF16)
        pack(0, b, (0, 1, 2, 4), (0, 1, 2, 3))

    fill(order[0])
    pl.semaphore_wait(barrier, len(NEAR) - 1)
    for copy in depth_copies():
        copy.start()
    send(0, order[0], 4)

    def fill_and_send(idx, carry):
        b = lax.rem(idx + 1, nb)
        fill(b)
        send(0, b, 4)
        return carry

    lax.fori_loop(1, nb, fill_and_send, 0)

    g = iota((ox, 2 * ox), 0)
    n = iota((ox, 2 * ox), 1)
    d = g - jnp.where(n < ox, n, n - ox - 1)
    c_x[...] = stencil(d).astype(BF16)
    c_xs[...] = jnp.where(d == jnp.where(n < ox, 1, 0), 1.0, 0.0).astype(BF16)
    r = iota((16, 2 * ox), 0)
    n = iota((16, 2 * ox), 1)
    x = jnp.where(n < ox, n, n - ox - 1)
    for f in range(4):
        at = jnp.where(r < 8, -2 + r - 2 * f, ox + r - 8 - 2 * f)
        mine = ((r & 7) >> 1) == f
        if f < 3:
            c_xh[f] = jnp.where(mine, stencil(at - x), 0.0).astype(BF16)
        else:
            hit = mine & (at - x == jnp.where(n < ox, 1, 0))
            c_xsh[...] = jnp.where(hit, 1.0, 0.0).astype(BF16)
    m = iota((2 * ROWS, ROWS), 0)
    n = iota((2 * ROWS, ROWS), 1)
    mm = jnp.where(m < ROWS, m, m - ROWS)
    y = jnp.where(m < ROWS, mm & 15, (mm & 15) - 1)
    d = (n & 15) - y
    same = (mm >> 4) == (n >> 4)
    c_y[...] = jnp.where(same, stencil(d), 0.0).astype(BF16)
    hit = same & (d == jnp.where(m < ROWS, 1, 0))
    c_ys[...] = jnp.where(hit, 1.0, 0.0).astype(BF16)
    m = iota((2 * ROWS, 2 * RIM), 0)
    n = iota((2 * ROWS, 2 * RIM), 1)
    mm = jnp.where(m < ROWS, m, m - ROWS)
    y = jnp.where(m < ROWS, mm & 15, (mm & 15) - 1)
    nn_ = jnp.where(n < RIM, n, n - RIM)
    d = jnp.where(n < RIM, -2 + (nn_ & 1), oy + (nn_ & 1)) - y
    same = (mm >> 4) == (nn_ >> 1)
    c_yh[...] = jnp.where(same, stencil(d), 0.0).astype(BF16)
    hit = same & (d == jnp.where(m < ROWS, 1, 0))
    c_ysh[...] = jnp.where(hit, 1.0, 0.0).astype(BF16)
    r = iota((slots, slots * oy), 0)
    n = iota((slots, slots * oy), 1)
    c_e[...] = jnp.where((n >> 4) == r, 1.0, 0.0).astype(BF16)

    for copy in small[1:]:
        copy.wait()

    cells = iota((oh.shape[0], slots), 0)
    for k, (di, dj) in enumerate(NEAR):
        ti, tj = device(di, dj)
        row = slot_cell[0, 0, pl.ds(ti * ntx + tj, 1), :]
        oh[:, k * slots : (k + 1) * slots] = jnp.where(cells == row, 1.0, 0.0).astype(BF16)
    flux = atm[...].astype(F32)
    flat[...] = jnp.zeros_like(flat)
    for c in range(flux.shape[0]):
        for r in range(flux.shape[1]):
            flat[c : c + 1, r * LANES : (r + 1) * LANES] = flux[c, r : r + 1, :]
    picks = nn(flat[...].astype(BF16), oh[...])
    for k in range(len(NEAR)):
        pk_s[k] = picks[:, k * slots : (k + 1) * slots]

    for copy in near_copies(pk_s, pk_r, pk_ss, pk_rs, lambda k, di, dj: k):
        copy.start()

    for copy in depth_copies():
        copy.wait()
    south = jnp.where(i == 0, 0, dr[0])
    north = jnp.where(i == nty - 1, 0, dr[1])
    west = jnp.where(j == 0, 0, dc[0])
    east = jnp.where(j == ntx - 1, 0, dc[1])
    wide = jnp.concatenate([dep, east], axis=1)
    depx[0] = pltpu.roll(wide, ox + LANES - 1, 1)[:, :ox]
    wide = jnp.concatenate([west, dep], axis=1)
    depx[1] = pltpu.roll(wide, 1, 1)[:, LANES:]
    tall = jnp.concatenate([dep, north], axis=0)
    depx[2] = pltpu.roll(tall, oy + 7, 0)[:oy]
    tall = jnp.concatenate([south, dep], axis=0)
    depx[3] = pltpu.roll(tall, 1, 0)[8:]

    def wait_rims(step, b, fields):
        for copy in rim_copies(step, b, fields):
            copy.wait()

    def faces(b):
        ux[0] = nn(fld[ntr, b], c_xs[...]) + tn(hc[0, b].astype(BF16), c_xsh[...])
        uy[0] = nn(c_ys[...], fld[ntr + 1, b]) + nn(c_ysh[...], hr[0, b, ntr])

        def level(k, carry):
            rows = pl.ds(pl.multiple_of(k * oy, oy), oy)
            later = pl.ds(pl.multiple_of(ROWS + k * oy, oy), oy)
            at = b * zb + k
            wet = at < dep
            own = jnp.where(wet, cour[0, b, k] * (1.0 / 24.0), 0.0)
            coef[0, b, k] = jnp.where(at < depx[0], own, 0.0) + jnp.where(
                wet, ux[0, rows, 0:ox] * (1.0 / 24.0), 0.0
            )
            coef[1, b, k] = jnp.where(at < depx[1], own, 0.0) + jnp.where(
                wet, ux[0, rows, ox : 2 * ox] * (1.0 / 24.0), 0.0
            )
            own = jnp.where(wet, cour[1, b, k] * (1.0 / 24.0), 0.0)
            coef[2, b, k] = jnp.where(at < depx[2], own, 0.0) + jnp.where(
                wet, uy[0, rows, :] * (1.0 / 24.0), 0.0
            )
            coef[3, b, k] = jnp.where(at < depx[3], own, 0.0) + jnp.where(
                wet, uy[0, later, :] * (1.0 / 24.0), 0.0
            )
            return carry

        lax.fori_loop(0, zb, level, 0)

    def advect(step, b):
        halo = hc[step, b].astype(BF16)
        for t in range(ntr):
            ux[t] = nn(fld[t, b], c_x[...]) + tn(halo, c_xh[t])
            uy[t] = nn(c_y[...], fld[t, b]) + nn(c_yh[...], hr[step, b, t])

        def level(k, carry):
            rows = pl.ds(pl.multiple_of(k * oy, oy), oy)
            later = pl.ds(pl.multiple_of(ROWS + k * oy, oy), oy)
            wet = (b * zb + k) < dep
            c0, c1, c2, c3 = (coef[a, b, k] for a in range(4))
            for t in range(ntr):
                moved = jnp.where(wet, q[t, b, k], 0.0)
                moved = moved - (c0 * ux[t, rows, 0:ox] - c1 * ux[t, rows, ox : 2 * ox])
                moved = moved - (c2 * uy[t, rows, :] - c3 * uy[t, later, :])
                mv[t, k] = moved.astype(BF16)
            return carry

        lax.fori_loop(0, zb, level, 0)

        @pl.when(b == 0)
        def _():
            rows, later = pl.ds(0, oy), pl.ds(ROWS, oy)
            wet = dep > 0
            for t in range(ntr):
                moved = jnp.where(wet, q[t, 0, 0] + forc[t], 0.0)
                moved = moved - (
                    coef[0, 0, 0] * ux[t, rows, 0:ox] - coef[1, 0, 0] * ux[t, rows, ox : 2 * ox]
                )
                moved = moved - (coef[2, 0, 0] * uy[t, rows, :] - coef[3, 0, 0] * uy[t, later, :])
                mv[t, 0] = moved.astype(BF16)

    def mixing(b, keep):
        groups = zb // RGROUP

        def part(idx, carry):
            lanes = pl.ds(pl.multiple_of((idx // groups) * LANES, LANES), LANES)
            first = lax.rem(idx, groups) * RGROUP
            acc = [[None] * ntr for _ in range(RGROUP)]
            for c0 in range(0, zb, CGROUP):
                for r in range(RGROUP):
                    sums = [None] * ntr
                    for c in range(c0, c0 + CGROUP):
                        weight = mixv[b, first + r, c, :, lanes]
                        for t in range(ntr):
                            term = weight * mv[t, c, :, lanes]
                            sums[t] = term if c == c0 else sums[t] + term
                    for t in range(ntr):
                        wide = sums[t].astype(F32)
                        acc[r][t] = wide if c0 == 0 else acc[r][t] + wide
            for r in range(RGROUP):
                k = first + r
                wet = (b * zb + k) < depth[:, lanes]
                for t in range(ntr):
                    value = jnp.where(wet, acc[r][t], 0.0)
                    if keep:
                        q[t, b, k, :, lanes] = value
                        fld[t, b, pl.ds(pl.multiple_of(k * oy, oy), oy), lanes] = value.astype(BF16)
                    else:
                        out[t, b * zb + k, :, lanes] = value
            return carry

        lax.fori_loop(0, groups * (ox // LANES), part, 0)

    def force():
        for copy in near_copies(pk_s, pk_r, pk_ss, pk_rs, lambda k, di, dj: k):
            copy.wait()
        pltpu.make_async_copy(to_ocean, toc, s_toc).wait()
        mine = pk_s[4]
        chosen = [mine, pk_r[5], pk_r[3]]
        for p, di in ((3, 1), (4, -1)):
            ids = [device(di, dj) for dj in (-1, 0, 1)]
            ids = [a * ntx + b for a, b in ids]
            base = (di + 1) * 3
            e = peer_list[0, 0, p]
            got = jnp.where(e == ids[0], pk_r[base], pk_r[base + 1])
            chosen.append(jnp.where(e == ids[2], pk_r[base + 2], got))
        slot = iota((8, slots), 1)
        y = iota((oy, slots * oy), 0)
        x = iota((oy, slots * oy), 1)
        diagonal = (x & 15) == y
        total = jnp.zeros((ntr * oy, ox), F32)
        for p in range(peers):
            live = jnp.where(slot < peer_count[0, 0, p], chosen[p], 0.0).astype(BF16)
            spread = nn(live, c_e[...])
            left = jnp.concatenate(
                [jnp.where(diagonal, spread[c : c + 1, :], 0.0).astype(BF16) for c in range(ntr)],
                axis=0,
            )
            total = total + nn(left, toc[p].reshape(slots * oy, ox))
        for t in range(ntr):
            forc[t] = total[t * oy : (t + 1) * oy]

    def ret_copies():
        of = lambda k, di, dj: {1: 3, -1: 4}[di] if di != 0 else {1: 1, -1: 2}[dj]
        return near_copies(rt_s, rt_r, rt_ss, rt_rs, of)

    def give_back():
        pltpu.make_async_copy(to_atmos, toa, s_toa).wait()
        surface = out[0, 0].astype(BF16)
        y = iota((oy, slots * oy), 0)
        x = iota((oy, slots * oy), 1)
        diagonal = (x & 15) == y
        for p in range(peers):
            sums = nt(surface, toa[p].reshape(slots * oy, ox))
            sums = jnp.where(diagonal, sums, 0.0)
            high = sums.astype(BF16)
            low = (sums - high.astype(F32)).astype(BF16)
            both = nt(high, c_e[...]) + nt(low, c_e[...])
            rt_s[p] = jnp.broadcast_to(jnp.sum(both, axis=0, keepdims=True), (8, slots))
        for copy in ret_copies():
            copy.start()

    def first_step(idx, carry):
        b = lax.rem(idx + 1, nb)
        wait_rims(0, b, 4)
        faces(b)

        @pl.when(b == 0)
        def _():
            force()

        advect(0, b)
        pltpu.make_async_copy(mix.at[0], mixv.at[b], s_mix.at[b]).wait()
        mixing(b, True)
        pack(1, b, (0, 1, 2), (0, 1, 2))
        send(1, b, 3)
        return carry

    lax.fori_loop(0, nb, first_step, 0)

    def second_step(idx, carry):
        b = jnp.where(idx < 2, 1 - idx, idx)
        wait_rims(1, b, 3)
        advect(1, b)
        mixing(b, False)

        @pl.when(b == 0)
        def _():
            give_back()

        return carry

    lax.fori_loop(0, nb, second_step, 0)

    for copy in ret_copies():
        copy.wait()
    slot = iota((1, slots), 1)
    parts = []
    for k, (di, dj) in enumerate(NEAR):
        ti, tj = device(di, dj)
        value = rt_s[0] if (di, dj) == (0, 0) else rt_r[k]
        kept = slot < send_count[0, 0, ti * ntx + tj]
        parts.append(jnp.where(kept, value, 0.0))
    values = jnp.concatenate(parts, axis=1)
    high = values.astype(BF16)
    low = (values - high.astype(F32)).astype(BF16)
    landed = nt(high, oh[...]) + nt(low, oh[...])
    for r in range(surf_out.shape[0]):
        surf_out[r : r + 1, :] = landed[0:1, r * LANES : (r + 1) * LANES]


def body(
    nty,
    ntx,
    tracers,
    courant,
    depth_levels,
    mix_inverse,
    to_ocean,
    to_atmos,
    atm_flux,
    peer_list,
    peer_count,
    send_count,
    slot_cell,
):
    ntr, levels, oy, ox = tracers.shape
    nb, zb = mix_inverse.shape[:2]
    peers, slots = to_ocean.shape[:2]
    cells = atm_flux.shape[1] * atm_flux.shape[2]
    near = len(NEAR)
    hbm = pl.BlockSpec(memory_space=pltpu.HBM)
    vmem = pl.BlockSpec(memory_space=pltpu.VMEM)
    dma = pltpu.SemaphoreType.DMA
    scratch = [
        pltpu.VMEM((ntr, nb, zb, oy, ox), F32),
        pltpu.VMEM((2, nb, zb, oy, ox), F32),
        pltpu.VMEM(mix_inverse.shape, BF16),
        pltpu.VMEM(to_ocean.shape, BF16),
        pltpu.VMEM(to_atmos.shape, BF16),
        pltpu.VMEM((ntr + 2, nb, ROWS, ox), BF16),
        pltpu.VMEM((SUBSTEPS, nb, 4, 2 * RIM, ox), BF16),
        pltpu.VMEM((SUBSTEPS, nb, 4, 2 * RIM, ox), BF16),
        pltpu.VMEM((SUBSTEPS, nb, 16, ox), F32),
        pltpu.VMEM((SUBSTEPS, nb, 16, ox), F32),
        pltpu.VMEM((4, nb, zb, oy, ox), F32),
        pltpu.VMEM((ntr, ROWS, 2 * ox), F32),
        pltpu.VMEM((ntr, 2 * ROWS, ox), F32),
        pltpu.VMEM((ntr, zb, oy, ox), BF16),
        pltpu.VMEM((ntr, oy, ox), F32),
        pltpu.VMEM((4, oy, ox), I32),
        pltpu.VMEM((2, 8, ox), I32),
        pltpu.VMEM((2, oy, LANES), I32),
        pltpu.VMEM((ox, 2 * ox), BF16),
        pltpu.VMEM((3, 16, 2 * ox), BF16),
        pltpu.VMEM((ox, 2 * ox), BF16),
        pltpu.VMEM((16, 2 * ox), BF16),
        pltpu.VMEM((2 * ROWS, ROWS), BF16),
        pltpu.VMEM((2 * ROWS, 2 * RIM), BF16),
        pltpu.VMEM((2 * ROWS, ROWS), BF16),
        pltpu.VMEM((2 * ROWS, 2 * RIM), BF16),
        pltpu.VMEM((2 * RIM, ROWS), BF16),
        pltpu.VMEM((4, 16, ox), BF16),
        pltpu.VMEM((slots, slots * oy), BF16),
        pltpu.VMEM((cells, near * slots), BF16),
        pltpu.VMEM((8, cells), F32),
        pltpu.VMEM((near, 8, slots), F32),
        pltpu.VMEM((near, 8, slots), F32),
        pltpu.VMEM((peers, 8, slots), F32),
        pltpu.VMEM((near, 8, slots), F32),
        pltpu.VMEM((oy, ox), I32),
        pltpu.VMEM(atm_flux.shape, BF16),
        pltpu.VMEM(slot_cell.shape, I32),
        pltpu.SMEM(peer_list.shape, I32),
        pltpu.SMEM(peer_count.shape, I32),
        pltpu.SMEM(send_count.shape, I32),
        dma((6,)),
        dma((nb,)),
        dma((nb,)),
        dma((nb,)),
        dma,
        dma,
        dma((SUBSTEPS, 2, nb)),
        dma((SUBSTEPS, 2, nb)),
        dma((SUBSTEPS, 2, nb)),
        dma((SUBSTEPS, 2, nb)),
        dma((4,)),
        dma((4,)),
        dma((near,)),
        dma((near,)),
        dma((near,)),
        dma((near,)),
    ]
    return pl.pallas_call(
        functools.partial(kernel, nty, ntx),
        out_shape=(
            pltpu.VMEM(tracers.shape, F32),
            pltpu.VMEM(atm_flux.shape[1:], F32),
        ),
        in_specs=[hbm] * 11,
        out_specs=(vmem, vmem),
        scratch_shapes=scratch,
        compiler_params=pltpu.CompilerParams(
            collective_id=0, has_side_effects=True, vmem_limit_bytes=62464 * 1024
        ),
        cost_estimate=pl.CostEstimate(flops=10**9, bytes_accessed=26 * 10**6, transcendentals=0),
        name="interval",
    )(
        tracers,
        courant,
        mix_inverse,
        to_ocean,
        to_atmos,
        depth_levels,
        atm_flux,
        slot_cell,
        peer_list,
        peer_count,
        send_count,
    )


def solution(mesh):
    in_specs = (
        P(None, None, "ty", "tx"),
        P(None, None, "ty", "tx"),
        P("ty", "tx"),
        P(None, None, None, "ty", "tx"),
        P(None, None, "ty", "tx"),
        P(None, None, "ty", "tx"),
        P(None, "ty", "tx"),
        P("ty", "tx", None),
        P("ty", "tx", None),
        P("ty", "tx", None),
        P("ty", "tx", None, None),
    )
    out_specs = (P(None, None, "ty", "tx"), P("ty", "tx"))
    part = functools.partial(body, mesh.shape["ty"], mesh.shape["tx"])
    return jax.shard_map(part, mesh=mesh, in_specs=in_specs, out_specs=out_specs, check_vma=False)
```

```python
import functools

import jax
import jax.numpy as jnp
from jax import lax
from jax.experimental import pallas as pl
from jax.experimental.pallas import tpu as pltpu
from jax.sharding import PartitionSpec as P

MESH = pl.DeviceIdType.MESH
F32 = jnp.float32
BF16 = jnp.bfloat16
I32 = jnp.int32
SUBSTEPS = 2
LANES = 128
RIM = 32
ROWS = 256
RGROUP = 5
PAD = 32
TOP = 8
NEAR = tuple((di, dj) for di in (-1, 0, 1) for dj in (-1, 0, 1))


def iota(shape, dim):
    return lax.broadcasted_iota(I32, shape, dim)


def stencil(d):
    return jnp.where((d == 0) | (d == 1), 7.0, jnp.where((d == -1) | (d == 2), -1.0, 0.0))


def nn(a, b):
    return jnp.dot(a, b, preferred_element_type=F32)


def nt(a, b):
    return lax.dot_general(a, b, (((1,), (1,)), ((), ())), preferred_element_type=F32)


def tn(a, b):
    return lax.dot_general(a, b, (((0,), (0,)), ((), ())), preferred_element_type=F32)


def kernel(
    nty,
    ntx,
    tracers,
    courant,
    mix,
    to_ocean,
    to_atmos,
    depth_in,
    atm_in,
    slot_cell_in,
    peer_list_in,
    peer_count_in,
    send_count_in,
    out,
    surf_out,
    qs,
    cx,
    mixv,
    toc,
    toa,
    fld,
    sr,
    hr,
    sc,
    hc,
    coef,
    ux,
    tmp,
    mv,
    forc,
    depx,
    dr,
    dc,
    c_x,
    c_xh,
    c_xs,
    c_xsh,
    c_sel,
    c_selc,
    c_e,
    c_et,
    oh,
    flat,
    pk_s,
    pk_r,
    rt_s,
    rt_r,
    depth,
    atm,
    slot_cell,
    peer_list,
    peer_count,
    send_count,
    s_in,
    s_tr,
    s_cx,
    s_cy,
    s_mix,
    s_toc,
    s_toa,
    row_ss,
    row_rs,
    col_ss,
    col_rs,
    dep_ss,
    dep_rs,
    pk_ss,
    pk_rs,
    rt_ss,
    rt_rs,
):
    nb, zb = mix.shape[:2]
    ntr, _, oy, ox = tracers.shape
    halves = ox // LANES
    own = slice(TOP, TOP + oy)
    peers, slots = to_ocean.shape[0], to_ocean.shape[1]
    i = lax.axis_index("ty")
    j = lax.axis_index("tx")

    def device(di, dj):
        return (lax.rem(i + di + nty, nty), lax.rem(j + dj + ntx, ntx))

    barrier = pltpu.get_barrier_semaphore()
    for di, dj in NEAR:
        if (di, dj) != (0, 0):
            pl.semaphore_signal(barrier, inc=1, device_id=device(di, dj), device_id_type=MESH)

    small = [
        pltpu.make_async_copy(source, target, s_in.at[k])
        for k, (source, target) in enumerate(
            (
                (depth_in, depth),
                (slot_cell_in, slot_cell),
                (atm_in, atm),
                (peer_list_in, peer_list),
                (peer_count_in, peer_count),
                (send_count_in, send_count),
            )
        )
    ]
    small[0].start()
    order = tuple((n + 1) % nb for n in range(nb))

    def loads(b, first):
        made = []
        for h in range(halves):
            lanes = pl.ds(h * LANES, LANES)
            levels = pl.ds(first, zb)
            made += [
                pltpu.make_async_copy(
                    tracers.at[:, levels, :, lanes],
                    qs.at[pl.ds(0, ntr), b, :, h, pl.ds(TOP, oy)],
                    s_tr.at[h, b],
                ),
                pltpu.make_async_copy(
                    courant.at[0, levels, :, lanes], cx.at[b, :, h], s_cx.at[h, b]
                ),
                pltpu.make_async_copy(
                    courant.at[1, levels, :, lanes],
                    qs.at[ntr, b, :, h, pl.ds(TOP, oy)],
                    s_cy.at[h, b],
                ),
            ]
        return made

    for b in order:
        for copy in loads(b, b * zb):
            copy.start()
    for copy in small[1:]:
        copy.start()
    for b in order[:-1]:
        pltpu.make_async_copy(mix.at[b], mixv.at[b], s_mix.at[b]).start()
    pltpu.make_async_copy(to_ocean, toc, s_toc).start()
    pltpu.make_async_copy(mix.at[order[-1]], mixv.at[order[-1]], s_mix.at[order[-1]]).start()
    pltpu.make_async_copy(to_atmos, toa, s_toa).start()

    m = iota((2 * RIM, ROWS), 0)
    n = iota((2 * RIM, ROWS), 1)
    mm = jnp.where(m < RIM, m, m - RIM)
    y = jnp.where(m < RIM, oy - 2 + (mm & 1), mm & 1)
    open_down = jnp.where(i == nty - 1, 0.0, 1.0)
    open_up = jnp.where(i == 0, 0.0, 1.0)
    hit = ((mm >> 1) == (n >> 4)) & ((n & 15) == y)
    c_sel[...] = jnp.where(hit, jnp.where(m < RIM, open_down, open_up), 0.0).astype(BF16)
    r = iota((16, ox), 0)
    n = iota((16, ox), 1)
    open_right = jnp.where(j == ntx - 1, 0.0, 1.0)
    open_left = jnp.where(j == 0, 0.0, 1.0)
    for f in range(4):
        at = jnp.where(r < 8, ox - 2 + r - 2 * f, r - 8 - 2 * f)
        mine = ((r & 7) >> 1) == f
        hit = mine & (at == n)
        c_selc[f] = jnp.where(hit, jnp.where(r < 8, open_right, open_left), 0.0).astype(BF16)
    def depth_copies():
        return (
            pltpu.make_async_remote_copy(
                depth.at[pl.ds(oy - 8, 8)], dr.at[0], dep_ss.at[0], dep_rs.at[0],
                device_id=device(1, 0), device_id_type=MESH,
            ),
            pltpu.make_async_remote_copy(
                depth.at[pl.ds(0, 8)], dr.at[1], dep_ss.at[1], dep_rs.at[1],
                device_id=device(-1, 0), device_id_type=MESH,
            ),
            pltpu.make_async_remote_copy(
                depth.at[:, pl.ds(ox - LANES, LANES)], dc.at[0], dep_ss.at[2], dep_rs.at[2],
                device_id=device(0, 1), device_id_type=MESH,
            ),
            pltpu.make_async_remote_copy(
                depth.at[:, pl.ds(0, LANES)], dc.at[1], dep_ss.at[3], dep_rs.at[3],
                device_id=device(0, -1), device_id_type=MESH,
            ),
        )

    def near_copies(source, target, ss, rs, of):
        made = []
        for k, (di, dj) in enumerate(NEAR):
            if (di, dj) != (0, 0):
                made.append(
                    pltpu.make_async_remote_copy(
                        source.at[of(k, di, dj)], target.at[len(NEAR) - 1 - k], ss.at[k],
                        rs.at[len(NEAR) - 1 - k], device_id=device(di, dj), device_id_type=MESH,
                    )
                )
        return made

    def rim_copies(step, b, fields):
        rows = [
            pltpu.make_async_remote_copy(
                sr.at[step, b, pl.ds(0, fields), pl.ds(s * RIM, RIM)],
                hr.at[step, b, pl.ds(0, fields), pl.ds(s * RIM, RIM)],
                row_ss.at[step, s, b], row_rs.at[step, s, b],
                device_id=device(1 - 2 * s, 0), device_id_type=MESH,
            )
            for s in range(2)
        ]
        cols = [
            pltpu.make_async_remote_copy(
                sc.at[step, b, pl.ds(s * 8, 8)],
                hc.at[step, b, pl.ds(s * 8, 8)],
                col_ss.at[step, s, b], col_rs.at[step, s, b],
                device_id=device(0, 1 - 2 * s), device_id_type=MESH,
            )
            for s in range(2)
        ]
        return rows + cols

    small[0].wait()
    dep = depth[...]

    def pack(step, b, row_fields, col_fields):
        for f, source in enumerate(row_fields):
            sr[step, b, f] = nn(c_sel[...], fld[source, b]).astype(BF16)
        cols = nt(c_selc[0], fld[col_fields[0], b])
        for f in range(1, len(col_fields)):
            cols = cols + nt(c_selc[f], fld[col_fields[f], b])
        sc[step, b] = cols

    def send(step, b, fields):
        for copy in rim_copies(step, b, fields):
            copy.start()

    def fill(b):
        for copy in loads(b, 0):
            copy.wait()
        for h in range(halves):
            lanes = slice(h * LANES, (h + 1) * LANES)
            for f in range(ntr + 2):
                if f == ntr:
                    value = cx[b, :, h]
                else:
                    value = qs[min(f, ntr), b, :, h, own, :]
                fld[f, b, 0 : zb * oy, lanes] = value.reshape(zb * oy, LANES).astype(BF16)
        for f in range(ntr + 2):
            fld[f, b, zb * oy :, :] = jnp.zeros((ROWS - zb * oy, ox), BF16)
        pack(0, b, (0, 1, 2, 4), (0, 1, 2, 3))

    fill(order[0])
    pl.semaphore_wait(barrier, len(NEAR) - 1)
    for copy in depth_copies():
        copy.start()
    send(0, order[0], 4)

    def fill_and_send(idx, carry):
        b = lax.rem(idx + 1, nb)
        fill(b)
        send(0, b, 4)
        return carry

    lax.fori_loop(1, nb, fill_and_send, 0)

    g = iota((ox, 2 * ox), 0)
    n = iota((ox, 2 * ox), 1)
    d = g - jnp.where(n < ox, n, n - ox - 1)
    c_x[...] = stencil(d).astype(BF16)
    c_xs[...] = jnp.where(d == jnp.where(n < ox, 1, 0), 1.0, 0.0).astype(BF16)
    r = iota((16, 2 * ox), 0)
    n = iota((16, 2 * ox), 1)
    x = jnp.where(n < ox, n, n - ox - 1)
    for f in range(4):
        at = jnp.where(r < 8, -2 + r - 2 * f, ox + r - 8 - 2 * f)
        mine = ((r & 7) >> 1) == f
        if f < 3:
            c_xh[f] = jnp.where(mine, stencil(at - x), 0.0).astype(BF16)
        else:
            hit = mine & (at - x == jnp.where(n < ox, 1, 0))
            c_xsh[...] = jnp.where(hit, 1.0, 0.0).astype(BF16)
    r = iota((slots, slots * oy), 0)
    n = iota((slots, slots * oy), 1)
    c_e[...] = jnp.where((n >> 4) == r, 1.0, 0.0).astype(BF16)
    r = iota((slots * oy, slots), 0)
    n = iota((slots * oy, slots), 1)
    c_et[...] = jnp.where((r >> 4) == n, 1.0, 0.0).astype(BF16)

    for copy in small[1:]:
        copy.wait()

    cells = iota((oh.shape[0], slots), 0)
    for k, (di, dj) in enumerate(NEAR):
        ti, tj = device(di, dj)
        row = slot_cell[0, 0, pl.ds(ti * ntx + tj, 1), :]
        oh[:, k * slots : (k + 1) * slots] = jnp.where(cells == row, 1.0, 0.0).astype(BF16)
    flux = atm[...].astype(F32)
    flat[...] = jnp.zeros_like(flat)
    for c in range(flux.shape[0]):
        for r in range(flux.shape[1]):
            flat[c : c + 1, r * LANES : (r + 1) * LANES] = flux[c, r : r + 1, :]
    picks = nn(flat[...].astype(BF16), oh[...])
    for k in range(len(NEAR)):
        pk_s[k] = picks[:, k * slots : (k + 1) * slots]

    for copy in near_copies(pk_s, pk_r, pk_ss, pk_rs, lambda k, di, dj: k):
        copy.start()

    for copy in depth_copies():
        copy.wait()
    south = jnp.where(i == 0, 0, dr[0])
    north = jnp.where(i == nty - 1, 0, dr[1])
    west = jnp.where(j == 0, 0, dc[0])
    east = jnp.where(j == ntx - 1, 0, dc[1])
    wide = jnp.concatenate([dep, east], axis=1)
    depx[0] = pltpu.roll(wide, ox + LANES - 1, 1)[:, :ox]
    wide = jnp.concatenate([west, dep], axis=1)
    depx[1] = pltpu.roll(wide, 1, 1)[:, LANES:]
    tall = jnp.concatenate([dep, north], axis=0)
    depx[2] = pltpu.roll(tall, oy + 7, 0)[:oy]
    tall = jnp.concatenate([south, dep], axis=0)
    depx[3] = pltpu.roll(tall, 1, 0)[8:]

    def wait_rims(step, b, fields):
        for copy in rim_copies(step, b, fields):
            copy.wait()

    def place(step, b, fields):
        for f in range(fields):
            for h in range(halves):
                tmp[f, h] = hr[step, b, f, :, h * LANES : (h + 1) * LANES].astype(F32)
        for f in range(fields):
            for h in range(halves):
                for k in range(zb):
                    qs[f, b, k, h, TOP - 2 : TOP, :] = tmp[f, h, 2 * k : 2 * k + 2, :]
                    qs[f, b, k, h, TOP + oy : TOP + oy + 2, :] = tmp[
                        f, h, RIM + 2 * k : RIM + 2 * k + 2, :
                    ]

    def faces(b):
        ux[0] = nn(fld[ntr, b], c_xs[...]) + tn(hc[0, b].astype(BF16), c_xsh[...])
        for k in range(zb):
            at = b * zb + k
            rows = slice(k * oy, (k + 1) * oy)
            for h in range(halves):
                lanes = slice(h * LANES, (h + 1) * LANES)
                wet = at < depth[:, lanes]
                near_wet = [wet & (at < depx[a, :, lanes]) for a in range(4)]
                x0 = cx[b, k, h]
                y0 = qs[ntr, b, k, h, own, :]
                others = (
                    ux[0, rows, lanes],
                    ux[0, rows, ox + h * LANES : ox + (h + 1) * LANES],
                    qs[ntr, b, k, h, TOP + 1 : TOP + 1 + oy, :],
                    qs[ntr, b, k, h, TOP - 1 : TOP - 1 + oy, :],
                )
                for a in range(4):
                    mean = ((x0, y0)[a // 2] + others[a]) * (1.0 / 24.0)
                    coef[a, b, k, h] = jnp.where(near_wet[a], mean, 0.0)

    def advect(step, b):
        halo = hc[step, b].astype(BF16)
        for t in range(ntr):
            ux[t] = nn(fld[t, b], c_x[...]) + tn(halo, c_xh[t])
        for k in range(zb):
            rows = slice(k * oy, (k + 1) * oy)
            for h in range(halves):
                lanes = slice(h * LANES, (h + 1) * LANES)
                c0, c1, c2, c3 = (coef[a, b, k, h] for a in range(4))
                for t in range(ntr):
                    m2, m1, q0, p1, p2 = (
                        qs[t, b, k, h, TOP + o : TOP + o + oy, :] for o in (-2, -1, 0, 1, 2)
                    )
                    east = c0 * ux[t, rows, lanes]
                    west = c1 * ux[t, rows, ox + h * LANES : ox + (h + 1) * LANES]
                    north = c2 * (7.0 * (q0 + p1) - (m1 + p2))
                    south = c3 * (7.0 * (m1 + q0) - (m2 + p1))
                    if step == 0:
                        q0 = jnp.where((b * zb + k) < depth[:, lanes], q0, 0.0)
                    mv[t, k, h] = q0 - (east - west) - (north - south)

        @pl.when(b == 0)
        def _():
            for t in range(ntr):
                for h in range(halves):
                    lanes = slice(h * LANES, (h + 1) * LANES)
                    mv[t, 0, h] = mv[t, 0, h] + jnp.where(depth[:, lanes] > 0, forc[t, :, lanes], 0.0)

    def mixing(b, keep):
        for h in range(halves):
            lanes = slice(h * LANES, (h + 1) * LANES)
            for first in range(0, zb, RGROUP):
                acc = [[None] * ntr for _ in range(RGROUP)]
                for c in range(zb):
                    moved = [mv[t, c, h] for t in range(ntr)]
                    for r in range(RGROUP):
                        weight = mixv[b, first + r, c, :, lanes].astype(F32)
                        for t in range(ntr):
                            term = weight * moved[t]
                            acc[r][t] = term if c == 0 else acc[r][t] + term
                for r in range(RGROUP):
                    k = first + r
                    wet = (b * zb + k) < depth[:, lanes]
                    for t in range(ntr):
                        value = jnp.where(wet, acc[r][t], 0.0)
                        if keep:
                            qs[t, b, k, h, own, :] = value
                            fld[t, b, k * oy : (k + 1) * oy, lanes] = value.astype(BF16)
                        else:
                            out[t, b * zb + k, :, lanes] = value

    def force():
        for copy in near_copies(pk_s, pk_r, pk_ss, pk_rs, lambda k, di, dj: k):
            copy.wait()
        pltpu.make_async_copy(to_ocean, toc, s_toc).wait()
        mine = pk_s[4]
        chosen = [mine, pk_r[5], pk_r[3]]
        for p, di in ((3, 1), (4, -1)):
            ids = [device(di, dj) for dj in (-1, 0, 1)]
            ids = [a * ntx + b for a, b in ids]
            base = (di + 1) * 3
            e = peer_list[0, 0, p]
            got = jnp.where(e == ids[0], pk_r[base], pk_r[base + 1])
            chosen.append(jnp.where(e == ids[2], pk_r[base + 2], got))
        slot = iota((8, slots), 1)
        y = iota((oy, slots * oy), 0)
        x = iota((oy, slots * oy), 1)
        diagonal = (x & 15) == y
        total = jnp.zeros((ntr * oy, ox), F32)
        live = [jnp.where(slot < peer_count[0, 0, p], chosen[p], 0.0) for p in range(peers)]
        spread = nn(jnp.concatenate(live, axis=0).astype(BF16), c_e[...])
        for p in range(peers):
            left = jnp.concatenate(
                [
                    jnp.where(diagonal, spread[8 * p + c : 8 * p + c + 1, :], 0.0).astype(BF16)
                    for c in range(ntr)
                ],
                axis=0,
            )
            total = total + nn(left, toc[p].reshape(slots * oy, ox))
        for t in range(ntr):
            forc[t] = total[t * oy : (t + 1) * oy]

    def ret_copies():
        of = lambda k, di, dj: {1: 3, -1: 4}[di] if di != 0 else {1: 1, -1: 2}[dj]
        return near_copies(rt_s, rt_r, rt_ss, rt_rs, of)

    def give_back():
        pltpu.make_async_copy(to_atmos, toa, s_toa).wait()
        surface = out[0, 0].astype(BF16)
        y = iota((oy, slots * oy), 0)
        x = iota((oy, slots * oy), 1)
        diagonal = (x & 15) == y
        rows = []
        for p in range(peers):
            sums = nt(surface, toa[p].reshape(slots * oy, ox))
            rows.append(jnp.sum(jnp.where(diagonal, sums, 0.0), axis=0, keepdims=True))
        rows.append(jnp.zeros((8 - peers, slots * oy), F32))
        sums = jnp.concatenate(rows, axis=0)
        high = sums.astype(BF16)
        low = (sums - high.astype(F32)).astype(BF16)
        both = nn(jnp.concatenate([high, low], axis=0), c_et[...])
        both = both[0:8] + both[8:16]
        for p in range(peers):
            rt_s[p] = jnp.broadcast_to(both[p : p + 1], (8, slots))
        for copy in ret_copies():
            copy.start()

    def first_step(idx, carry):
        b = lax.rem(idx + 1, nb)
        wait_rims(0, b, 4)
        place(0, b, ntr + 1)
        faces(b)

        @pl.when(b == 0)
        def _():
            force()

        advect(0, b)
        pltpu.make_async_copy(mix.at[0], mixv.at[b], s_mix.at[b]).wait()
        mixing(b, True)
        pack(1, b, (0, 1, 2), (0, 1, 2))
        send(1, b, 3)
        return carry

    lax.fori_loop(0, nb, first_step, 0)

    def second_step(idx, carry):
        b = jnp.where(idx < 2, 1 - idx, idx)
        wait_rims(1, b, 3)
        place(1, b, ntr)
        advect(1, b)
        mixing(b, False)

        @pl.when(b == 0)
        def _():
            give_back()

        return carry

    lax.fori_loop(0, nb, second_step, 0)

    for copy in ret_copies():
        copy.wait()
    slot = iota((1, slots), 1)
    parts = []
    for k, (di, dj) in enumerate(NEAR):
        ti, tj = device(di, dj)
        value = rt_s[0] if (di, dj) == (0, 0) else rt_r[k]
        kept = slot < send_count[0, 0, ti * ntx + tj]
        parts.append(jnp.where(kept, value, 0.0))
    values = jnp.concatenate(parts, axis=1)
    high = values.astype(BF16)
    low = (values - high.astype(F32)).astype(BF16)
    landed = nt(high, oh[...]) + nt(low, oh[...])
    for r in range(surf_out.shape[0]):
        surf_out[r : r + 1, :] = landed[0:1, r * LANES : (r + 1) * LANES]


def body(
    nty,
    ntx,
    tracers,
    courant,
    depth_levels,
    mix_inverse,
    to_ocean,
    to_atmos,
    atm_flux,
    peer_list,
    peer_count,
    send_count,
    slot_cell,
):
    ntr, levels, oy, ox = tracers.shape
    nb, zb = mix_inverse.shape[:2]
    peers, slots = to_ocean.shape[:2]
    cells = atm_flux.shape[1] * atm_flux.shape[2]
    near = len(NEAR)
    hbm = pl.BlockSpec(memory_space=pltpu.HBM)
    vmem = pl.BlockSpec(memory_space=pltpu.VMEM)
    dma = pltpu.SemaphoreType.DMA
    scratch = [
        pltpu.VMEM((ntr + 1, nb, zb, ox // LANES, PAD, LANES), F32),
        pltpu.VMEM((nb, zb, ox // LANES, oy, LANES), F32),
        pltpu.VMEM(mix_inverse.shape, BF16),
        pltpu.VMEM(to_ocean.shape, BF16),
        pltpu.VMEM(to_atmos.shape, BF16),
        pltpu.VMEM((ntr + 2, nb, ROWS, ox), BF16),
        pltpu.VMEM((SUBSTEPS, nb, 4, 2 * RIM, ox), BF16),
        pltpu.VMEM((SUBSTEPS, nb, 4, 2 * RIM, ox), BF16),
        pltpu.VMEM((SUBSTEPS, nb, 16, ox), F32),
        pltpu.VMEM((SUBSTEPS, nb, 16, ox), F32),
        pltpu.VMEM((4, nb, zb, ox // LANES, oy, LANES), F32),
        pltpu.VMEM((ntr, ROWS, 2 * ox), F32),
        pltpu.VMEM((ntr + 1, ox // LANES, 2 * RIM, LANES), F32),
        pltpu.VMEM((ntr, zb, ox // LANES, oy, LANES), F32),
        pltpu.VMEM((ntr, oy, ox), F32),
        pltpu.VMEM((4, oy, ox), I32),
        pltpu.VMEM((2, 8, ox), I32),
        pltpu.VMEM((2, oy, LANES), I32),
        pltpu.VMEM((ox, 2 * ox), BF16),
        pltpu.VMEM((3, 16, 2 * ox), BF16),
        pltpu.VMEM((ox, 2 * ox), BF16),
        pltpu.VMEM((16, 2 * ox), BF16),
        pltpu.VMEM((2 * RIM, ROWS), BF16),
        pltpu.VMEM((4, 16, ox), BF16),
        pltpu.VMEM((slots, slots * oy), BF16),
        pltpu.VMEM((slots * oy, slots), BF16),
        pltpu.VMEM((cells, near * slots), BF16),
        pltpu.VMEM((8, cells), F32),
        pltpu.VMEM((near, 8, slots), F32),
        pltpu.VMEM((near, 8, slots), F32),
        pltpu.VMEM((peers, 8, slots), F32),
        pltpu.VMEM((near, 8, slots), F32),
        pltpu.VMEM((oy, ox), I32),
        pltpu.VMEM(atm_flux.shape, BF16),
        pltpu.VMEM(slot_cell.shape, I32),
        pltpu.SMEM(peer_list.shape, I32),
        pltpu.SMEM(peer_count.shape, I32),
        pltpu.SMEM(send_count.shape, I32),
        dma((6,)),
        dma((ox // LANES, nb)),
        dma((ox // LANES, nb)),
        dma((ox // LANES, nb)),
        dma((nb,)),
        dma,
        dma,
        dma((SUBSTEPS, 2, nb)),
        dma((SUBSTEPS, 2, nb)),
        dma((SUBSTEPS, 2, nb)),
        dma((SUBSTEPS, 2, nb)),
        dma((4,)),
        dma((4,)),
        dma((near,)),
        dma((near,)),
        dma((near,)),
        dma((near,)),
    ]
    return pl.pallas_call(
        functools.partial(kernel, nty, ntx),
        out_shape=(
            pltpu.VMEM(tracers.shape, F32),
            pltpu.VMEM(atm_flux.shape[1:], F32),
        ),
        in_specs=[hbm] * 11,
        out_specs=(vmem, vmem),
        scratch_shapes=scratch,
        compiler_params=pltpu.CompilerParams(
            collective_id=0, has_side_effects=True, vmem_limit_bytes=62464 * 1024
        ),
        cost_estimate=pl.CostEstimate(flops=10**9, bytes_accessed=26 * 10**6, transcendentals=0),
        name="interval",
    )(
        tracers,
        courant,
        mix_inverse,
        to_ocean,
        to_atmos,
        depth_levels,
        atm_flux,
        slot_cell,
        peer_list,
        peer_count,
        send_count,
    )


def solution(mesh):
    in_specs = (
        P(None, None, "ty", "tx"),
        P(None, None, "ty", "tx"),
        P("ty", "tx"),
        P(None, None, None, "ty", "tx"),
        P(None, None, "ty", "tx"),
        P(None, None, "ty", "tx"),
        P(None, "ty", "tx"),
        P("ty", "tx", None),
        P("ty", "tx", None),
        P("ty", "tx", None),
        P("ty", "tx", None, None),
    )
    out_specs = (P(None, None, "ty", "tx"), P("ty", "tx"))
    part = functools.partial(body, mesh.shape["ty"], mesh.shape["tx"])
    return jax.shard_map(part, mesh=mesh, in_specs=in_specs, out_specs=out_specs, check_vma=False)
```

```python
import functools

import jax
import jax.numpy as jnp
from jax import lax
from jax.experimental import pallas as pl
from jax.experimental.pallas import tpu as pltpu
from jax.sharding import PartitionSpec as P

MESH = pl.DeviceIdType.MESH
F32 = jnp.float32
BF16 = jnp.bfloat16
I32 = jnp.int32
SUBSTEPS = 2
LANES = 128
RIM = 32
ROWS = 256
RGROUP = 5
PAD = 32
TOP = 8
NEAR = tuple((di, dj) for di in (-1, 0, 1) for dj in (-1, 0, 1))


def iota(shape, dim):
    return lax.broadcasted_iota(I32, shape, dim)


def stencil(d):
    return jnp.where((d == 0) | (d == 1), 7.0, jnp.where((d == -1) | (d == 2), -1.0, 0.0))


def nn(a, b):
    return jnp.dot(a, b, preferred_element_type=F32)


def nt(a, b):
    return lax.dot_general(a, b, (((1,), (1,)), ((), ())), preferred_element_type=F32)


def tn(a, b):
    return lax.dot_general(a, b, (((0,), (0,)), ((), ())), preferred_element_type=F32)


def kernel(
    nty,
    ntx,
    tracers,
    courant,
    mix,
    to_ocean,
    to_atmos,
    depth_in,
    atm_in,
    slot_cell_in,
    peer_list_in,
    peer_count_in,
    send_count_in,
    out,
    surf_out,
    qs,
    cx,
    mixv,
    toc,
    toa,
    fld,
    sr,
    hr,
    sc,
    hc,
    coef,
    ux,
    tmp,
    mv,
    forc,
    depx,
    dr,
    dc,
    c_x,
    c_xh,
    c_xs,
    c_xsh,
    c_selc,
    c_e,
    c_et,
    oh,
    flat,
    pk_s,
    pk_r,
    rt_s,
    rt_r,
    depth,
    atm,
    slot_cell,
    peer_list,
    peer_count,
    send_count,
    s_in,
    s_tr,
    s_cx,
    s_cy,
    s_mix,
    s_toc,
    s_toa,
    row_ss,
    row_rs,
    col_ss,
    col_rs,
    dep_ss,
    dep_rs,
    pk_ss,
    pk_rs,
    rt_ss,
    rt_rs,
):
    nb, zb = mix.shape[:2]
    ntr, _, oy, ox = tracers.shape
    halves = ox // LANES
    own = slice(TOP, TOP + oy)
    peers, slots = to_ocean.shape[0], to_ocean.shape[1]
    i = lax.axis_index("ty")
    j = lax.axis_index("tx")

    def device(di, dj):
        return (lax.rem(i + di + nty, nty), lax.rem(j + dj + ntx, ntx))

    barrier = pltpu.get_barrier_semaphore()
    for di, dj in NEAR:
        if (di, dj) != (0, 0):
            pl.semaphore_signal(barrier, inc=1, device_id=device(di, dj), device_id_type=MESH)

    small = [
        pltpu.make_async_copy(source, target, s_in.at[k])
        for k, (source, target) in enumerate(
            (
                (depth_in, depth),
                (slot_cell_in, slot_cell),
                (atm_in, atm),
                (peer_list_in, peer_list),
                (peer_count_in, peer_count),
                (send_count_in, send_count),
            )
        )
    ]
    small[0].start()
    order = tuple((n + 1) % nb for n in range(nb))

    def loads(b, first):
        made = []
        for h in range(halves):
            lanes = pl.ds(h * LANES, LANES)
            levels = pl.ds(first, zb)
            made += [
                pltpu.make_async_copy(
                    tracers.at[:, levels, :, lanes],
                    qs.at[pl.ds(0, ntr), b, :, h, pl.ds(TOP, oy)],
                    s_tr.at[h, b],
                ),
                pltpu.make_async_copy(
                    courant.at[0, levels, :, lanes], cx.at[b, :, h], s_cx.at[h, b]
                ),
                pltpu.make_async_copy(
                    courant.at[1, levels, :, lanes],
                    qs.at[ntr, b, :, h, pl.ds(TOP, oy)],
                    s_cy.at[h, b],
                ),
            ]
        return made

    for b in order:
        for copy in loads(b, b * zb):
            copy.start()
    for copy in small[1:]:
        copy.start()
    for b in order[:-1]:
        pltpu.make_async_copy(mix.at[b], mixv.at[b], s_mix.at[b]).start()
    pltpu.make_async_copy(to_ocean, toc, s_toc).start()
    pltpu.make_async_copy(mix.at[order[-1]], mixv.at[order[-1]], s_mix.at[order[-1]]).start()
    pltpu.make_async_copy(to_atmos, toa, s_toa).start()

    r = iota((16, ox), 0)
    n = iota((16, ox), 1)
    for f in range(4):
        at = jnp.where(r < 8, ox - 2 + r - 2 * f, r - 8 - 2 * f)
        mine = ((r & 7) >> 1) == f
        hit = mine & (at == n)
        c_selc[f] = jnp.where(hit, 1.0, 0.0).astype(BF16)
    sends = (i < nty - 1, i > 0, j < ntx - 1, j > 0)
    takes = (i > 0, i < nty - 1, j > 0, j < ntx - 1)

    def start_all(copies):
        for copy, mine in zip(copies, sends):
            pl.when(mine)(copy.start)

    def wait_all(copies):
        for copy, mine, theirs in zip(copies, sends, takes):
            pl.when(mine)(copy.wait_send)
            pl.when(theirs)(copy.wait_recv)

    def depth_copies():
        return (
            pltpu.make_async_remote_copy(
                depth.at[pl.ds(oy - 8, 8)], dr.at[0], dep_ss.at[0], dep_rs.at[0],
                device_id=device(1, 0), device_id_type=MESH,
            ),
            pltpu.make_async_remote_copy(
                depth.at[pl.ds(0, 8)], dr.at[1], dep_ss.at[1], dep_rs.at[1],
                device_id=device(-1, 0), device_id_type=MESH,
            ),
            pltpu.make_async_remote_copy(
                depth.at[:, pl.ds(ox - LANES, LANES)], dc.at[0], dep_ss.at[2], dep_rs.at[2],
                device_id=device(0, 1), device_id_type=MESH,
            ),
            pltpu.make_async_remote_copy(
                depth.at[:, pl.ds(0, LANES)], dc.at[1], dep_ss.at[3], dep_rs.at[3],
                device_id=device(0, -1), device_id_type=MESH,
            ),
        )

    def near_copies(source, target, ss, rs, of):
        made = []
        for k, (di, dj) in enumerate(NEAR):
            if (di, dj) != (0, 0):
                made.append(
                    pltpu.make_async_remote_copy(
                        source.at[of(k, di, dj)], target.at[len(NEAR) - 1 - k], ss.at[k],
                        rs.at[len(NEAR) - 1 - k], device_id=device(di, dj), device_id_type=MESH,
                    )
                )
        return made

    def rim_copies(step, b, fields):
        rows = [
            pltpu.make_async_remote_copy(
                sr.at[step, b, pl.ds(0, fields), pl.ds(s * RIM, RIM)],
                hr.at[step, b, pl.ds(0, fields), pl.ds(s * RIM, RIM)],
                row_ss.at[step, s, b], row_rs.at[step, s, b],
                device_id=device(1 - 2 * s, 0), device_id_type=MESH,
            )
            for s in range(2)
        ]
        cols = [
            pltpu.make_async_remote_copy(
                sc.at[step, b, pl.ds(s * 8, 8)],
                hc.at[step, b, pl.ds(s * 8, 8)],
                col_ss.at[step, s, b], col_rs.at[step, s, b],
                device_id=device(0, 1 - 2 * s), device_id_type=MESH,
            )
            for s in range(2)
        ]
        return rows + cols

    small[0].wait()
    dep = depth[...]

    def pack(step, b, row_fields, col_fields):
        for f in range(row_fields):
            for h in range(halves):
                for k in range(zb):
                    tmp[f, h, 2 * k : 2 * k + 2, :] = qs[f, b, k, h, TOP + oy - 2 : TOP + oy, :]
                    tmp[f, h, RIM + 2 * k : RIM + 2 * k + 2, :] = qs[f, b, k, h, TOP : TOP + 2, :]
                sr[step, b, f, :, h * LANES : (h + 1) * LANES] = tmp[f, h].astype(BF16)
        cols = nt(c_selc[0], fld[0, b])
        for f in range(1, col_fields):
            cols = cols + nt(c_selc[f], fld[f, b])
        sc[step, b] = cols

    def send(step, b, fields):
        start_all(rim_copies(step, b, fields))

    def fill(b):
        for copy in loads(b, 0):
            copy.wait()
        for h in range(halves):
            lanes = slice(h * LANES, (h + 1) * LANES)
            for f in range(ntr + 1):
                value = cx[b, :, h] if f == ntr else qs[f, b, :, h, own, :]
                fld[f, b, 0 : zb * oy, lanes] = value.reshape(zb * oy, LANES).astype(BF16)
        for f in range(ntr + 1):
            fld[f, b, zb * oy :, :] = jnp.zeros((ROWS - zb * oy, ox), BF16)
        pack(0, b, ntr + 1, ntr + 1)

    tmp[...] = jnp.zeros_like(tmp)
    fill(order[0])

    for s in range(2):
        @pl.when(jnp.logical_not(takes[s]))
        def _():
            hr[:, :, :, s * RIM : (s + 1) * RIM, :] = jnp.zeros((SUBSTEPS, nb, 4, RIM, ox), BF16)
            dr[s] = jnp.zeros((8, ox), I32)

        @pl.when(jnp.logical_not(takes[2 + s]))
        def _():
            hc[:, :, s * 8 : (s + 1) * 8, :] = jnp.zeros((SUBSTEPS, nb, 8, ox), F32)
            dc[s] = jnp.zeros((oy, LANES), I32)

    pl.semaphore_wait(barrier, len(NEAR) - 1)
    start_all(depth_copies())
    send(0, order[0], 4)

    def fill_and_send(idx, carry):
        b = lax.rem(idx + 1, nb)
        fill(b)
        send(0, b, 4)
        return carry

    lax.fori_loop(1, nb, fill_and_send, 0)

    g = iota((ox, 2 * ox), 0)
    n = iota((ox, 2 * ox), 1)
    d = g - jnp.where(n < ox, n, n - ox - 1)
    c_x[...] = stencil(d).astype(BF16)
    c_xs[...] = jnp.where(d == jnp.where(n < ox, 1, 0), 1.0, 0.0).astype(BF16)
    r = iota((16, 2 * ox), 0)
    n = iota((16, 2 * ox), 1)
    x = jnp.where(n < ox, n, n - ox - 1)
    for f in range(4):
        at = jnp.where(r < 8, -2 + r - 2 * f, ox + r - 8 - 2 * f)
        mine = ((r & 7) >> 1) == f
        if f < 3:
            c_xh[f] = jnp.where(mine, stencil(at - x), 0.0).astype(BF16)
        else:
            hit = mine & (at - x == jnp.where(n < ox, 1, 0))
            c_xsh[...] = jnp.where(hit, 1.0, 0.0).astype(BF16)
    r = iota((slots, slots * oy), 0)
    n = iota((slots, slots * oy), 1)
    c_e[...] = jnp.where((n >> 4) == r, 1.0, 0.0).astype(BF16)
    r = iota((slots * oy, slots), 0)
    n = iota((slots * oy, slots), 1)
    c_et[...] = jnp.where((r >> 4) == n, 1.0, 0.0).astype(BF16)

    for copy in small[1:]:
        copy.wait()

    cells = iota((oh.shape[0], slots), 0)
    for k, (di, dj) in enumerate(NEAR):
        ti, tj = device(di, dj)
        row = slot_cell[0, 0, pl.ds(ti * ntx + tj, 1), :]
        oh[:, k * slots : (k + 1) * slots] = jnp.where(cells == row, 1.0, 0.0).astype(BF16)
    flux = atm[...].astype(F32)
    flat[...] = jnp.zeros_like(flat)
    for c in range(flux.shape[0]):
        for r in range(flux.shape[1]):
            flat[c : c + 1, r * LANES : (r + 1) * LANES] = flux[c, r : r + 1, :]
    picks = nn(flat[...].astype(BF16), oh[...])
    for k in range(len(NEAR)):
        pk_s[k] = picks[:, k * slots : (k + 1) * slots]

    for copy in near_copies(pk_s, pk_r, pk_ss, pk_rs, lambda k, di, dj: k):
        copy.start()

    wait_all(depth_copies())
    south, north, west, east = dr[0], dr[1], dc[0], dc[1]
    wide = jnp.concatenate([dep, east], axis=1)
    depx[0] = pltpu.roll(wide, ox + LANES - 1, 1)[:, :ox]
    wide = jnp.concatenate([west, dep], axis=1)
    depx[1] = pltpu.roll(wide, 1, 1)[:, LANES:]
    tall = jnp.concatenate([dep, north], axis=0)
    depx[2] = pltpu.roll(tall, oy + 7, 0)[:oy]
    tall = jnp.concatenate([south, dep], axis=0)
    depx[3] = pltpu.roll(tall, 1, 0)[8:]

    def wait_rims(step, b, fields):
        wait_all(rim_copies(step, b, fields))

    def place(step, b, fields):
        for f in range(fields):
            for h in range(halves):
                tmp[f, h] = hr[step, b, f, :, h * LANES : (h + 1) * LANES].astype(F32)
        for f in range(fields):
            for h in range(halves):
                for k in range(zb):
                    qs[f, b, k, h, TOP - 2 : TOP, :] = tmp[f, h, 2 * k : 2 * k + 2, :]
                    qs[f, b, k, h, TOP + oy : TOP + oy + 2, :] = tmp[
                        f, h, RIM + 2 * k : RIM + 2 * k + 2, :
                    ]

    def faces(b):
        ux[0] = nn(fld[ntr, b], c_xs[...]) + tn(hc[0, b].astype(BF16), c_xsh[...])
        for k in range(zb):
            at = b * zb + k
            rows = slice(k * oy, (k + 1) * oy)
            for h in range(halves):
                lanes = slice(h * LANES, (h + 1) * LANES)
                wet = at < depth[:, lanes]
                near_wet = [wet & (at < depx[a, :, lanes]) for a in range(4)]
                x0 = cx[b, k, h]
                y0 = qs[ntr, b, k, h, own, :]
                others = (
                    ux[0, rows, lanes],
                    ux[0, rows, ox + h * LANES : ox + (h + 1) * LANES],
                    qs[ntr, b, k, h, TOP + 1 : TOP + 1 + oy, :],
                    qs[ntr, b, k, h, TOP - 1 : TOP - 1 + oy, :],
                )
                for a in range(4):
                    mean = ((x0, y0)[a // 2] + others[a]) * (1.0 / 24.0)
                    coef[a, b, k, h] = jnp.where(near_wet[a], mean, 0.0)

    def advect(step, b):
        halo = hc[step, b].astype(BF16)
        for t in range(ntr):
            ux[t] = nn(fld[t, b], c_x[...]) + tn(halo, c_xh[t])
        for k in range(zb):
            rows = slice(k * oy, (k + 1) * oy)
            for h in range(halves):
                lanes = slice(h * LANES, (h + 1) * LANES)
                c0, c1, c2, c3 = (coef[a, b, k, h] for a in range(4))
                for t in range(ntr):
                    m2, m1, q0, p1, p2 = (
                        qs[t, b, k, h, TOP + o : TOP + o + oy, :] for o in (-2, -1, 0, 1, 2)
                    )
                    east = c0 * ux[t, rows, lanes]
                    west = c1 * ux[t, rows, ox + h * LANES : ox + (h + 1) * LANES]
                    north = c2 * (7.0 * (q0 + p1) - (m1 + p2))
                    south = c3 * (7.0 * (m1 + q0) - (m2 + p1))
                    if step == 0:
                        q0 = jnp.where((b * zb + k) < depth[:, lanes], q0, 0.0)
                    mv[t, k, h] = q0 - (east - west) - (north - south)

        @pl.when(b == 0)
        def _():
            for t in range(ntr):
                for h in range(halves):
                    lanes = slice(h * LANES, (h + 1) * LANES)
                    mv[t, 0, h] = mv[t, 0, h] + jnp.where(depth[:, lanes] > 0, forc[t, :, lanes], 0.0)

    def mixing(b, keep):
        for h in range(halves):
            lanes = slice(h * LANES, (h + 1) * LANES)
            for first in range(0, zb, RGROUP):
                acc = [[None] * ntr for _ in range(RGROUP)]
                for c in range(zb):
                    moved = [mv[t, c, h] for t in range(ntr)]
                    for r in range(RGROUP):
                        weight = mixv[b, first + r, c, :, lanes].astype(F32)
                        for t in range(ntr):
                            term = weight * moved[t]
                            acc[r][t] = term if c == 0 else acc[r][t] + term
                for r in range(RGROUP):
                    k = first + r
                    wet = (b * zb + k) < depth[:, lanes]
                    for t in range(ntr):
                        value = jnp.where(wet, acc[r][t], 0.0)
                        if keep:
                            qs[t, b, k, h, own, :] = value
                            fld[t, b, k * oy : (k + 1) * oy, lanes] = value.astype(BF16)
                        else:
                            out[t, b * zb + k, :, lanes] = value

    def force():
        for copy in near_copies(pk_s, pk_r, pk_ss, pk_rs, lambda k, di, dj: k):
            copy.wait()
        pltpu.make_async_copy(to_ocean, toc, s_toc).wait()
        mine = pk_s[4]
        chosen = [mine, pk_r[5], pk_r[3]]
        for p, di in ((3, 1), (4, -1)):
            ids = [device(di, dj) for dj in (-1, 0, 1)]
            ids = [a * ntx + b for a, b in ids]
            base = (di + 1) * 3
            e = peer_list[0, 0, p]
            got = jnp.where(e == ids[0], pk_r[base], pk_r[base + 1])
            chosen.append(jnp.where(e == ids[2], pk_r[base + 2], got))
        slot = iota((8, slots), 1)
        y = iota((oy, slots * oy), 0)
        x = iota((oy, slots * oy), 1)
        diagonal = (x & 15) == y
        total = jnp.zeros((ntr * oy, ox), F32)
        live = [jnp.where(slot < peer_count[0, 0, p], chosen[p], 0.0) for p in range(peers)]
        spread = nn(jnp.concatenate(live, axis=0).astype(BF16), c_e[...])
        for p in range(peers):
            left = jnp.concatenate(
                [
                    jnp.where(diagonal, spread[8 * p + c : 8 * p + c + 1, :], 0.0).astype(BF16)
                    for c in range(ntr)
                ],
                axis=0,
            )
            total = total + nn(left, toc[p].reshape(slots * oy, ox))
        for t in range(ntr):
            forc[t] = total[t * oy : (t + 1) * oy]

    def ret_copies():
        of = lambda k, di, dj: {1: 3, -1: 4}[di] if di != 0 else {1: 1, -1: 2}[dj]
        return near_copies(rt_s, rt_r, rt_ss, rt_rs, of)

    def give_back():
        pltpu.make_async_copy(to_atmos, toa, s_toa).wait()
        surface = out[0, 0].astype(BF16)
        y = iota((oy, slots * oy), 0)
        x = iota((oy, slots * oy), 1)
        diagonal = (x & 15) == y
        rows = []
        for p in range(peers):
            sums = nt(surface, toa[p].reshape(slots * oy, ox))
            rows.append(jnp.sum(jnp.where(diagonal, sums, 0.0), axis=0, keepdims=True))
        rows.append(jnp.zeros((8 - peers, slots * oy), F32))
        sums = jnp.concatenate(rows, axis=0)
        high = sums.astype(BF16)
        low = (sums - high.astype(F32)).astype(BF16)
        both = nn(jnp.concatenate([high, low], axis=0), c_et[...])
        both = both[0:8] + both[8:16]
        for p in range(peers):
            rt_s[p] = jnp.broadcast_to(both[p : p + 1], (8, slots))
        for copy in ret_copies():
            copy.start()

    def first_step(idx, carry):
        b = lax.rem(idx + 1, nb)
        wait_rims(0, b, 4)
        place(0, b, ntr + 1)
        faces(b)

        @pl.when(b == 0)
        def _():
            force()

        advect(0, b)
        pltpu.make_async_copy(mix.at[0], mixv.at[b], s_mix.at[b]).wait()
        mixing(b, True)
        pack(1, b, ntr, ntr)
        send(1, b, 3)
        return carry

    lax.fori_loop(0, nb, first_step, 0)

    def second_step(idx, carry):
        b = jnp.where(idx < 2, 1 - idx, idx)
        wait_rims(1, b, 3)
        place(1, b, ntr)
        advect(1, b)
        mixing(b, False)

        @pl.when(b == 0)
        def _():
            give_back()

        return carry

    lax.fori_loop(0, nb, second_step, 0)

    for copy in ret_copies():
        copy.wait()
    slot = iota((1, slots), 1)
    parts = []
    for k, (di, dj) in enumerate(NEAR):
        ti, tj = device(di, dj)
        value = rt_s[0] if (di, dj) == (0, 0) else rt_r[k]
        kept = slot < send_count[0, 0, ti * ntx + tj]
        parts.append(jnp.where(kept, value, 0.0))
    values = jnp.concatenate(parts, axis=1)
    high = values.astype(BF16)
    low = (values - high.astype(F32)).astype(BF16)
    landed = nt(high, oh[...]) + nt(low, oh[...])
    for r in range(surf_out.shape[0]):
        surf_out[r : r + 1, :] = landed[0:1, r * LANES : (r + 1) * LANES]


def body(
    nty,
    ntx,
    tracers,
    courant,
    depth_levels,
    mix_inverse,
    to_ocean,
    to_atmos,
    atm_flux,
    peer_list,
    peer_count,
    send_count,
    slot_cell,
):
    ntr, levels, oy, ox = tracers.shape
    nb, zb = mix_inverse.shape[:2]
    peers, slots = to_ocean.shape[:2]
    cells = atm_flux.shape[1] * atm_flux.shape[2]
    near = len(NEAR)
    hbm = pl.BlockSpec(memory_space=pltpu.HBM)
    vmem = pl.BlockSpec(memory_space=pltpu.VMEM)
    dma = pltpu.SemaphoreType.DMA
    scratch = [
        pltpu.VMEM((ntr + 1, nb, zb, ox // LANES, PAD, LANES), F32),
        pltpu.VMEM((nb, zb, ox // LANES, oy, LANES), F32),
        pltpu.VMEM(mix_inverse.shape, BF16),
        pltpu.VMEM(to_ocean.shape, BF16),
        pltpu.VMEM(to_atmos.shape, BF16),
        pltpu.VMEM((ntr + 1, nb, ROWS, ox), BF16),
        pltpu.VMEM((SUBSTEPS, nb, 4, 2 * RIM, ox), BF16),
        pltpu.VMEM((SUBSTEPS, nb, 4, 2 * RIM, ox), BF16),
        pltpu.VMEM((SUBSTEPS, nb, 16, ox), F32),
        pltpu.VMEM((SUBSTEPS, nb, 16, ox), F32),
        pltpu.VMEM((4, nb, zb, ox // LANES, oy, LANES), F32),
        pltpu.VMEM((ntr, ROWS, 2 * ox), F32),
        pltpu.VMEM((ntr + 1, ox // LANES, 2 * RIM, LANES), F32),
        pltpu.VMEM((ntr, zb, ox // LANES, oy, LANES), F32),
        pltpu.VMEM((ntr, oy, ox), F32),
        pltpu.VMEM((4, oy, ox), I32),
        pltpu.VMEM((2, 8, ox), I32),
        pltpu.VMEM((2, oy, LANES), I32),
        pltpu.VMEM((ox, 2 * ox), BF16),
        pltpu.VMEM((3, 16, 2 * ox), BF16),
        pltpu.VMEM((ox, 2 * ox), BF16),
        pltpu.VMEM((16, 2 * ox), BF16),
        pltpu.VMEM((4, 16, ox), BF16),
        pltpu.VMEM((slots, slots * oy), BF16),
        pltpu.VMEM((slots * oy, slots), BF16),
        pltpu.VMEM((cells, near * slots), BF16),
        pltpu.VMEM((8, cells), F32),
        pltpu.VMEM((near, 8, slots), F32),
        pltpu.VMEM((near, 8, slots), F32),
        pltpu.VMEM((peers, 8, slots), F32),
        pltpu.VMEM((near, 8, slots), F32),
        pltpu.VMEM((oy, ox), I32),
        pltpu.VMEM(atm_flux.shape, BF16),
        pltpu.VMEM(slot_cell.shape, I32),
        pltpu.SMEM(peer_list.shape, I32),
        pltpu.SMEM(peer_count.shape, I32),
        pltpu.SMEM(send_count.shape, I32),
        dma((6,)),
        dma((ox // LANES, nb)),
        dma((ox // LANES, nb)),
        dma((ox // LANES, nb)),
        dma((nb,)),
        dma,
        dma,
        dma((SUBSTEPS, 2, nb)),
        dma((SUBSTEPS, 2, nb)),
        dma((SUBSTEPS, 2, nb)),
        dma((SUBSTEPS, 2, nb)),
        dma((4,)),
        dma((4,)),
        dma((near,)),
        dma((near,)),
        dma((near,)),
        dma((near,)),
    ]
    return pl.pallas_call(
        functools.partial(kernel, nty, ntx),
        out_shape=(
            pltpu.VMEM(tracers.shape, F32),
            pltpu.VMEM(atm_flux.shape[1:], F32),
        ),
        in_specs=[hbm] * 11,
        out_specs=(vmem, vmem),
        scratch_shapes=scratch,
        compiler_params=pltpu.CompilerParams(
            collective_id=0, has_side_effects=True, vmem_limit_bytes=62464 * 1024
        ),
        cost_estimate=pl.CostEstimate(flops=10**9, bytes_accessed=26 * 10**6, transcendentals=0),
        name="interval",
    )(
        tracers,
        courant,
        mix_inverse,
        to_ocean,
        to_atmos,
        depth_levels,
        atm_flux,
        slot_cell,
        peer_list,
        peer_count,
        send_count,
    )


def solution(mesh):
    in_specs = (
        P(None, None, "ty", "tx"),
        P(None, None, "ty", "tx"),
        P("ty", "tx"),
        P(None, None, None, "ty", "tx"),
        P(None, None, "ty", "tx"),
        P(None, None, "ty", "tx"),
        P(None, "ty", "tx"),
        P("ty", "tx", None),
        P("ty", "tx", None),
        P("ty", "tx", None),
        P("ty", "tx", None, None),
    )
    out_specs = (P(None, None, "ty", "tx"), P("ty", "tx"))
    part = functools.partial(body, mesh.shape["ty"], mesh.shape["tx"])
    return jax.shard_map(part, mesh=mesh, in_specs=in_specs, out_specs=out_specs, check_vma=False)
```

```python
import functools

import jax
import jax.numpy as jnp
from jax import lax
from jax.experimental import pallas as pl
from jax.experimental.pallas import tpu as pltpu
from jax.sharding import PartitionSpec as P

MESH = pl.DeviceIdType.MESH
F32 = jnp.float32
BF16 = jnp.bfloat16
I32 = jnp.int32
SUBSTEPS = 2
LANES = 128
RIM = 32
ROWS = 256
RGROUP = 5
PAD = 32
TOP = 8
NEAR = tuple((di, dj) for di in (-1, 0, 1) for dj in (-1, 0, 1))


def iota(shape, dim):
    return lax.broadcasted_iota(I32, shape, dim)


def stencil(d):
    return jnp.where((d == 0) | (d == 1), 7.0, jnp.where((d == -1) | (d == 2), -1.0, 0.0))


def nn(a, b):
    return jnp.dot(a, b, preferred_element_type=F32)


def nt(a, b):
    return lax.dot_general(a, b, (((1,), (1,)), ((), ())), preferred_element_type=F32)


def tn(a, b):
    return lax.dot_general(a, b, (((0,), (0,)), ((), ())), preferred_element_type=F32)


def kernel(
    nty,
    ntx,
    tracers,
    courant,
    mix,
    to_ocean,
    to_atmos,
    depth_in,
    atm_in,
    slot_cell_in,
    peer_list_in,
    peer_count_in,
    send_count_in,
    out,
    surf_out,
    qs,
    cx,
    mixv,
    toc,
    toa,
    fld,
    sr,
    hr,
    sc,
    hc,
    coef,
    ux,
    tmp,
    mv,
    forc,
    depx,
    dr,
    dc,
    c_x,
    c_xh,
    c_xs,
    c_xsh,
    c_selc,
    c_e,
    c_et,
    oh,
    flat,
    pk_s,
    pk_r,
    rt_s,
    rt_r,
    depth,
    atm,
    slot_cell,
    peer_list,
    peer_count,
    send_count,
    s_in,
    s_tr,
    s_cx,
    s_cy,
    s_mix,
    s_toc,
    s_toa,
    row_ss,
    row_rs,
    col_ss,
    col_rs,
    dep_ss,
    dep_rs,
    pk_ss,
    pk_rs,
    rt_ss,
    rt_rs,
):
    nb, zb = mix.shape[:2]
    ntr, _, oy, ox = tracers.shape
    halves = ox // LANES
    own = slice(TOP, TOP + oy)
    peers, slots = to_ocean.shape[0], to_ocean.shape[1]
    i = lax.axis_index("ty")
    j = lax.axis_index("tx")

    def device(di, dj):
        return (lax.rem(i + di + nty, nty), lax.rem(j + dj + ntx, ntx))

    barrier = pltpu.get_barrier_semaphore()
    for di, dj in NEAR:
        if (di, dj) != (0, 0):
            pl.semaphore_signal(barrier, inc=1, device_id=device(di, dj), device_id_type=MESH)

    small = [
        pltpu.make_async_copy(source, target, s_in.at[k])
        for k, (source, target) in enumerate(
            (
                (depth_in, depth),
                (slot_cell_in, slot_cell),
                (atm_in, atm),
                (peer_list_in, peer_list),
                (peer_count_in, peer_count),
                (send_count_in, send_count),
            )
        )
    ]
    small[0].start()
    order = (1, 0) + tuple(range(2, nb))

    def loads(b, first):
        made = []
        for h in range(halves):
            lanes = pl.ds(h * LANES, LANES)
            levels = pl.ds(first, zb)
            made += [
                pltpu.make_async_copy(
                    tracers.at[:, levels, :, lanes],
                    qs.at[pl.ds(0, ntr), b, :, h, pl.ds(TOP, oy)],
                    s_tr.at[h, b],
                ),
                pltpu.make_async_copy(
                    courant.at[0, levels, :, lanes], cx.at[b, :, h], s_cx.at[h, b]
                ),
                pltpu.make_async_copy(
                    courant.at[1, levels, :, lanes],
                    qs.at[ntr, b, :, h, pl.ds(TOP, oy)],
                    s_cy.at[h, b],
                ),
            ]
        return made

    for b in order:
        for copy in loads(b, b * zb):
            copy.start()
    for copy in small[1:]:
        copy.start()
    pltpu.make_async_copy(mix.at[order[0]], mixv.at[order[0]], s_mix.at[order[0]]).start()
    pltpu.make_async_copy(to_ocean, toc, s_toc).start()
    for b in order[1:]:
        pltpu.make_async_copy(mix.at[b], mixv.at[b], s_mix.at[b]).start()
    pltpu.make_async_copy(to_atmos, toa, s_toa).start()

    r = iota((16, ox), 0)
    n = iota((16, ox), 1)
    for f in range(4):
        at = jnp.where(r < 8, ox - 2 + r - 2 * f, r - 8 - 2 * f)
        mine = ((r & 7) >> 1) == f
        hit = mine & (at == n)
        c_selc[f] = jnp.where(hit, 1.0, 0.0).astype(BF16)
    sends = (i < nty - 1, i > 0, j < ntx - 1, j > 0)
    takes = (i > 0, i < nty - 1, j > 0, j < ntx - 1)

    def start_all(copies):
        for copy, mine in zip(copies, sends):
            pl.when(mine)(copy.start)

    def wait_all(copies):
        for copy, mine, theirs in zip(copies, sends, takes):
            pl.when(mine)(copy.wait_send)
            pl.when(theirs)(copy.wait_recv)

    def depth_copies():
        return (
            pltpu.make_async_remote_copy(
                depth.at[pl.ds(oy - 8, 8)], dr.at[0], dep_ss.at[0], dep_rs.at[0],
                device_id=device(1, 0), device_id_type=MESH,
            ),
            pltpu.make_async_remote_copy(
                depth.at[pl.ds(0, 8)], dr.at[1], dep_ss.at[1], dep_rs.at[1],
                device_id=device(-1, 0), device_id_type=MESH,
            ),
            pltpu.make_async_remote_copy(
                depth.at[:, pl.ds(ox - LANES, LANES)], dc.at[0], dep_ss.at[2], dep_rs.at[2],
                device_id=device(0, 1), device_id_type=MESH,
            ),
            pltpu.make_async_remote_copy(
                depth.at[:, pl.ds(0, LANES)], dc.at[1], dep_ss.at[3], dep_rs.at[3],
                device_id=device(0, -1), device_id_type=MESH,
            ),
        )

    def near_copies(source, target, ss, rs, of):
        made = []
        for k, (di, dj) in enumerate(NEAR):
            if (di, dj) != (0, 0):
                made.append(
                    pltpu.make_async_remote_copy(
                        source.at[of(k, di, dj)], target.at[len(NEAR) - 1 - k], ss.at[k],
                        rs.at[len(NEAR) - 1 - k], device_id=device(di, dj), device_id_type=MESH,
                    )
                )
        return made

    def rim_copies(step, b, fields):
        rows = [
            pltpu.make_async_remote_copy(
                sr.at[step, b, pl.ds(0, fields), pl.ds(s * RIM, RIM)],
                hr.at[step, b, pl.ds(0, fields), pl.ds(s * RIM, RIM)],
                row_ss.at[step, s, b], row_rs.at[step, s, b],
                device_id=device(1 - 2 * s, 0), device_id_type=MESH,
            )
            for s in range(2)
        ]
        cols = [
            pltpu.make_async_remote_copy(
                sc.at[step, b, pl.ds(s * 8, 8)],
                hc.at[step, b, pl.ds(s * 8, 8)],
                col_ss.at[step, s, b], col_rs.at[step, s, b],
                device_id=device(0, 1 - 2 * s), device_id_type=MESH,
            )
            for s in range(2)
        ]
        return rows + cols

    small[0].wait()
    dep = depth[...]

    def pack(step, b, row_fields, col_fields):
        for f in range(row_fields):
            for h in range(halves):
                for k in range(zb):
                    tmp[f, h, 2 * k : 2 * k + 2, :] = qs[f, b, k, h, TOP + oy - 2 : TOP + oy, :]
                    tmp[f, h, RIM + 2 * k : RIM + 2 * k + 2, :] = qs[f, b, k, h, TOP : TOP + 2, :]
                sr[step, b, f, :, h * LANES : (h + 1) * LANES] = tmp[f, h].astype(BF16)
        cols = nt(c_selc[0], fld[0, b])
        for f in range(1, col_fields):
            cols = cols + nt(c_selc[f], fld[f, b])
        sc[step, b] = cols

    def send(step, b, fields):
        start_all(rim_copies(step, b, fields))

    def fill(b):
        for copy in loads(b, 0):
            copy.wait()
        for h in range(halves):
            lanes = slice(h * LANES, (h + 1) * LANES)
            for f in range(ntr + 1):
                value = cx[b, :, h] if f == ntr else qs[f, b, :, h, own, :]
                fld[f, b, 0 : zb * oy, lanes] = value.reshape(zb * oy, LANES).astype(BF16)
        for f in range(ntr + 1):
            fld[f, b, zb * oy :, :] = jnp.zeros((ROWS - zb * oy, ox), BF16)
        pack(0, b, ntr + 1, ntr + 1)

    tmp[...] = jnp.zeros_like(tmp)
    fill(order[0])

    for s in range(2):
        @pl.when(jnp.logical_not(takes[s]))
        def _():
            hr[:, :, :, s * RIM : (s + 1) * RIM, :] = jnp.zeros((SUBSTEPS, nb, 4, RIM, ox), BF16)
            dr[s] = jnp.zeros((8, ox), I32)

        @pl.when(jnp.logical_not(takes[2 + s]))
        def _():
            hc[:, :, s * 8 : (s + 1) * 8, :] = jnp.zeros((SUBSTEPS, nb, 8, ox), F32)
            dc[s] = jnp.zeros((oy, LANES), I32)

    pl.semaphore_wait(barrier, len(NEAR) - 1)
    start_all(depth_copies())
    send(0, order[0], 4)

    def fill_and_send(idx, carry):
        b = jnp.where(idx < 2, 1 - idx, idx)
        fill(b)
        send(0, b, 4)
        return carry

    lax.fori_loop(1, nb, fill_and_send, 0)

    for copy in small[1:]:
        copy.wait()

    cells = iota((oh.shape[0], slots), 0)
    for k, (di, dj) in enumerate(NEAR):
        ti, tj = device(di, dj)
        row = slot_cell[0, 0, pl.ds(ti * ntx + tj, 1), :]
        oh[:, k * slots : (k + 1) * slots] = jnp.where(cells == row, 1.0, 0.0).astype(BF16)
    flux = atm[...].astype(F32)
    flat[...] = jnp.zeros_like(flat)
    for c in range(flux.shape[0]):
        for r in range(flux.shape[1]):
            flat[c : c + 1, r * LANES : (r + 1) * LANES] = flux[c, r : r + 1, :]
    picks = nn(flat[...].astype(BF16), oh[...])
    for k in range(len(NEAR)):
        pk_s[k] = picks[:, k * slots : (k + 1) * slots]

    for copy in near_copies(pk_s, pk_r, pk_ss, pk_rs, lambda k, di, dj: k):
        copy.start()

    g = iota((ox, 2 * ox), 0)
    n = iota((ox, 2 * ox), 1)
    d = g - jnp.where(n < ox, n, n - ox - 1)
    c_x[...] = stencil(d).astype(BF16)
    c_xs[...] = jnp.where(d == jnp.where(n < ox, 1, 0), 1.0, 0.0).astype(BF16)
    r = iota((16, 2 * ox), 0)
    n = iota((16, 2 * ox), 1)
    x = jnp.where(n < ox, n, n - ox - 1)
    for f in range(4):
        at = jnp.where(r < 8, -2 + r - 2 * f, ox + r - 8 - 2 * f)
        mine = ((r & 7) >> 1) == f
        if f < 3:
            c_xh[f] = jnp.where(mine, stencil(at - x), 0.0).astype(BF16)
        else:
            hit = mine & (at - x == jnp.where(n < ox, 1, 0))
            c_xsh[...] = jnp.where(hit, 1.0, 0.0).astype(BF16)
    r = iota((slots, slots * oy), 0)
    n = iota((slots, slots * oy), 1)
    c_e[...] = jnp.where((n >> 4) == r, 1.0, 0.0).astype(BF16)
    r = iota((slots * oy, slots), 0)
    n = iota((slots * oy, slots), 1)
    c_et[...] = jnp.where((r >> 4) == n, 1.0, 0.0).astype(BF16)

    wait_all(depth_copies())
    south, north, west, east = dr[0], dr[1], dc[0], dc[1]
    wide = jnp.concatenate([dep, east], axis=1)
    depx[0] = pltpu.roll(wide, ox + LANES - 1, 1)[:, :ox]
    wide = jnp.concatenate([west, dep], axis=1)
    depx[1] = pltpu.roll(wide, 1, 1)[:, LANES:]
    tall = jnp.concatenate([dep, north], axis=0)
    depx[2] = pltpu.roll(tall, oy + 7, 0)[:oy]
    tall = jnp.concatenate([south, dep], axis=0)
    depx[3] = pltpu.roll(tall, 1, 0)[8:]

    def wait_rims(step, b, fields):
        wait_all(rim_copies(step, b, fields))

    def place(step, b, fields):
        for f in range(fields):
            for h in range(halves):
                tmp[f, h] = hr[step, b, f, :, h * LANES : (h + 1) * LANES].astype(F32)
        for f in range(fields):
            for h in range(halves):
                for k in range(zb):
                    qs[f, b, k, h, TOP - 2 : TOP, :] = tmp[f, h, 2 * k : 2 * k + 2, :]
                    qs[f, b, k, h, TOP + oy : TOP + oy + 2, :] = tmp[
                        f, h, RIM + 2 * k : RIM + 2 * k + 2, :
                    ]

    def faces(b):
        ux[0] = nn(fld[ntr, b], c_xs[...]) + tn(hc[0, b].astype(BF16), c_xsh[...])
        for k in range(zb):
            at = b * zb + k
            rows = slice(k * oy, (k + 1) * oy)
            for h in range(halves):
                lanes = slice(h * LANES, (h + 1) * LANES)
                wet = at < depth[:, lanes]
                near_wet = [wet & (at < depx[a, :, lanes]) for a in range(4)]
                x0 = cx[b, k, h]
                y0 = qs[ntr, b, k, h, own, :]
                others = (
                    ux[0, rows, lanes],
                    ux[0, rows, ox + h * LANES : ox + (h + 1) * LANES],
                    qs[ntr, b, k, h, TOP + 1 : TOP + 1 + oy, :],
                    qs[ntr, b, k, h, TOP - 1 : TOP - 1 + oy, :],
                )
                for a in range(4):
                    mean = ((x0, y0)[a // 2] + others[a]) * (1.0 / 24.0)
                    coef[a, b, k, h] = jnp.where(near_wet[a], mean, 0.0)

    def advect(step, b):
        halo = hc[step, b].astype(BF16)
        for t in range(ntr):
            ux[t] = nn(fld[t, b], c_x[...]) + tn(halo, c_xh[t])
        for k in range(zb):
            rows = slice(k * oy, (k + 1) * oy)
            for h in range(halves):
                lanes = slice(h * LANES, (h + 1) * LANES)
                c0, c1, c2, c3 = (coef[a, b, k, h] for a in range(4))
                for t in range(ntr):
                    m2, m1, q0, p1, p2 = (
                        qs[t, b, k, h, TOP + o : TOP + o + oy, :] for o in (-2, -1, 0, 1, 2)
                    )
                    east = c0 * ux[t, rows, lanes]
                    west = c1 * ux[t, rows, ox + h * LANES : ox + (h + 1) * LANES]
                    north = c2 * (7.0 * (q0 + p1) - (m1 + p2))
                    south = c3 * (7.0 * (m1 + q0) - (m2 + p1))
                    if step == 0:
                        q0 = jnp.where((b * zb + k) < depth[:, lanes], q0, 0.0)
                    mv[t, k, h] = q0 - (east - west) - (north - south)

        @pl.when(b == 0)
        def _():
            for t in range(ntr):
                for h in range(halves):
                    lanes = slice(h * LANES, (h + 1) * LANES)
                    mv[t, 0, h] = mv[t, 0, h] + jnp.where(depth[:, lanes] > 0, forc[t, :, lanes], 0.0)

    def mixing(b, keep):
        for h in range(halves):
            lanes = slice(h * LANES, (h + 1) * LANES)
            for first in range(0, zb, RGROUP):
                acc = [[None] * ntr for _ in range(RGROUP)]
                for c in range(zb):
                    moved = [mv[t, c, h] for t in range(ntr)]
                    for r in range(RGROUP):
                        weight = mixv[b, first + r, c, :, lanes].astype(F32)
                        for t in range(ntr):
                            term = weight * moved[t]
                            acc[r][t] = term if c == 0 else acc[r][t] + term
                for r in range(RGROUP):
                    k = first + r
                    wet = (b * zb + k) < depth[:, lanes]
                    for t in range(ntr):
                        value = jnp.where(wet, acc[r][t], 0.0)
                        if keep:
                            qs[t, b, k, h, own, :] = value
                            fld[t, b, k * oy : (k + 1) * oy, lanes] = value.astype(BF16)
                        else:
                            out[t, b * zb + k, :, lanes] = value

    def force():
        for copy in near_copies(pk_s, pk_r, pk_ss, pk_rs, lambda k, di, dj: k):
            copy.wait()
        pltpu.make_async_copy(to_ocean, toc, s_toc).wait()
        mine = pk_s[4]
        chosen = [mine, pk_r[5], pk_r[3]]
        for p, di in ((3, 1), (4, -1)):
            ids = [device(di, dj) for dj in (-1, 0, 1)]
            ids = [a * ntx + b for a, b in ids]
            base = (di + 1) * 3
            e = peer_list[0, 0, p]
            got = jnp.where(e == ids[0], pk_r[base], pk_r[base + 1])
            chosen.append(jnp.where(e == ids[2], pk_r[base + 2], got))
        slot = iota((8, slots), 1)
        y = iota((oy, slots * oy), 0)
        x = iota((oy, slots * oy), 1)
        diagonal = (x & 15) == y
        total = jnp.zeros((ntr * oy, ox), F32)
        live = [jnp.where(slot < peer_count[0, 0, p], chosen[p], 0.0) for p in range(peers)]
        spread = nn(jnp.concatenate(live, axis=0).astype(BF16), c_e[...])
        for p in range(peers):
            left = jnp.concatenate(
                [
                    jnp.where(diagonal, spread[8 * p + c : 8 * p + c + 1, :], 0.0).astype(BF16)
                    for c in range(ntr)
                ],
                axis=0,
            )
            total = total + nn(left, toc[p].reshape(slots * oy, ox))
        for t in range(ntr):
            forc[t] = total[t * oy : (t + 1) * oy]

    def ret_copies():
        of = lambda k, di, dj: {1: 3, -1: 4}[di] if di != 0 else {1: 1, -1: 2}[dj]
        return near_copies(rt_s, rt_r, rt_ss, rt_rs, of)

    def give_back():
        pltpu.make_async_copy(to_atmos, toa, s_toa).wait()
        surface = out[0, 0].astype(BF16)
        y = iota((oy, slots * oy), 0)
        x = iota((oy, slots * oy), 1)
        diagonal = (x & 15) == y
        rows = []
        for p in range(peers):
            sums = nt(surface, toa[p].reshape(slots * oy, ox))
            rows.append(jnp.sum(jnp.where(diagonal, sums, 0.0), axis=0, keepdims=True))
        rows.append(jnp.zeros((8 - peers, slots * oy), F32))
        sums = jnp.concatenate(rows, axis=0)
        high = sums.astype(BF16)
        low = (sums - high.astype(F32)).astype(BF16)
        both = nn(jnp.concatenate([high, low], axis=0), c_et[...])
        both = both[0:8] + both[8:16]
        for p in range(peers):
            rt_s[p] = jnp.broadcast_to(both[p : p + 1], (8, slots))
        for copy in ret_copies():
            copy.start()

    def first_step(idx, carry):
        b = jnp.where(idx < 2, 1 - idx, idx)
        wait_rims(0, b, 4)
        place(0, b, ntr + 1)
        faces(b)

        @pl.when(b == 0)
        def _():
            force()

        advect(0, b)
        pltpu.make_async_copy(mix.at[0], mixv.at[b], s_mix.at[b]).wait()
        mixing(b, True)
        pack(1, b, ntr, ntr)
        send(1, b, 3)
        return carry

    lax.fori_loop(0, nb, first_step, 0)

    def second_step(b, carry):
        wait_rims(1, b, 3)
        place(1, b, ntr)
        advect(1, b)
        mixing(b, False)

        @pl.when(b == 0)
        def _():
            give_back()

        return carry

    lax.fori_loop(0, nb, second_step, 0)

    for copy in ret_copies():
        copy.wait()
    slot = iota((1, slots), 1)
    parts = []
    for k, (di, dj) in enumerate(NEAR):
        ti, tj = device(di, dj)
        value = rt_s[0] if (di, dj) == (0, 0) else rt_r[k]
        kept = slot < send_count[0, 0, ti * ntx + tj]
        parts.append(jnp.where(kept, value, 0.0))
    values = jnp.concatenate(parts, axis=1)
    high = values.astype(BF16)
    low = (values - high.astype(F32)).astype(BF16)
    landed = nt(high, oh[...]) + nt(low, oh[...])
    for r in range(surf_out.shape[0]):
        surf_out[r : r + 1, :] = landed[0:1, r * LANES : (r + 1) * LANES]


def export(tracers, surface, tracers_out, surface_out, sems):
    copies = [
        pltpu.make_async_copy(tracers.at[t], tracers_out.at[t], sems.at[t])
        for t in range(tracers.shape[0])
    ]
    copies.append(pltpu.make_async_copy(surface, surface_out, sems.at[len(copies)]))
    for copy in copies:
        copy.start()
    for copy in copies:
        copy.wait()


def body(
    nty,
    ntx,
    tracers,
    courant,
    depth_levels,
    mix_inverse,
    to_ocean,
    to_atmos,
    atm_flux,
    peer_list,
    peer_count,
    send_count,
    slot_cell,
):
    ntr, levels, oy, ox = tracers.shape
    nb, zb = mix_inverse.shape[:2]
    peers, slots = to_ocean.shape[:2]
    cells = atm_flux.shape[1] * atm_flux.shape[2]
    near = len(NEAR)
    hbm = pl.BlockSpec(memory_space=pltpu.HBM)
    vmem = pl.BlockSpec(memory_space=pltpu.VMEM)
    dma = pltpu.SemaphoreType.DMA
    scratch = [
        pltpu.VMEM((ntr + 1, nb, zb, ox // LANES, PAD, LANES), F32),
        pltpu.VMEM((nb, zb, ox // LANES, oy, LANES), F32),
        pltpu.VMEM(mix_inverse.shape, BF16),
        pltpu.VMEM(to_ocean.shape, BF16),
        pltpu.VMEM(to_atmos.shape, BF16),
        pltpu.VMEM((ntr + 1, nb, ROWS, ox), BF16),
        pltpu.VMEM((SUBSTEPS, nb, 4, 2 * RIM, ox), BF16),
        pltpu.VMEM((SUBSTEPS, nb, 4, 2 * RIM, ox), BF16),
        pltpu.VMEM((SUBSTEPS, nb, 16, ox), F32),
        pltpu.VMEM((SUBSTEPS, nb, 16, ox), F32),
        pltpu.VMEM((4, nb, zb, ox // LANES, oy, LANES), F32),
        pltpu.VMEM((ntr, ROWS, 2 * ox), F32),
        pltpu.VMEM((ntr + 1, ox // LANES, 2 * RIM, LANES), F32),
        pltpu.VMEM((ntr, zb, ox // LANES, oy, LANES), F32),
        pltpu.VMEM((ntr, oy, ox), F32),
        pltpu.VMEM((4, oy, ox), I32),
        pltpu.VMEM((2, 8, ox), I32),
        pltpu.VMEM((2, oy, LANES), I32),
        pltpu.VMEM((ox, 2 * ox), BF16),
        pltpu.VMEM((3, 16, 2 * ox), BF16),
        pltpu.VMEM((ox, 2 * ox), BF16),
        pltpu.VMEM((16, 2 * ox), BF16),
        pltpu.VMEM((4, 16, ox), BF16),
        pltpu.VMEM((slots, slots * oy), BF16),
        pltpu.VMEM((slots * oy, slots), BF16),
        pltpu.VMEM((cells, near * slots), BF16),
        pltpu.VMEM((8, cells), F32),
        pltpu.VMEM((near, 8, slots), F32),
        pltpu.VMEM((near, 8, slots), F32),
        pltpu.VMEM((peers, 8, slots), F32),
        pltpu.VMEM((near, 8, slots), F32),
        pltpu.VMEM((oy, ox), I32),
        pltpu.VMEM(atm_flux.shape, BF16),
        pltpu.VMEM(slot_cell.shape, I32),
        pltpu.SMEM(peer_list.shape, I32),
        pltpu.SMEM(peer_count.shape, I32),
        pltpu.SMEM(send_count.shape, I32),
        dma((6,)),
        dma((ox // LANES, nb)),
        dma((ox // LANES, nb)),
        dma((ox // LANES, nb)),
        dma((nb,)),
        dma,
        dma,
        dma((SUBSTEPS, 2, nb)),
        dma((SUBSTEPS, 2, nb)),
        dma((SUBSTEPS, 2, nb)),
        dma((SUBSTEPS, 2, nb)),
        dma((4,)),
        dma((4,)),
        dma((near,)),
        dma((near,)),
        dma((near,)),
        dma((near,)),
    ]
    results = pl.pallas_call(
        functools.partial(kernel, nty, ntx),
        out_shape=(
            pltpu.VMEM(tracers.shape, F32),
            pltpu.VMEM(atm_flux.shape[1:], F32),
        ),
        in_specs=[hbm] * 11,
        out_specs=(vmem, vmem),
        scratch_shapes=scratch,
        compiler_params=pltpu.CompilerParams(
            collective_id=0, has_side_effects=True, vmem_limit_bytes=62464 * 1024
        ),
        cost_estimate=pl.CostEstimate(flops=10**9, bytes_accessed=26 * 10**6, transcendentals=0),
        name="interval",
    )(
        tracers,
        courant,
        mix_inverse,
        to_ocean,
        to_atmos,
        depth_levels,
        atm_flux,
        slot_cell,
        peer_list,
        peer_count,
        send_count,
    )
    anywhere = pl.BlockSpec(memory_space=pl.ANY)
    return pl.pallas_call(
        export,
        out_shape=(
            jax.ShapeDtypeStruct(tracers.shape, F32),
            jax.ShapeDtypeStruct(atm_flux.shape[1:], F32),
        ),
        in_specs=[pl.BlockSpec(memory_space=pl.ANY)] * 2,
        out_specs=(anywhere, anywhere),
        scratch_shapes=[dma((ntr + 1,))],
        compiler_params=pltpu.CompilerParams(has_side_effects=True, vmem_limit_bytes=1024 * 1024),
        name="export",
    )(*results)


def solution(mesh):
    in_specs = (
        P(None, None, "ty", "tx"),
        P(None, None, "ty", "tx"),
        P("ty", "tx"),
        P(None, None, None, "ty", "tx"),
        P(None, None, "ty", "tx"),
        P(None, None, "ty", "tx"),
        P(None, "ty", "tx"),
        P("ty", "tx", None),
        P("ty", "tx", None),
        P("ty", "tx", None),
        P("ty", "tx", None, None),
    )
    out_specs = (P(None, None, "ty", "tx"), P("ty", "tx"))
    part = functools.partial(body, mesh.shape["ty"], mesh.shape["tx"])
    return jax.shard_map(part, mesh=mesh, in_specs=in_specs, out_specs=out_specs, check_vma=False)
```

```python
import functools

import jax
import jax.numpy as jnp
from jax import lax
from jax.experimental import pallas as pl
from jax.experimental.pallas import tpu as pltpu
from jax.sharding import PartitionSpec as P

MESH = pl.DeviceIdType.MESH
F32 = jnp.float32
BF16 = jnp.bfloat16
I32 = jnp.int32
SUBSTEPS = 2
LANES = 128
RIM = 32
ROWS = 256
RGROUP = 3
PAD = 32
TOP = 8
NEAR = tuple((di, dj) for di in (-1, 0, 1) for dj in (-1, 0, 1))


def iota(shape, dim):
    return lax.broadcasted_iota(I32, shape, dim)


def stencil(d):
    return jnp.where((d == 0) | (d == 1), 7.0, jnp.where((d == -1) | (d == 2), -1.0, 0.0))


def nn(a, b):
    return jnp.dot(a, b, preferred_element_type=F32)


def nt(a, b):
    return lax.dot_general(a, b, (((1,), (1,)), ((), ())), preferred_element_type=F32)


def tn(a, b):
    return lax.dot_general(a, b, (((0,), (0,)), ((), ())), preferred_element_type=F32)


def kernel(
    nty,
    ntx,
    tracers,
    courant,
    mix,
    to_ocean,
    to_atmos,
    depth_in,
    atm_in,
    slot_cell_in,
    peer_list_in,
    peer_count_in,
    send_count_in,
    out,
    surf_out,
    qs,
    cx,
    mixv,
    toc,
    toa,
    fld,
    sr,
    hr,
    sc,
    hc,
    coef,
    ux,
    tmp,
    mv,
    forc,
    depx,
    dr,
    dc,
    c_x,
    c_xh,
    c_xs,
    c_xsh,
    c_selc,
    c_e,
    c_et,
    oh,
    flat,
    pk_s,
    pk_r,
    rt_s,
    rt_r,
    depth,
    atm,
    slot_cell,
    peer_list,
    peer_count,
    send_count,
    s_in,
    s_tr,
    s_cx,
    s_cy,
    s_mix,
    s_toc,
    s_toa,
    row_ss,
    row_rs,
    col_ss,
    col_rs,
    dep_ss,
    dep_rs,
    pk_ss,
    pk_rs,
    rt_ss,
    rt_rs,
):
    nb, zb = mix.shape[:2]
    ntr, _, oy, ox = tracers.shape
    halves = ox // LANES
    own = slice(TOP, TOP + oy)
    peers, slots = to_ocean.shape[0], to_ocean.shape[1]
    i = lax.axis_index("ty")
    j = lax.axis_index("tx")

    def device(di, dj):
        return (lax.rem(i + di + nty, nty), lax.rem(j + dj + ntx, ntx))

    barrier = pltpu.get_barrier_semaphore()
    for di, dj in NEAR:
        if (di, dj) != (0, 0):
            pl.semaphore_signal(barrier, inc=1, device_id=device(di, dj), device_id_type=MESH)

    small = [
        pltpu.make_async_copy(source, target, s_in.at[k])
        for k, (source, target) in enumerate(
            (
                (depth_in, depth),
                (slot_cell_in, slot_cell),
                (atm_in, atm),
                (peer_list_in, peer_list),
                (peer_count_in, peer_count),
                (send_count_in, send_count),
            )
        )
    ]
    small[0].start()
    order = (1, 2, 0) + tuple(range(3, nb))

    def nth(idx):
        return jnp.where(idx < 2, idx + 1, jnp.where(idx == 2, 0, idx))

    def loads(b, first):
        made = []
        for h in range(halves):
            lanes = pl.ds(h * LANES, LANES)
            levels = pl.ds(first, zb)
            made += [
                pltpu.make_async_copy(
                    tracers.at[:, levels, :, lanes],
                    qs.at[pl.ds(0, ntr), b, :, h, pl.ds(TOP, oy)],
                    s_tr.at[h, b],
                ),
                pltpu.make_async_copy(
                    courant.at[0, levels, :, lanes], cx.at[b, :, h], s_cx.at[h, b]
                ),
                pltpu.make_async_copy(
                    courant.at[1, levels, :, lanes],
                    qs.at[ntr, b, :, h, pl.ds(TOP, oy)],
                    s_cy.at[h, b],
                ),
            ]
        return made

    for b in order:
        for copy in loads(b, b * zb):
            copy.start()
    for copy in small[1:]:
        copy.start()
    for b in order[:2]:
        pltpu.make_async_copy(mix.at[b], mixv.at[b], s_mix.at[b]).start()
    pltpu.make_async_copy(to_ocean, toc, s_toc).start()
    for b in order[2:]:
        pltpu.make_async_copy(mix.at[b], mixv.at[b], s_mix.at[b]).start()
    pltpu.make_async_copy(to_atmos, toa, s_toa).start()

    r = iota((16, ox), 0)
    n = iota((16, ox), 1)
    for f in range(4):
        at = jnp.where(r < 8, ox - 2 + r - 2 * f, r - 8 - 2 * f)
        mine = ((r & 7) >> 1) == f
        hit = mine & (at == n)
        c_selc[f] = jnp.where(hit, 1.0, 0.0).astype(BF16)
    sends = (i < nty - 1, i > 0, j < ntx - 1, j > 0)
    takes = (i > 0, i < nty - 1, j > 0, j < ntx - 1)

    def start_all(copies):
        for copy, mine in zip(copies, sends):
            pl.when(mine)(copy.start)

    def wait_all(copies):
        for copy, mine, theirs in zip(copies, sends, takes):
            pl.when(mine)(copy.wait_send)
            pl.when(theirs)(copy.wait_recv)

    def depth_copies():
        return (
            pltpu.make_async_remote_copy(
                depth.at[pl.ds(oy - 8, 8)], dr.at[0], dep_ss.at[0], dep_rs.at[0],
                device_id=device(1, 0), device_id_type=MESH,
            ),
            pltpu.make_async_remote_copy(
                depth.at[pl.ds(0, 8)], dr.at[1], dep_ss.at[1], dep_rs.at[1],
                device_id=device(-1, 0), device_id_type=MESH,
            ),
            pltpu.make_async_remote_copy(
                depth.at[:, pl.ds(ox - LANES, LANES)], dc.at[0], dep_ss.at[2], dep_rs.at[2],
                device_id=device(0, 1), device_id_type=MESH,
            ),
            pltpu.make_async_remote_copy(
                depth.at[:, pl.ds(0, LANES)], dc.at[1], dep_ss.at[3], dep_rs.at[3],
                device_id=device(0, -1), device_id_type=MESH,
            ),
        )

    def near_copies(source, target, ss, rs, of):
        made = []
        for k, (di, dj) in enumerate(NEAR):
            if (di, dj) != (0, 0):
                made.append(
                    pltpu.make_async_remote_copy(
                        source.at[of(k, di, dj)], target.at[len(NEAR) - 1 - k], ss.at[k],
                        rs.at[len(NEAR) - 1 - k], device_id=device(di, dj), device_id_type=MESH,
                    )
                )
        return made

    def rim_copies(step, b, fields):
        rows = [
            pltpu.make_async_remote_copy(
                sr.at[step, b, pl.ds(0, fields), pl.ds(s * RIM, RIM)],
                hr.at[step, b, pl.ds(0, fields), pl.ds(s * RIM, RIM)],
                row_ss.at[step, s, b], row_rs.at[step, s, b],
                device_id=device(1 - 2 * s, 0), device_id_type=MESH,
            )
            for s in range(2)
        ]
        cols = [
            pltpu.make_async_remote_copy(
                sc.at[step, b, pl.ds(s * 8, 8)],
                hc.at[step, b, pl.ds(s * 8, 8)],
                col_ss.at[step, s, b], col_rs.at[step, s, b],
                device_id=device(0, 1 - 2 * s), device_id_type=MESH,
            )
            for s in range(2)
        ]
        return rows + cols

    small[0].wait()
    dep = depth[...]

    def pack(step, b, row_fields, col_fields):
        for f in range(row_fields):
            for h in range(halves):
                for k in range(zb):
                    tmp[f, h, 2 * k : 2 * k + 2, :] = qs[f, b, k, h, TOP + oy - 2 : TOP + oy, :]
                    tmp[f, h, RIM + 2 * k : RIM + 2 * k + 2, :] = qs[f, b, k, h, TOP : TOP + 2, :]
                sr[step, b, f, :, h * LANES : (h + 1) * LANES] = tmp[f, h].astype(BF16)
        cols = nt(c_selc[0], fld[0, b])
        for f in range(1, col_fields):
            cols = cols + nt(c_selc[f], fld[f, b])
        sc[step, b] = cols

    def send(step, b, fields):
        start_all(rim_copies(step, b, fields))

    def fill(b):
        for copy in loads(b, 0):
            copy.wait()
        for h in range(halves):
            lanes = slice(h * LANES, (h + 1) * LANES)
            for f in range(ntr + 1):
                value = cx[b, :, h] if f == ntr else qs[f, b, :, h, own, :]
                fld[f, b, 0 : zb * oy, lanes] = value.reshape(zb * oy, LANES).astype(BF16)
        for f in range(ntr + 1):
            fld[f, b, zb * oy :, :] = jnp.zeros((ROWS - zb * oy, ox), BF16)
        pack(0, b, ntr + 1, ntr + 1)

    tmp[...] = jnp.zeros_like(tmp)
    fill(order[0])

    for s in range(2):
        @pl.when(jnp.logical_not(takes[s]))
        def _():
            hr[:, :, :, s * RIM : (s + 1) * RIM, :] = jnp.zeros((SUBSTEPS, nb, 4, RIM, ox), BF16)
            dr[s] = jnp.zeros((8, ox), I32)

        @pl.when(jnp.logical_not(takes[2 + s]))
        def _():
            hc[:, :, s * 8 : (s + 1) * 8, :] = jnp.zeros((SUBSTEPS, nb, 8, ox), F32)
            dc[s] = jnp.zeros((oy, LANES), I32)

    pl.semaphore_wait(barrier, len(NEAR) - 1)
    start_all(depth_copies())
    send(0, order[0], 4)

    def fill_and_send(idx, carry):
        b = nth(idx)
        fill(b)
        send(0, b, 4)
        return carry

    lax.fori_loop(1, nb, fill_and_send, 0)

    for copy in small[1:]:
        copy.wait()

    cells = iota((oh.shape[0], slots), 0)
    for k, (di, dj) in enumerate(NEAR):
        ti, tj = device(di, dj)
        row = slot_cell[0, 0, pl.ds(ti * ntx + tj, 1), :]
        oh[:, k * slots : (k + 1) * slots] = jnp.where(cells == row, 1.0, 0.0).astype(BF16)
    flux = atm[...].astype(F32)
    flat[...] = jnp.zeros_like(flat)
    for c in range(flux.shape[0]):
        for r in range(flux.shape[1]):
            flat[c : c + 1, r * LANES : (r + 1) * LANES] = flux[c, r : r + 1, :]
    picks = nn(flat[...].astype(BF16), oh[...])
    for k in range(len(NEAR)):
        pk_s[k] = picks[:, k * slots : (k + 1) * slots]

    for copy in near_copies(pk_s, pk_r, pk_ss, pk_rs, lambda k, di, dj: k):
        copy.start()

    g = iota((ox, 2 * ox), 0)
    n = iota((ox, 2 * ox), 1)
    d = g - jnp.where(n < ox, n, n - ox - 1)
    c_x[...] = stencil(d).astype(BF16)
    c_xs[...] = jnp.where(d == jnp.where(n < ox, 1, 0), 1.0, 0.0).astype(BF16)
    r = iota((16, 2 * ox), 0)
    n = iota((16, 2 * ox), 1)
    x = jnp.where(n < ox, n, n - ox - 1)
    for f in range(4):
        at = jnp.where(r < 8, -2 + r - 2 * f, ox + r - 8 - 2 * f)
        mine = ((r & 7) >> 1) == f
        if f < 3:
            c_xh[f] = jnp.where(mine, stencil(at - x), 0.0).astype(BF16)
        else:
            hit = mine & (at - x == jnp.where(n < ox, 1, 0))
            c_xsh[...] = jnp.where(hit, 1.0, 0.0).astype(BF16)
    r = iota((slots, slots * oy), 0)
    n = iota((slots, slots * oy), 1)
    c_e[...] = jnp.where((n >> 4) == r, 1.0, 0.0).astype(BF16)
    r = iota((slots * oy, slots), 0)
    n = iota((slots * oy, slots), 1)
    c_et[...] = jnp.where((r >> 4) == n, 1.0, 0.0).astype(BF16)

    wait_all(depth_copies())
    south, north, west, east = dr[0], dr[1], dc[0], dc[1]
    wide = jnp.concatenate([dep, east], axis=1)
    depx[0] = pltpu.roll(wide, ox + LANES - 1, 1)[:, :ox]
    wide = jnp.concatenate([west, dep], axis=1)
    depx[1] = pltpu.roll(wide, 1, 1)[:, LANES:]
    tall = jnp.concatenate([dep, north], axis=0)
    depx[2] = pltpu.roll(tall, oy + 7, 0)[:oy]
    tall = jnp.concatenate([south, dep], axis=0)
    depx[3] = pltpu.roll(tall, 1, 0)[8:]

    def wait_rims(step, b, fields):
        wait_all(rim_copies(step, b, fields))

    def place(step, b, fields):
        for f in range(fields):
            for h in range(halves):
                tmp[f, h] = hr[step, b, f, :, h * LANES : (h + 1) * LANES].astype(F32)
        for f in range(fields):
            for h in range(halves):
                for k in range(zb):
                    qs[f, b, k, h, TOP - 2 : TOP, :] = tmp[f, h, 2 * k : 2 * k + 2, :]
                    qs[f, b, k, h, TOP + oy : TOP + oy + 2, :] = tmp[
                        f, h, RIM + 2 * k : RIM + 2 * k + 2, :
                    ]

    def faces(b):
        ux[0] = nn(fld[ntr, b], c_xs[...]) + tn(hc[0, b].astype(BF16), c_xsh[...])
        for k in range(zb):
            at = b * zb + k
            rows = slice(k * oy, (k + 1) * oy)
            for h in range(halves):
                lanes = slice(h * LANES, (h + 1) * LANES)
                wet = at < depth[:, lanes]
                near_wet = [wet & (at < depx[a, :, lanes]) for a in range(4)]
                x0 = cx[b, k, h]
                y0 = qs[ntr, b, k, h, own, :]
                others = (
                    ux[0, rows, lanes],
                    ux[0, rows, ox + h * LANES : ox + (h + 1) * LANES],
                    qs[ntr, b, k, h, TOP + 1 : TOP + 1 + oy, :],
                    qs[ntr, b, k, h, TOP - 1 : TOP - 1 + oy, :],
                )
                for a in range(4):
                    mean = ((x0, y0)[a // 2] + others[a]) * (1.0 / 24.0)
                    coef[a, b, k, h] = jnp.where(near_wet[a], mean, 0.0)

    def advect(step, b):
        halo = hc[step, b].astype(BF16)
        for t in range(ntr):
            ux[t] = nn(fld[t, b], c_x[...]) + tn(halo, c_xh[t])
        for k in range(zb):
            rows = slice(k * oy, (k + 1) * oy)
            for h in range(halves):
                lanes = slice(h * LANES, (h + 1) * LANES)
                c0, c1, c2, c3 = (coef[a, b, k, h] for a in range(4))
                for t in range(ntr):
                    m2, m1, q0, p1, p2 = (
                        qs[t, b, k, h, TOP + o : TOP + o + oy, :] for o in (-2, -1, 0, 1, 2)
                    )
                    east = c0 * ux[t, rows, lanes]
                    west = c1 * ux[t, rows, ox + h * LANES : ox + (h + 1) * LANES]
                    north = c2 * (7.0 * (q0 + p1) - (m1 + p2))
                    south = c3 * (7.0 * (m1 + q0) - (m2 + p1))
                    if step == 0:
                        q0 = jnp.where((b * zb + k) < depth[:, lanes], q0, 0.0)
                    mv[t, k, h] = q0 - (east - west) - (north - south)

        @pl.when(b == 0)
        def _():
            for t in range(ntr):
                for h in range(halves):
                    lanes = slice(h * LANES, (h + 1) * LANES)
                    mv[t, 0, h] = mv[t, 0, h] + jnp.where(depth[:, lanes] > 0, forc[t, :, lanes], 0.0)

    def mixing(b, keep):
        for h in range(halves):
            lanes = slice(h * LANES, (h + 1) * LANES)
            for first in range(0, zb, RGROUP):
                acc = [[None] * ntr for _ in range(RGROUP)]
                for c in range(zb):
                    moved = [mv[t, c, h] for t in range(ntr)]
                    for r in range(RGROUP):
                        weight = mixv[b, first + r, c, :, lanes].astype(F32)
                        for t in range(ntr):
                            term = weight * moved[t]
                            acc[r][t] = term if c == 0 else acc[r][t] + term
                for r in range(RGROUP):
                    k = first + r
                    wet = (b * zb + k) < depth[:, lanes]
                    for t in range(ntr):
                        value = jnp.where(wet, acc[r][t], 0.0)
                        if keep:
                            qs[t, b, k, h, own, :] = value
                            fld[t, b, k * oy : (k + 1) * oy, lanes] = value.astype(BF16)
                        else:
                            out[t, b * zb + k, :, lanes] = value

    def force():
        for copy in near_copies(pk_s, pk_r, pk_ss, pk_rs, lambda k, di, dj: k):
            copy.wait()
        pltpu.make_async_copy(to_ocean, toc, s_toc).wait()
        mine = pk_s[4]
        chosen = [mine, pk_r[5], pk_r[3]]
        for p, di in ((3, 1), (4, -1)):
            ids = [device(di, dj) for dj in (-1, 0, 1)]
            ids = [a * ntx + b for a, b in ids]
            base = (di + 1) * 3
            e = peer_list[0, 0, p]
            got = jnp.where(e == ids[0], pk_r[base], pk_r[base + 1])
            chosen.append(jnp.where(e == ids[2], pk_r[base + 2], got))
        slot = iota((8, slots), 1)
        y = iota((oy, slots * oy), 0)
        x = iota((oy, slots * oy), 1)
        diagonal = (x & 15) == y
        total = jnp.zeros((ntr * oy, ox), F32)
        live = [jnp.where(slot < peer_count[0, 0, p], chosen[p], 0.0) for p in range(peers)]
        spread = nn(jnp.concatenate(live, axis=0).astype(BF16), c_e[...])
        for p in range(peers):
            left = jnp.concatenate(
                [
                    jnp.where(diagonal, spread[8 * p + c : 8 * p + c + 1, :], 0.0).astype(BF16)
                    for c in range(ntr)
                ],
                axis=0,
            )
            total = total + nn(left, toc[p].reshape(slots * oy, ox))
        for t in range(ntr):
            forc[t] = total[t * oy : (t + 1) * oy]

    def ret_copies():
        of = lambda k, di, dj: {1: 3, -1: 4}[di] if di != 0 else {1: 1, -1: 2}[dj]
        return near_copies(rt_s, rt_r, rt_ss, rt_rs, of)

    def give_back():
        pltpu.make_async_copy(to_atmos, toa, s_toa).wait()
        surface = out[0, 0].astype(BF16)
        y = iota((oy, slots * oy), 0)
        x = iota((oy, slots * oy), 1)
        diagonal = (x & 15) == y
        rows = []
        for p in range(peers):
            sums = jnp.where(diagonal, nt(surface, toa[p].reshape(slots * oy, ox)), 0.0)
            high = sums.astype(BF16)
            rows += [high, (sums - high.astype(F32)).astype(BF16)]
        both = nn(jnp.concatenate(rows, axis=0), c_et[...])
        both = jnp.sum(both.reshape(peers, 2 * oy, slots), axis=1)
        for p in range(peers):
            rt_s[p] = jnp.broadcast_to(both[p : p + 1], (8, slots))
        for copy in ret_copies():
            copy.start()

    def first_step(idx, carry):
        b = nth(idx)
        wait_rims(0, b, 4)
        place(0, b, ntr + 1)
        faces(b)

        @pl.when(b == 0)
        def _():
            force()

        advect(0, b)
        pltpu.make_async_copy(mix.at[0], mixv.at[b], s_mix.at[b]).wait()
        mixing(b, True)
        pack(1, b, ntr, ntr)
        send(1, b, 3)
        return carry

    lax.fori_loop(0, nb, first_step, 0)

    def second_step(idx, carry):
        b = jnp.where(idx < 2, 1 - idx, idx)
        wait_rims(1, b, 3)
        place(1, b, ntr)
        advect(1, b)
        mixing(b, False)

        @pl.when(b == 0)
        def _():
            give_back()

        return carry

    lax.fori_loop(0, nb, second_step, 0)

    for copy in ret_copies():
        copy.wait()
    slot = iota((1, slots), 1)
    parts = []
    for k, (di, dj) in enumerate(NEAR):
        ti, tj = device(di, dj)
        value = rt_s[0] if (di, dj) == (0, 0) else rt_r[k]
        kept = slot < send_count[0, 0, ti * ntx + tj]
        parts.append(jnp.where(kept, value, 0.0))
    values = jnp.concatenate(parts, axis=1)
    high = values.astype(BF16)
    low = (values - high.astype(F32)).astype(BF16)
    landed = nt(jnp.concatenate([high, low], axis=0), oh[...])
    landed = landed[0:8] + landed[8:16]
    for r in range(surf_out.shape[0]):
        surf_out[r : r + 1, :] = landed[0:1, r * LANES : (r + 1) * LANES]


def export(tracers, surface, tracers_out, surface_out, sems):
    copies = [
        pltpu.make_async_copy(tracers.at[t], tracers_out.at[t], sems.at[t])
        for t in range(tracers.shape[0])
    ]
    copies.append(pltpu.make_async_copy(surface, surface_out, sems.at[len(copies)]))
    for copy in copies:
        copy.start()
    for copy in copies:
        copy.wait()


def body(
    nty,
    ntx,
    tracers,
    courant,
    depth_levels,
    mix_inverse,
    to_ocean,
    to_atmos,
    atm_flux,
    peer_list,
    peer_count,
    send_count,
    slot_cell,
):
    ntr, levels, oy, ox = tracers.shape
    nb, zb = mix_inverse.shape[:2]
    peers, slots = to_ocean.shape[:2]
    cells = atm_flux.shape[1] * atm_flux.shape[2]
    near = len(NEAR)
    hbm = pl.BlockSpec(memory_space=pltpu.HBM)
    vmem = pl.BlockSpec(memory_space=pltpu.VMEM)
    dma = pltpu.SemaphoreType.DMA
    scratch = [
        pltpu.VMEM((ntr + 1, nb, zb, ox // LANES, PAD, LANES), F32),
        pltpu.VMEM((nb, zb, ox // LANES, oy, LANES), F32),
        pltpu.VMEM(mix_inverse.shape, BF16),
        pltpu.VMEM(to_ocean.shape, BF16),
        pltpu.VMEM(to_atmos.shape, BF16),
        pltpu.VMEM((ntr + 1, nb, ROWS, ox), BF16),
        pltpu.VMEM((SUBSTEPS, nb, 4, 2 * RIM, ox), BF16),
        pltpu.VMEM((SUBSTEPS, nb, 4, 2 * RIM, ox), BF16),
        pltpu.VMEM((SUBSTEPS, nb, 16, ox), F32),
        pltpu.VMEM((SUBSTEPS, nb, 16, ox), F32),
        pltpu.VMEM((4, nb, zb, ox // LANES, oy, LANES), F32),
        pltpu.VMEM((ntr, ROWS, 2 * ox), F32),
        pltpu.VMEM((ntr + 1, ox // LANES, 2 * RIM, LANES), F32),
        pltpu.VMEM((ntr, zb, ox // LANES, oy, LANES), F32),
        pltpu.VMEM((ntr, oy, ox), F32),
        pltpu.VMEM((4, oy, ox), I32),
        pltpu.VMEM((2, 8, ox), I32),
        pltpu.VMEM((2, oy, LANES), I32),
        pltpu.VMEM((ox, 2 * ox), BF16),
        pltpu.VMEM((3, 16, 2 * ox), BF16),
        pltpu.VMEM((ox, 2 * ox), BF16),
        pltpu.VMEM((16, 2 * ox), BF16),
        pltpu.VMEM((4, 16, ox), BF16),
        pltpu.VMEM((slots, slots * oy), BF16),
        pltpu.VMEM((slots * oy, slots), BF16),
        pltpu.VMEM((cells, near * slots), BF16),
        pltpu.VMEM((8, cells), F32),
        pltpu.VMEM((near, 8, slots), F32),
        pltpu.VMEM((near, 8, slots), F32),
        pltpu.VMEM((peers, 8, slots), F32),
        pltpu.VMEM((near, 8, slots), F32),
        pltpu.VMEM((oy, ox), I32),
        pltpu.VMEM(atm_flux.shape, BF16),
        pltpu.VMEM(slot_cell.shape, I32),
        pltpu.SMEM(peer_list.shape, I32),
        pltpu.SMEM(peer_count.shape, I32),
        pltpu.SMEM(send_count.shape, I32),
        dma((6,)),
        dma((ox // LANES, nb)),
        dma((ox // LANES, nb)),
        dma((ox // LANES, nb)),
        dma((nb,)),
        dma,
        dma,
        dma((SUBSTEPS, 2, nb)),
        dma((SUBSTEPS, 2, nb)),
        dma((SUBSTEPS, 2, nb)),
        dma((SUBSTEPS, 2, nb)),
        dma((4,)),
        dma((4,)),
        dma((near,)),
        dma((near,)),
        dma((near,)),
        dma((near,)),
    ]
    results = pl.pallas_call(
        functools.partial(kernel, nty, ntx),
        out_shape=(
            pltpu.VMEM(tracers.shape, F32),
            pltpu.VMEM(atm_flux.shape[1:], F32),
        ),
        in_specs=[hbm] * 11,
        out_specs=(vmem, vmem),
        scratch_shapes=scratch,
        compiler_params=pltpu.CompilerParams(
            collective_id=0, has_side_effects=True, vmem_limit_bytes=62464 * 1024
        ),
        cost_estimate=pl.CostEstimate(flops=10**9, bytes_accessed=26 * 10**6, transcendentals=0),
        name="interval",
    )(
        tracers,
        courant,
        mix_inverse,
        to_ocean,
        to_atmos,
        depth_levels,
        atm_flux,
        slot_cell,
        peer_list,
        peer_count,
        send_count,
    )
    anywhere = pl.BlockSpec(memory_space=pl.ANY)
    return pl.pallas_call(
        export,
        out_shape=(
            jax.ShapeDtypeStruct(tracers.shape, F32),
            jax.ShapeDtypeStruct(atm_flux.shape[1:], F32),
        ),
        in_specs=[pl.BlockSpec(memory_space=pl.ANY)] * 2,
        out_specs=(anywhere, anywhere),
        scratch_shapes=[dma((ntr + 1,))],
        compiler_params=pltpu.CompilerParams(has_side_effects=True, vmem_limit_bytes=1024 * 1024),
        name="export",
    )(*results)


def solution(mesh):
    in_specs = (
        P(None, None, "ty", "tx"),
        P(None, None, "ty", "tx"),
        P("ty", "tx"),
        P(None, None, None, "ty", "tx"),
        P(None, None, "ty", "tx"),
        P(None, None, "ty", "tx"),
        P(None, "ty", "tx"),
        P("ty", "tx", None),
        P("ty", "tx", None),
        P("ty", "tx", None),
        P("ty", "tx", None, None),
    )
    out_specs = (P(None, None, "ty", "tx"), P("ty", "tx"))
    part = functools.partial(body, mesh.shape["ty"], mesh.shape["tx"])
    return jax.shard_map(part, mesh=mesh, in_specs=in_specs, out_specs=out_specs, check_vma=False)
```

```python
import functools

import jax
import jax.numpy as jnp
from jax import lax
from jax.experimental import pallas as pl
from jax.experimental.pallas import tpu as pltpu
from jax.sharding import PartitionSpec as P

MESH = pl.DeviceIdType.MESH
F32 = jnp.float32
BF16 = jnp.bfloat16
I32 = jnp.int32
SUBSTEPS = 2
LANES = 128
RIM = 32
ROWS = 256
RGROUP = 3
PAD = 32
TOP = 8
NEAR = tuple((di, dj) for di in (-1, 0, 1) for dj in (-1, 0, 1))


def iota(shape, dim):
    return lax.broadcasted_iota(I32, shape, dim)


def stencil(d):
    return jnp.where((d == 0) | (d == 1), 7.0, jnp.where((d == -1) | (d == 2), -1.0, 0.0))


def nn(a, b):
    return jnp.dot(a, b, preferred_element_type=F32)


def nt(a, b):
    return lax.dot_general(a, b, (((1,), (1,)), ((), ())), preferred_element_type=F32)


def tn(a, b):
    return lax.dot_general(a, b, (((0,), (0,)), ((), ())), preferred_element_type=F32)


def kernel(
    nty,
    ntx,
    tracers,
    courant,
    mix,
    to_ocean,
    to_atmos,
    depth_in,
    atm_in,
    slot_cell_in,
    peer_list_in,
    peer_count_in,
    send_count_in,
    out,
    surf_out,
    qs,
    cx,
    mixv,
    toc,
    toa,
    fld,
    sr,
    hr,
    sc,
    hc,
    coef,
    ux,
    tmp,
    mv,
    forc,
    depx,
    dr,
    dc,
    c_x,
    c_xh,
    c_xs,
    c_xsh,
    c_selc,
    c_e,
    c_et,
    oh,
    flat,
    pk_s,
    pk_r,
    rt_s,
    rt_r,
    depth,
    atm,
    slot_cell,
    peer_list,
    peer_count,
    send_count,
    s_in,
    s_tr,
    s_cx,
    s_cy,
    s_mix,
    s_toc,
    s_toa,
    row_ss,
    row_rs,
    col_ss,
    col_rs,
    dep_ss,
    dep_rs,
    pk_ss,
    pk_rs,
    rt_ss,
    rt_rs,
):
    nb, zb = mix.shape[:2]
    ntr, _, oy, ox = tracers.shape
    halves = ox // LANES
    own = slice(TOP, TOP + oy)
    peers, slots = to_ocean.shape[0], to_ocean.shape[1]
    i = lax.axis_index("ty")
    j = lax.axis_index("tx")

    def device(di, dj):
        return (lax.rem(i + di + nty, nty), lax.rem(j + dj + ntx, ntx))

    barrier = pltpu.get_barrier_semaphore()
    for di, dj in NEAR:
        if (di, dj) != (0, 0):
            pl.semaphore_signal(barrier, inc=1, device_id=device(di, dj), device_id_type=MESH)

    small = [
        pltpu.make_async_copy(source, target, s_in.at[k])
        for k, (source, target) in enumerate(
            (
                (depth_in, depth),
                (slot_cell_in, slot_cell),
                (atm_in, atm),
                (peer_list_in, peer_list),
                (peer_count_in, peer_count),
                (send_count_in, send_count),
            )
        )
    ]
    order = (1, 0) + tuple(range(2, nb))

    def nth(idx):
        return jnp.where(idx < 2, 1 - idx, idx)

    def loads(b, first):
        made = []
        for h in range(halves):
            lanes = pl.ds(h * LANES, LANES)
            levels = pl.ds(first, zb)
            made += [
                pltpu.make_async_copy(
                    tracers.at[:, levels, :, lanes],
                    qs.at[pl.ds(0, ntr), b, :, h, pl.ds(TOP, oy)],
                    s_tr.at[h, b],
                ),
                pltpu.make_async_copy(
                    courant.at[0, levels, :, lanes], cx.at[b, :, h], s_cx.at[h, b]
                ),
                pltpu.make_async_copy(
                    courant.at[1, levels, :, lanes],
                    qs.at[ntr, b, :, h, pl.ds(TOP, oy)],
                    s_cy.at[h, b],
                ),
            ]
        return made

    for copy in small:
        copy.start()
    for b in order:
        for copy in loads(b, b * zb):
            copy.start()
    pltpu.make_async_copy(mix.at[order[0]], mixv.at[order[0]], s_mix.at[order[0]]).start()
    pltpu.make_async_copy(to_ocean, toc, s_toc).start()
    for b in order[1:]:
        pltpu.make_async_copy(mix.at[b], mixv.at[b], s_mix.at[b]).start()
    pltpu.make_async_copy(to_atmos, toa, s_toa).start()

    r = iota((16, ox), 0)
    n = iota((16, ox), 1)
    for f in range(4):
        at = jnp.where(r < 8, ox - 2 + r - 2 * f, r - 8 - 2 * f)
        mine = ((r & 7) >> 1) == f
        hit = mine & (at == n)
        c_selc[f] = jnp.where(hit, 1.0, 0.0).astype(BF16)
    sends = (i < nty - 1, i > 0, j < ntx - 1, j > 0)
    takes = (i > 0, i < nty - 1, j > 0, j < ntx - 1)

    def start_all(copies):
        for copy, mine in zip(copies, sends):
            pl.when(mine)(copy.start)

    def wait_all(copies):
        for copy, mine, theirs in zip(copies, sends, takes):
            pl.when(mine)(copy.wait_send)
            pl.when(theirs)(copy.wait_recv)

    def depth_copies():
        return (
            pltpu.make_async_remote_copy(
                depth.at[pl.ds(oy - 8, 8)], dr.at[0], dep_ss.at[0], dep_rs.at[0],
                device_id=device(1, 0), device_id_type=MESH,
            ),
            pltpu.make_async_remote_copy(
                depth.at[pl.ds(0, 8)], dr.at[1], dep_ss.at[1], dep_rs.at[1],
                device_id=device(-1, 0), device_id_type=MESH,
            ),
            pltpu.make_async_remote_copy(
                depth.at[:, pl.ds(ox - LANES, LANES)], dc.at[0], dep_ss.at[2], dep_rs.at[2],
                device_id=device(0, 1), device_id_type=MESH,
            ),
            pltpu.make_async_remote_copy(
                depth.at[:, pl.ds(0, LANES)], dc.at[1], dep_ss.at[3], dep_rs.at[3],
                device_id=device(0, -1), device_id_type=MESH,
            ),
        )

    def near_copies(source, target, ss, rs, of):
        made = []
        for k, (di, dj) in enumerate(NEAR):
            if (di, dj) != (0, 0):
                made.append(
                    pltpu.make_async_remote_copy(
                        source.at[of(k, di, dj)], target.at[len(NEAR) - 1 - k], ss.at[k],
                        rs.at[len(NEAR) - 1 - k], device_id=device(di, dj), device_id_type=MESH,
                    )
                )
        return made

    def rim_copies(step, b, fields):
        rows = [
            pltpu.make_async_remote_copy(
                sr.at[step, b, pl.ds(0, fields), pl.ds(s * RIM, RIM)],
                hr.at[step, b, pl.ds(0, fields), pl.ds(s * RIM, RIM)],
                row_ss.at[step, s, b], row_rs.at[step, s, b],
                device_id=device(1 - 2 * s, 0), device_id_type=MESH,
            )
            for s in range(2)
        ]
        cols = [
            pltpu.make_async_remote_copy(
                sc.at[step, b, pl.ds(s * 8, 8)],
                hc.at[step, b, pl.ds(s * 8, 8)],
                col_ss.at[step, s, b], col_rs.at[step, s, b],
                device_id=device(0, 1 - 2 * s), device_id_type=MESH,
            )
            for s in range(2)
        ]
        return rows + cols

    small[0].wait()
    dep = depth[...]

    def pack(step, b, row_fields, col_fields):
        for f in range(row_fields):
            for h in range(halves):
                for k in range(zb):
                    tmp[f, h, 2 * k : 2 * k + 2, :] = qs[f, b, k, h, TOP + oy - 2 : TOP + oy, :]
                    tmp[f, h, RIM + 2 * k : RIM + 2 * k + 2, :] = qs[f, b, k, h, TOP : TOP + 2, :]
                sr[step, b, f, :, h * LANES : (h + 1) * LANES] = tmp[f, h].astype(BF16)
        cols = nt(c_selc[0], fld[0, b])
        for f in range(1, col_fields):
            cols = cols + nt(c_selc[f], fld[f, b])
        sc[step, b] = cols

    def send(step, b, fields):
        start_all(rim_copies(step, b, fields))

    def fill(b):
        for copy in loads(b, 0):
            copy.wait()
        for h in range(halves):
            lanes = slice(h * LANES, (h + 1) * LANES)
            for f in range(ntr + 1):
                value = cx[b, :, h] if f == ntr else qs[f, b, :, h, own, :]
                fld[f, b, 0 : zb * oy, lanes] = value.reshape(zb * oy, LANES).astype(BF16)
        for f in range(ntr + 1):
            fld[f, b, zb * oy :, :] = jnp.zeros((ROWS - zb * oy, ox), BF16)
        pack(0, b, ntr + 1, ntr + 1)

    tmp[...] = jnp.zeros_like(tmp)
    for copy in small[1:]:
        copy.wait()

    cells = iota((oh.shape[0], slots), 0)
    for k, (di, dj) in enumerate(NEAR):
        ti, tj = device(di, dj)
        row = slot_cell[0, 0, pl.ds(ti * ntx + tj, 1), :]
        oh[:, k * slots : (k + 1) * slots] = jnp.where(cells == row, 1.0, 0.0).astype(BF16)
    flux = atm[...].astype(F32)
    flat[...] = jnp.zeros_like(flat)
    for c in range(flux.shape[0]):
        for r in range(flux.shape[1]):
            flat[c : c + 1, r * LANES : (r + 1) * LANES] = flux[c, r : r + 1, :]
    picks = nn(flat[...].astype(BF16), oh[...])
    for k in range(len(NEAR)):
        pk_s[k] = picks[:, k * slots : (k + 1) * slots]
    fill(order[0])

    for s in range(2):
        @pl.when(jnp.logical_not(takes[s]))
        def _():
            hr[:, :, :, s * RIM : (s + 1) * RIM, :] = jnp.zeros((SUBSTEPS, nb, 4, RIM, ox), BF16)
            dr[s] = jnp.zeros((8, ox), I32)

        @pl.when(jnp.logical_not(takes[2 + s]))
        def _():
            hc[:, :, s * 8 : (s + 1) * 8, :] = jnp.zeros((SUBSTEPS, nb, 8, ox), F32)
            dc[s] = jnp.zeros((oy, LANES), I32)

    pl.semaphore_wait(barrier, len(NEAR) - 1)
    start_all(depth_copies())
    send(0, order[0], 4)
    for copy in near_copies(pk_s, pk_r, pk_ss, pk_rs, lambda k, di, dj: k):
        copy.start()

    def fill_and_send(idx, carry):
        b = nth(idx)
        fill(b)
        send(0, b, 4)
        return carry

    lax.fori_loop(1, nb, fill_and_send, 0)


    g = iota((ox, 2 * ox), 0)
    n = iota((ox, 2 * ox), 1)
    d = g - jnp.where(n < ox, n, n - ox - 1)
    c_x[...] = stencil(d).astype(BF16)
    c_xs[...] = jnp.where(d == jnp.where(n < ox, 1, 0), 1.0, 0.0).astype(BF16)
    r = iota((16, 2 * ox), 0)
    n = iota((16, 2 * ox), 1)
    x = jnp.where(n < ox, n, n - ox - 1)
    for f in range(4):
        at = jnp.where(r < 8, -2 + r - 2 * f, ox + r - 8 - 2 * f)
        mine = ((r & 7) >> 1) == f
        if f < 3:
            c_xh[f] = jnp.where(mine, stencil(at - x), 0.0).astype(BF16)
        else:
            hit = mine & (at - x == jnp.where(n < ox, 1, 0))
            c_xsh[...] = jnp.where(hit, 1.0, 0.0).astype(BF16)
    r = iota((slots, slots * oy), 0)
    n = iota((slots, slots * oy), 1)
    c_e[...] = jnp.where((n >> 4) == r, 1.0, 0.0).astype(BF16)
    r = iota((slots * oy, slots), 0)
    n = iota((slots * oy, slots), 1)
    c_et[...] = jnp.where((r >> 4) == n, 1.0, 0.0).astype(BF16)

    wait_all(depth_copies())
    south, north, west, east = dr[0], dr[1], dc[0], dc[1]
    wide = jnp.concatenate([dep, east], axis=1)
    depx[0] = pltpu.roll(wide, ox + LANES - 1, 1)[:, :ox]
    wide = jnp.concatenate([west, dep], axis=1)
    depx[1] = pltpu.roll(wide, 1, 1)[:, LANES:]
    tall = jnp.concatenate([dep, north], axis=0)
    depx[2] = pltpu.roll(tall, oy + 7, 0)[:oy]
    tall = jnp.concatenate([south, dep], axis=0)
    depx[3] = pltpu.roll(tall, 1, 0)[8:]

    def wait_rims(step, b, fields):
        wait_all(rim_copies(step, b, fields))

    def place(step, b, fields):
        for f in range(fields):
            for h in range(halves):
                tmp[f, h] = hr[step, b, f, :, h * LANES : (h + 1) * LANES].astype(F32)
        for f in range(fields):
            for h in range(halves):
                for k in range(zb):
                    qs[f, b, k, h, TOP - 2 : TOP, :] = tmp[f, h, 2 * k : 2 * k + 2, :]
                    qs[f, b, k, h, TOP + oy : TOP + oy + 2, :] = tmp[
                        f, h, RIM + 2 * k : RIM + 2 * k + 2, :
                    ]

    def faces(b):
        ux[0] = nn(fld[ntr, b], c_xs[...]) + tn(hc[0, b].astype(BF16), c_xsh[...])
        for k in range(zb):
            at = b * zb + k
            rows = slice(k * oy, (k + 1) * oy)
            for h in range(halves):
                lanes = slice(h * LANES, (h + 1) * LANES)
                wet = at < depth[:, lanes]
                near_wet = [wet & (at < depx[a, :, lanes]) for a in range(4)]
                x0 = cx[b, k, h]
                y0 = qs[ntr, b, k, h, own, :]
                others = (
                    ux[0, rows, lanes],
                    ux[0, rows, ox + h * LANES : ox + (h + 1) * LANES],
                    qs[ntr, b, k, h, TOP + 1 : TOP + 1 + oy, :],
                    qs[ntr, b, k, h, TOP - 1 : TOP - 1 + oy, :],
                )
                for a in range(4):
                    mean = ((x0, y0)[a // 2] + others[a]) * (1.0 / 24.0)
                    coef[a, b, k, h] = jnp.where(near_wet[a], mean, 0.0)

    def advect(step, b):
        halo = hc[step, b].astype(BF16)
        for t in range(ntr):
            ux[t] = nn(fld[t, b], c_x[...]) + tn(halo, c_xh[t])
        for k in range(zb):
            rows = slice(k * oy, (k + 1) * oy)
            for h in range(halves):
                lanes = slice(h * LANES, (h + 1) * LANES)
                c0, c1, c2, c3 = (coef[a, b, k, h] for a in range(4))
                for t in range(ntr):
                    m2, m1, q0, p1, p2 = (
                        qs[t, b, k, h, TOP + o : TOP + o + oy, :] for o in (-2, -1, 0, 1, 2)
                    )
                    east = c0 * ux[t, rows, lanes]
                    west = c1 * ux[t, rows, ox + h * LANES : ox + (h + 1) * LANES]
                    north = c2 * (7.0 * (q0 + p1) - (m1 + p2))
                    south = c3 * (7.0 * (m1 + q0) - (m2 + p1))
                    if step == 0:
                        q0 = jnp.where((b * zb + k) < depth[:, lanes], q0, 0.0)
                    mv[t, k, h] = q0 - (east - west) - (north - south)

        @pl.when(b == 0)
        def _():
            for t in range(ntr):
                for h in range(halves):
                    lanes = slice(h * LANES, (h + 1) * LANES)
                    mv[t, 0, h] = mv[t, 0, h] + jnp.where(depth[:, lanes] > 0, forc[t, :, lanes], 0.0)

    def mixing(b, keep):
        for h in range(halves):
            lanes = slice(h * LANES, (h + 1) * LANES)
            for first in range(0, zb, RGROUP):
                acc = [[None] * ntr for _ in range(RGROUP)]
                for c in range(zb):
                    moved = [mv[t, c, h] for t in range(ntr)]
                    for r in range(RGROUP):
                        weight = mixv[b, first + r, c, :, lanes].astype(F32)
                        for t in range(ntr):
                            term = weight * moved[t]
                            acc[r][t] = term if c == 0 else acc[r][t] + term
                for r in range(RGROUP):
                    k = first + r
                    wet = (b * zb + k) < depth[:, lanes]
                    for t in range(ntr):
                        value = jnp.where(wet, acc[r][t], 0.0)
                        if keep:
                            qs[t, b, k, h, own, :] = value
                            fld[t, b, k * oy : (k + 1) * oy, lanes] = value.astype(BF16)
                        else:
                            out[t, b * zb + k, :, lanes] = value

    def force():
        for copy in near_copies(pk_s, pk_r, pk_ss, pk_rs, lambda k, di, dj: k):
            copy.wait()
        pltpu.make_async_copy(to_ocean, toc, s_toc).wait()
        mine = pk_s[4]
        chosen = [mine, pk_r[5], pk_r[3]]
        for p, di in ((3, 1), (4, -1)):
            ids = [device(di, dj) for dj in (-1, 0, 1)]
            ids = [a * ntx + b for a, b in ids]
            base = (di + 1) * 3
            e = peer_list[0, 0, p]
            got = jnp.where(e == ids[0], pk_r[base], pk_r[base + 1])
            chosen.append(jnp.where(e == ids[2], pk_r[base + 2], got))
        slot = iota((8, slots), 1)
        y = iota((oy, slots * oy), 0)
        x = iota((oy, slots * oy), 1)
        diagonal = (x & 15) == y
        total = jnp.zeros((ntr * oy, ox), F32)
        live = [jnp.where(slot < peer_count[0, 0, p], chosen[p], 0.0) for p in range(peers)]
        spread = nn(jnp.concatenate(live, axis=0).astype(BF16), c_e[...])
        for p in range(peers):
            left = jnp.concatenate(
                [
                    jnp.where(diagonal, spread[8 * p + c : 8 * p + c + 1, :], 0.0).astype(BF16)
                    for c in range(ntr)
                ],
                axis=0,
            )
            total = total + nn(left, toc[p].reshape(slots * oy, ox))
        for t in range(ntr):
            forc[t] = total[t * oy : (t + 1) * oy]

    def ret_copies():
        of = lambda k, di, dj: {1: 3, -1: 4}[di] if di != 0 else {1: 1, -1: 2}[dj]
        return near_copies(rt_s, rt_r, rt_ss, rt_rs, of)

    def give_back():
        pltpu.make_async_copy(to_atmos, toa, s_toa).wait()
        surface = out[0, 0].astype(BF16)
        y = iota((oy, slots * oy), 0)
        x = iota((oy, slots * oy), 1)
        diagonal = (x & 15) == y
        rows = []
        for p in range(peers):
            sums = jnp.where(diagonal, nt(surface, toa[p].reshape(slots * oy, ox)), 0.0)
            high = sums.astype(BF16)
            rows += [high, (sums - high.astype(F32)).astype(BF16)]
        both = nn(jnp.concatenate(rows, axis=0), c_et[...])
        both = jnp.sum(both.reshape(peers, 2 * oy, slots), axis=1)
        for p in range(peers):
            rt_s[p] = jnp.broadcast_to(both[p : p + 1], (8, slots))
        for copy in ret_copies():
            copy.start()

    def first_step(idx, carry):
        b = nth(idx)
        wait_rims(0, b, 4)
        place(0, b, ntr + 1)
        faces(b)

        @pl.when(b == 0)
        def _():
            force()

        advect(0, b)
        pltpu.make_async_copy(mix.at[0], mixv.at[b], s_mix.at[b]).wait()
        mixing(b, True)
        pack(1, b, ntr, ntr)
        send(1, b, 3)
        return carry

    lax.fori_loop(0, nb, first_step, 0)

    def second_step(b, carry):
        wait_rims(1, b, 3)
        place(1, b, ntr)
        advect(1, b)
        mixing(b, False)

        @pl.when(b == 0)
        def _():
            give_back()

        return carry

    lax.fori_loop(0, nb, second_step, 0)

    for copy in ret_copies():
        copy.wait()
    slot = iota((1, slots), 1)
    parts = []
    for k, (di, dj) in enumerate(NEAR):
        ti, tj = device(di, dj)
        value = rt_s[0] if (di, dj) == (0, 0) else rt_r[k]
        kept = slot < send_count[0, 0, ti * ntx + tj]
        parts.append(jnp.where(kept, value, 0.0))
    values = jnp.concatenate(parts, axis=1)
    high = values.astype(BF16)
    low = (values - high.astype(F32)).astype(BF16)
    landed = nt(jnp.concatenate([high, low], axis=0), oh[...])
    landed = landed[0:8] + landed[8:16]
    for r in range(surf_out.shape[0]):
        surf_out[r : r + 1, :] = landed[0:1, r * LANES : (r + 1) * LANES]


def export(tracers, surface, tracers_out, surface_out, sems):
    copies = [
        pltpu.make_async_copy(tracers.at[t], tracers_out.at[t], sems.at[t])
        for t in range(tracers.shape[0])
    ]
    copies.append(pltpu.make_async_copy(surface, surface_out, sems.at[len(copies)]))
    for copy in copies:
        copy.start()
    for copy in copies:
        copy.wait()


def body(
    nty,
    ntx,
    tracers,
    courant,
    depth_levels,
    mix_inverse,
    to_ocean,
    to_atmos,
    atm_flux,
    peer_list,
    peer_count,
    send_count,
    slot_cell,
):
    ntr, levels, oy, ox = tracers.shape
    nb, zb = mix_inverse.shape[:2]
    peers, slots = to_ocean.shape[:2]
    cells = atm_flux.shape[1] * atm_flux.shape[2]
    near = len(NEAR)
    hbm = pl.BlockSpec(memory_space=pltpu.HBM)
    vmem = pl.BlockSpec(memory_space=pltpu.VMEM)
    dma = pltpu.SemaphoreType.DMA
    scratch = [
        pltpu.VMEM((ntr + 1, nb, zb, ox // LANES, PAD, LANES), F32),
        pltpu.VMEM((nb, zb, ox // LANES, oy, LANES), F32),
        pltpu.VMEM(mix_inverse.shape, BF16),
        pltpu.VMEM(to_ocean.shape, BF16),
        pltpu.VMEM(to_atmos.shape, BF16),
        pltpu.VMEM((ntr + 1, nb, ROWS, ox), BF16),
        pltpu.VMEM((SUBSTEPS, nb, 4, 2 * RIM, ox), BF16),
        pltpu.VMEM((SUBSTEPS, nb, 4, 2 * RIM, ox), BF16),
        pltpu.VMEM((SUBSTEPS, nb, 16, ox), F32),
        pltpu.VMEM((SUBSTEPS, nb, 16, ox), F32),
        pltpu.VMEM((4, nb, zb, ox // LANES, oy, LANES), F32),
        pltpu.VMEM((ntr, ROWS, 2 * ox), F32),
        pltpu.VMEM((ntr + 1, ox // LANES, 2 * RIM, LANES), F32),
        pltpu.VMEM((ntr, zb, ox // LANES, oy, LANES), F32),
        pltpu.VMEM((ntr, oy, ox), F32),
        pltpu.VMEM((4, oy, ox), I32),
        pltpu.VMEM((2, 8, ox), I32),
        pltpu.VMEM((2, oy, LANES), I32),
        pltpu.VMEM((ox, 2 * ox), BF16),
        pltpu.VMEM((3, 16, 2 * ox), BF16),
        pltpu.VMEM((ox, 2 * ox), BF16),
        pltpu.VMEM((16, 2 * ox), BF16),
        pltpu.VMEM((4, 16, ox), BF16),
        pltpu.VMEM((slots, slots * oy), BF16),
        pltpu.VMEM((slots * oy, slots), BF16),
        pltpu.VMEM((cells, near * slots), BF16),
        pltpu.VMEM((8, cells), F32),
        pltpu.VMEM((near, 8, slots), F32),
        pltpu.VMEM((near, 8, slots), F32),
        pltpu.VMEM((peers, 8, slots), F32),
        pltpu.VMEM((near, 8, slots), F32),
        pltpu.VMEM((oy, ox), I32),
        pltpu.VMEM(atm_flux.shape, BF16),
        pltpu.VMEM(slot_cell.shape, I32),
        pltpu.SMEM(peer_list.shape, I32),
        pltpu.SMEM(peer_count.shape, I32),
        pltpu.SMEM(send_count.shape, I32),
        dma((6,)),
        dma((ox // LANES, nb)),
        dma((ox // LANES, nb)),
        dma((ox // LANES, nb)),
        dma((nb,)),
        dma,
        dma,
        dma((SUBSTEPS, 2, nb)),
        dma((SUBSTEPS, 2, nb)),
        dma((SUBSTEPS, 2, nb)),
        dma((SUBSTEPS, 2, nb)),
        dma((4,)),
        dma((4,)),
        dma((near,)),
        dma((near,)),
        dma((near,)),
        dma((near,)),
    ]
    results = pl.pallas_call(
        functools.partial(kernel, nty, ntx),
        out_shape=(
            pltpu.VMEM(tracers.shape, F32),
            pltpu.VMEM(atm_flux.shape[1:], F32),
        ),
        in_specs=[hbm] * 11,
        out_specs=(vmem, vmem),
        scratch_shapes=scratch,
        compiler_params=pltpu.CompilerParams(
            collective_id=0, has_side_effects=True, vmem_limit_bytes=62464 * 1024
        ),
        cost_estimate=pl.CostEstimate(flops=10**9, bytes_accessed=26 * 10**6, transcendentals=0),
        name="interval",
    )(
        tracers,
        courant,
        mix_inverse,
        to_ocean,
        to_atmos,
        depth_levels,
        atm_flux,
        slot_cell,
        peer_list,
        peer_count,
        send_count,
    )
    anywhere = pl.BlockSpec(memory_space=pl.ANY)
    return pl.pallas_call(
        export,
        out_shape=(
            jax.ShapeDtypeStruct(tracers.shape, F32),
            jax.ShapeDtypeStruct(atm_flux.shape[1:], F32),
        ),
        in_specs=[pl.BlockSpec(memory_space=pl.ANY)] * 2,
        out_specs=(anywhere, anywhere),
        scratch_shapes=[dma((ntr + 1,))],
        compiler_params=pltpu.CompilerParams(has_side_effects=True, vmem_limit_bytes=1024 * 1024),
        name="export",
    )(*results)


def solution(mesh):
    in_specs = (
        P(None, None, "ty", "tx"),
        P(None, None, "ty", "tx"),
        P("ty", "tx"),
        P(None, None, None, "ty", "tx"),
        P(None, None, "ty", "tx"),
        P(None, None, "ty", "tx"),
        P(None, "ty", "tx"),
        P("ty", "tx", None),
        P("ty", "tx", None),
        P("ty", "tx", None),
        P("ty", "tx", None, None),
    )
    out_specs = (P(None, None, "ty", "tx"), P("ty", "tx"))
    part = functools.partial(body, mesh.shape["ty"], mesh.shape["tx"])
    return jax.shard_map(part, mesh=mesh, in_specs=in_specs, out_specs=out_specs, check_vma=False)
```

```python
import functools

import jax
import jax.numpy as jnp
from jax import lax
from jax.experimental import pallas as pl
from jax.experimental.pallas import tpu as pltpu
from jax.sharding import PartitionSpec as P

MESH = pl.DeviceIdType.MESH
F32 = jnp.float32
BF16 = jnp.bfloat16
I32 = jnp.int32
SUBSTEPS = 2
LANES = 128
RIM = 32
ROWS = 256
RGROUP = 3
PAD = 32
TOP = 8
NEAR = tuple((di, dj) for di in (-1, 0, 1) for dj in (-1, 0, 1))


def iota(shape, dim):
    return lax.broadcasted_iota(I32, shape, dim)


def stencil(d):
    return jnp.where((d == 0) | (d == 1), 7.0, jnp.where((d == -1) | (d == 2), -1.0, 0.0))


def nn(a, b):
    return jnp.dot(a, b, preferred_element_type=F32)


def nt(a, b):
    return lax.dot_general(a, b, (((1,), (1,)), ((), ())), preferred_element_type=F32)


def tn(a, b):
    return lax.dot_general(a, b, (((0,), (0,)), ((), ())), preferred_element_type=F32)


def kernel(
    nty,
    ntx,
    tracers,
    courant,
    mix,
    to_ocean,
    to_atmos,
    depth_in,
    atm_in,
    slot_cell_in,
    peer_list_in,
    peer_count_in,
    send_count_in,
    out,
    surf_out,
    qs,
    cx,
    mixv,
    toc,
    toa,
    fld,
    sr,
    hr,
    sc,
    hc,
    coef,
    ux,
    tmp,
    mv,
    forc,
    depx,
    dr,
    dc,
    c_x,
    c_xh,
    c_xs,
    c_xsh,
    c_selc,
    c_e,
    c_et,
    oh,
    flat,
    pk_s,
    pk_r,
    rt_s,
    rt_r,
    depth,
    atm,
    slot_cell,
    peer_list,
    peer_count,
    send_count,
    s_in,
    s_tr,
    s_cx,
    s_cy,
    s_mix,
    s_toc,
    s_toa,
    row_ss,
    row_rs,
    col_ss,
    col_rs,
    dep_ss,
    dep_rs,
    pk_ss,
    pk_rs,
    rt_ss,
    rt_rs,
):
    nb, zb = mix.shape[:2]
    ntr, _, oy, ox = tracers.shape
    halves = ox // LANES
    own = slice(TOP, TOP + oy)
    peers, slots = to_ocean.shape[0], to_ocean.shape[1]
    i = lax.axis_index("ty")
    j = lax.axis_index("tx")

    def device(di, dj):
        return (lax.rem(i + di + nty, nty), lax.rem(j + dj + ntx, ntx))

    barrier = pltpu.get_barrier_semaphore()
    for di, dj in NEAR:
        if (di, dj) != (0, 0):
            pl.semaphore_signal(barrier, inc=1, device_id=device(di, dj), device_id_type=MESH)

    small = [
        pltpu.make_async_copy(source, target, s_in.at[k])
        for k, (source, target) in enumerate(
            (
                (depth_in, depth),
                (slot_cell_in, slot_cell),
                (atm_in, atm),
                (peer_list_in, peer_list),
                (peer_count_in, peer_count),
                (send_count_in, send_count),
            )
        )
    ]
    order = (1, 0) + tuple(range(2, nb))

    def nth(idx):
        return jnp.where(idx < 2, 1 - idx, idx)

    def loads(b, first):
        made = []
        for h in range(halves):
            lanes = pl.ds(h * LANES, LANES)
            levels = pl.ds(first, zb)
            made += [
                pltpu.make_async_copy(
                    tracers.at[:, levels, :, lanes],
                    qs.at[pl.ds(0, ntr), b, :, h, pl.ds(TOP, oy)],
                    s_tr.at[h, b],
                ),
                pltpu.make_async_copy(
                    courant.at[0, levels, :, lanes], cx.at[b, :, h], s_cx.at[h, b]
                ),
                pltpu.make_async_copy(
                    courant.at[1, levels, :, lanes],
                    qs.at[ntr, b, :, h, pl.ds(TOP, oy)],
                    s_cy.at[h, b],
                ),
            ]
        return made

    for copy in small:
        copy.start()
    for b in order:
        for copy in loads(b, b * zb):
            copy.start()
    pltpu.make_async_copy(mix.at[order[0]], mixv.at[order[0]], s_mix.at[order[0]]).start()
    pltpu.make_async_copy(to_ocean, toc, s_toc).start()
    for b in order[1:]:
        pltpu.make_async_copy(mix.at[b], mixv.at[b], s_mix.at[b]).start()
    pltpu.make_async_copy(to_atmos, toa, s_toa).start()

    r = iota((16, ox), 0)
    n = iota((16, ox), 1)
    for f in range(4):
        at = jnp.where(r < 8, ox - 2 + r - 2 * f, r - 8 - 2 * f)
        mine = ((r & 7) >> 1) == f
        hit = mine & (at == n)
        c_selc[f] = jnp.where(hit, 1.0, 0.0).astype(BF16)
    sends = (i < nty - 1, i > 0, j < ntx - 1, j > 0)
    takes = (i > 0, i < nty - 1, j > 0, j < ntx - 1)

    def start_all(copies):
        for copy, mine in zip(copies, sends):
            pl.when(mine)(copy.start)

    def wait_all(copies):
        for copy, mine, theirs in zip(copies, sends, takes):
            pl.when(mine)(copy.wait_send)
            pl.when(theirs)(copy.wait_recv)

    def depth_copies():
        return (
            pltpu.make_async_remote_copy(
                depth.at[pl.ds(oy - 8, 8)], dr.at[0], dep_ss.at[0], dep_rs.at[0],
                device_id=device(1, 0), device_id_type=MESH,
            ),
            pltpu.make_async_remote_copy(
                depth.at[pl.ds(0, 8)], dr.at[1], dep_ss.at[1], dep_rs.at[1],
                device_id=device(-1, 0), device_id_type=MESH,
            ),
            pltpu.make_async_remote_copy(
                depth.at[:, pl.ds(ox - LANES, LANES)], dc.at[0], dep_ss.at[2], dep_rs.at[2],
                device_id=device(0, 1), device_id_type=MESH,
            ),
            pltpu.make_async_remote_copy(
                depth.at[:, pl.ds(0, LANES)], dc.at[1], dep_ss.at[3], dep_rs.at[3],
                device_id=device(0, -1), device_id_type=MESH,
            ),
        )

    def near_copies(source, target, ss, rs, of):
        made = []
        for k, (di, dj) in enumerate(NEAR):
            if (di, dj) != (0, 0):
                made.append(
                    pltpu.make_async_remote_copy(
                        source.at[of(k, di, dj)], target.at[len(NEAR) - 1 - k], ss.at[k],
                        rs.at[len(NEAR) - 1 - k], device_id=device(di, dj), device_id_type=MESH,
                    )
                )
        return made

    def rim_copies(step, b, fields):
        rows = [
            pltpu.make_async_remote_copy(
                sr.at[step, b, pl.ds(0, fields), pl.ds(s * RIM, RIM)],
                hr.at[step, b, pl.ds(0, fields), pl.ds(s * RIM, RIM)],
                row_ss.at[step, s, b], row_rs.at[step, s, b],
                device_id=device(1 - 2 * s, 0), device_id_type=MESH,
            )
            for s in range(2)
        ]
        cols = [
            pltpu.make_async_remote_copy(
                sc.at[step, b, pl.ds(s * 8, 8)],
                hc.at[step, b, pl.ds(s * 8, 8)],
                col_ss.at[step, s, b], col_rs.at[step, s, b],
                device_id=device(0, 1 - 2 * s), device_id_type=MESH,
            )
            for s in range(2)
        ]
        return rows + cols

    small[0].wait()
    dep = depth[...]

    def pack(step, b, row_fields, col_fields):
        for f in range(row_fields):
            for h in range(halves):
                for k in range(zb):
                    tmp[f, h, 2 * k : 2 * k + 2, :] = qs[f, b, k, h, TOP + oy - 2 : TOP + oy, :]
                    tmp[f, h, RIM + 2 * k : RIM + 2 * k + 2, :] = qs[f, b, k, h, TOP : TOP + 2, :]
                sr[step, b, f, :, h * LANES : (h + 1) * LANES] = tmp[f, h].astype(BF16)
        cols = nt(c_selc[0], fld[0, b])
        for f in range(1, col_fields):
            cols = cols + nt(c_selc[f], fld[f, b])
        sc[step, b] = cols

    def send(step, b, fields):
        start_all(rim_copies(step, b, fields))

    def fill(b):
        for copy in loads(b, 0):
            copy.wait()
        for h in range(halves):
            lanes = slice(h * LANES, (h + 1) * LANES)
            for f in range(ntr + 1):
                value = cx[b, :, h] if f == ntr else qs[f, b, :, h, own, :]
                fld[f, b, 0 : zb * oy, lanes] = value.reshape(zb * oy, LANES).astype(BF16)
        for f in range(ntr + 1):
            fld[f, b, zb * oy :, :] = jnp.zeros((ROWS - zb * oy, ox), BF16)
        pack(0, b, ntr + 1, ntr + 1)

    tmp[...] = jnp.zeros_like(tmp)
    for copy in small[1:]:
        copy.wait()

    cells = iota((oh.shape[0], slots), 0)
    for k, (di, dj) in enumerate(NEAR):
        ti, tj = device(di, dj)
        row = slot_cell[0, 0, pl.ds(ti * ntx + tj, 1), :]
        oh[:, k * slots : (k + 1) * slots] = jnp.where(cells == row, 1.0, 0.0).astype(BF16)
    flux = atm[...].astype(F32)
    flat[...] = jnp.zeros_like(flat)
    for c in range(flux.shape[0]):
        for r in range(flux.shape[1]):
            flat[c : c + 1, r * LANES : (r + 1) * LANES] = flux[c, r : r + 1, :]
    picks = nn(flat[...].astype(BF16), oh[...])
    for k in range(len(NEAR)):
        pk_s[k] = picks[:, k * slots : (k + 1) * slots]
    pl.semaphore_wait(barrier, len(NEAR) - 1)
    for copy in near_copies(pk_s, pk_r, pk_ss, pk_rs, lambda k, di, dj: k):
        copy.start()
    fill(order[0])

    for s in range(2):
        @pl.when(jnp.logical_not(takes[s]))
        def _():
            hr[:, :, :, s * RIM : (s + 1) * RIM, :] = jnp.zeros((SUBSTEPS, nb, 4, RIM, ox), BF16)
            dr[s] = jnp.zeros((8, ox), I32)

        @pl.when(jnp.logical_not(takes[2 + s]))
        def _():
            hc[:, :, s * 8 : (s + 1) * 8, :] = jnp.zeros((SUBSTEPS, nb, 8, ox), F32)
            dc[s] = jnp.zeros((oy, LANES), I32)

    start_all(depth_copies())
    send(0, order[0], 4)

    def fill_and_send(idx, carry):
        b = nth(idx)
        fill(b)
        send(0, b, 4)
        return carry

    lax.fori_loop(1, nb, fill_and_send, 0)


    g = iota((ox, 2 * ox), 0)
    n = iota((ox, 2 * ox), 1)
    d = g - jnp.where(n < ox, n, n - ox - 1)
    c_x[...] = stencil(d).astype(BF16)
    c_xs[...] = jnp.where(d == jnp.where(n < ox, 1, 0), 1.0, 0.0).astype(BF16)
    r = iota((16, 2 * ox), 0)
    n = iota((16, 2 * ox), 1)
    x = jnp.where(n < ox, n, n - ox - 1)
    for f in range(4):
        at = jnp.where(r < 8, -2 + r - 2 * f, ox + r - 8 - 2 * f)
        mine = ((r & 7) >> 1) == f
        if f < 3:
            c_xh[f] = jnp.where(mine, stencil(at - x), 0.0).astype(BF16)
        else:
            hit = mine & (at - x == jnp.where(n < ox, 1, 0))
            c_xsh[...] = jnp.where(hit, 1.0, 0.0).astype(BF16)
    r = iota((slots, slots * oy), 0)
    n = iota((slots, slots * oy), 1)
    c_e[...] = jnp.where((n >> 4) == r, 1.0, 0.0).astype(BF16)
    r = iota((slots * oy, slots), 0)
    n = iota((slots * oy, slots), 1)
    c_et[...] = jnp.where((r >> 4) == n, 1.0, 0.0).astype(BF16)

    wait_all(depth_copies())
    south, north, west, east = dr[0], dr[1], dc[0], dc[1]
    wide = jnp.concatenate([dep, east], axis=1)
    depx[0] = pltpu.roll(wide, ox + LANES - 1, 1)[:, :ox]
    wide = jnp.concatenate([west, dep], axis=1)
    depx[1] = pltpu.roll(wide, 1, 1)[:, LANES:]
    tall = jnp.concatenate([dep, north], axis=0)
    depx[2] = pltpu.roll(tall, oy + 7, 0)[:oy]
    tall = jnp.concatenate([south, dep], axis=0)
    depx[3] = pltpu.roll(tall, 1, 0)[8:]
    for a in range(4):
        depx[a] = jnp.minimum(depx[a], dep)

    def wait_rims(step, b, fields):
        wait_all(rim_copies(step, b, fields))

    def place(step, b, fields):
        for f in range(fields):
            for h in range(halves):
                tmp[f, h] = hr[step, b, f, :, h * LANES : (h + 1) * LANES].astype(F32)
        for f in range(fields):
            for h in range(halves):
                for k in range(zb):
                    qs[f, b, k, h, TOP - 2 : TOP, :] = tmp[f, h, 2 * k : 2 * k + 2, :]
                    qs[f, b, k, h, TOP + oy : TOP + oy + 2, :] = tmp[
                        f, h, RIM + 2 * k : RIM + 2 * k + 2, :
                    ]

    def faces(b):
        ux[0] = nn(fld[ntr, b], c_xs[...]) + tn(hc[0, b].astype(BF16), c_xsh[...])
        for k in range(zb):
            at = b * zb + k
            rows = slice(k * oy, (k + 1) * oy)
            for h in range(halves):
                lanes = slice(h * LANES, (h + 1) * LANES)
                near_wet = [at < depx[a, :, lanes] for a in range(4)]
                x0 = cx[b, k, h]
                y0 = qs[ntr, b, k, h, own, :]
                others = (
                    ux[0, rows, lanes],
                    ux[0, rows, ox + h * LANES : ox + (h + 1) * LANES],
                    qs[ntr, b, k, h, TOP + 1 : TOP + 1 + oy, :],
                    qs[ntr, b, k, h, TOP - 1 : TOP - 1 + oy, :],
                )
                for a in range(4):
                    mean = ((x0, y0)[a // 2] + others[a]) * (1.0 / 24.0)
                    coef[a, b, k, h] = jnp.where(near_wet[a], mean, 0.0)

    def advect(step, b):
        halo = hc[step, b].astype(BF16)
        for t in range(ntr):
            ux[t] = nn(fld[t, b], c_x[...]) + tn(halo, c_xh[t])
        for k in range(zb):
            rows = slice(k * oy, (k + 1) * oy)
            for h in range(halves):
                lanes = slice(h * LANES, (h + 1) * LANES)
                c0, c1, c2, c3 = (coef[a, b, k, h] for a in range(4))
                for t in range(ntr):
                    m2, m1, q0, p1, p2 = (
                        qs[t, b, k, h, TOP + o : TOP + o + oy, :] for o in (-2, -1, 0, 1, 2)
                    )
                    east = c0 * ux[t, rows, lanes]
                    west = c1 * ux[t, rows, ox + h * LANES : ox + (h + 1) * LANES]
                    north = c2 * (7.0 * (q0 + p1) - (m1 + p2))
                    south = c3 * (7.0 * (m1 + q0) - (m2 + p1))
                    if step == 0:
                        q0 = jnp.where((b * zb + k) < depth[:, lanes], q0, 0.0)
                    mv[t, k, h] = q0 - (east - west) - (north - south)

        @pl.when(b == 0)
        def _():
            for t in range(ntr):
                for h in range(halves):
                    lanes = slice(h * LANES, (h + 1) * LANES)
                    mv[t, 0, h] = mv[t, 0, h] + jnp.where(depth[:, lanes] > 0, forc[t, :, lanes], 0.0)

    def mixing(b, keep):
        for h in range(halves):
            lanes = slice(h * LANES, (h + 1) * LANES)
            for first in range(0, zb, RGROUP):
                acc = [[None] * ntr for _ in range(RGROUP)]
                for c in range(zb):
                    moved = [mv[t, c, h] for t in range(ntr)]
                    for r in range(RGROUP):
                        weight = mixv[b, first + r, c, :, lanes].astype(F32)
                        for t in range(ntr):
                            term = weight * moved[t]
                            acc[r][t] = term if c == 0 else acc[r][t] + term
                for r in range(RGROUP):
                    k = first + r
                    wet = (b * zb + k) < depth[:, lanes]
                    for t in range(ntr):
                        value = jnp.where(wet, acc[r][t], 0.0)
                        if keep:
                            qs[t, b, k, h, own, :] = value
                            fld[t, b, k * oy : (k + 1) * oy, lanes] = value.astype(BF16)
                        else:
                            out[t, b * zb + k, :, lanes] = value

    def force():
        for copy in near_copies(pk_s, pk_r, pk_ss, pk_rs, lambda k, di, dj: k):
            copy.wait()
        pltpu.make_async_copy(to_ocean, toc, s_toc).wait()
        mine = pk_s[4]
        chosen = [mine, pk_r[5], pk_r[3]]
        for p, di in ((3, 1), (4, -1)):
            ids = [device(di, dj) for dj in (-1, 0, 1)]
            ids = [a * ntx + b for a, b in ids]
            base = (di + 1) * 3
            e = peer_list[0, 0, p]
            got = jnp.where(e == ids[0], pk_r[base], pk_r[base + 1])
            chosen.append(jnp.where(e == ids[2], pk_r[base + 2], got))
        slot = iota((8, slots), 1)
        y = iota((oy, slots * oy), 0)
        x = iota((oy, slots * oy), 1)
        diagonal = (x & 15) == y
        total = jnp.zeros((ntr * oy, ox), F32)
        live = [jnp.where(slot < peer_count[0, 0, p], chosen[p], 0.0) for p in range(peers)]
        spread = nn(jnp.concatenate(live, axis=0).astype(BF16), c_e[...])
        for p in range(peers):
            left = jnp.concatenate(
                [
                    jnp.where(diagonal, spread[8 * p + c : 8 * p + c + 1, :], 0.0).astype(BF16)
                    for c in range(ntr)
                ],
                axis=0,
            )
            total = total + nn(left, toc[p].reshape(slots * oy, ox))
        for t in range(ntr):
            forc[t] = total[t * oy : (t + 1) * oy]

    def ret_copies():
        of = lambda k, di, dj: {1: 3, -1: 4}[di] if di != 0 else {1: 1, -1: 2}[dj]
        return near_copies(rt_s, rt_r, rt_ss, rt_rs, of)

    def give_back():
        pltpu.make_async_copy(to_atmos, toa, s_toa).wait()
        surface = out[0, 0].astype(BF16)
        y = iota((oy, slots * oy), 0)
        x = iota((oy, slots * oy), 1)
        diagonal = (x & 15) == y
        rows = []
        for p in range(peers):
            sums = jnp.where(diagonal, nt(surface, toa[p].reshape(slots * oy, ox)), 0.0)
            high = sums.astype(BF16)
            rows += [high, (sums - high.astype(F32)).astype(BF16)]
        both = nn(jnp.concatenate(rows, axis=0), c_et[...])
        both = jnp.sum(both.reshape(peers, 2 * oy, slots), axis=1)
        for p in range(peers):
            rt_s[p] = jnp.broadcast_to(both[p : p + 1], (8, slots))
        for copy in ret_copies():
            copy.start()

    def first_step(idx, carry):
        b = nth(idx)
        wait_rims(0, b, 4)
        place(0, b, ntr + 1)
        faces(b)

        @pl.when(b == 0)
        def _():
            force()

        advect(0, b)
        pltpu.make_async_copy(mix.at[0], mixv.at[b], s_mix.at[b]).wait()
        mixing(b, True)
        pack(1, b, ntr, ntr)
        send(1, b, 3)
        return carry

    lax.fori_loop(0, nb, first_step, 0)

    def second_step(b, carry):
        wait_rims(1, b, 3)
        place(1, b, ntr)
        advect(1, b)
        mixing(b, False)

        @pl.when(b == 0)
        def _():
            give_back()

        return carry

    lax.fori_loop(0, nb, second_step, 0)

    for copy in ret_copies():
        copy.wait()
    slot = iota((1, slots), 1)
    parts = []
    for k, (di, dj) in enumerate(NEAR):
        ti, tj = device(di, dj)
        value = rt_s[0] if (di, dj) == (0, 0) else rt_r[k]
        kept = slot < send_count[0, 0, ti * ntx + tj]
        parts.append(jnp.where(kept, value, 0.0))
    values = jnp.concatenate(parts, axis=1)
    high = values.astype(BF16)
    low = (values - high.astype(F32)).astype(BF16)
    landed = nt(jnp.concatenate([high, low], axis=0), oh[...])
    landed = landed[0:8] + landed[8:16]
    for r in range(surf_out.shape[0]):
        surf_out[r : r + 1, :] = landed[0:1, r * LANES : (r + 1) * LANES]


def export(tracers, surface, tracers_out, surface_out, sems):
    copies = [
        pltpu.make_async_copy(tracers.at[t], tracers_out.at[t], sems.at[t])
        for t in range(tracers.shape[0])
    ]
    copies.append(pltpu.make_async_copy(surface, surface_out, sems.at[len(copies)]))
    for copy in copies:
        copy.start()
    for copy in copies:
        copy.wait()


def body(
    nty,
    ntx,
    tracers,
    courant,
    depth_levels,
    mix_inverse,
    to_ocean,
    to_atmos,
    atm_flux,
    peer_list,
    peer_count,
    send_count,
    slot_cell,
):
    ntr, levels, oy, ox = tracers.shape
    nb, zb = mix_inverse.shape[:2]
    peers, slots = to_ocean.shape[:2]
    cells = atm_flux.shape[1] * atm_flux.shape[2]
    near = len(NEAR)
    hbm = pl.BlockSpec(memory_space=pltpu.HBM)
    vmem = pl.BlockSpec(memory_space=pltpu.VMEM)
    dma = pltpu.SemaphoreType.DMA
    scratch = [
        pltpu.VMEM((ntr + 1, nb, zb, ox // LANES, PAD, LANES), F32),
        pltpu.VMEM((nb, zb, ox // LANES, oy, LANES), F32),
        pltpu.VMEM(mix_inverse.shape, BF16),
        pltpu.VMEM(to_ocean.shape, BF16),
        pltpu.VMEM(to_atmos.shape, BF16),
        pltpu.VMEM((ntr + 1, nb, ROWS, ox), BF16),
        pltpu.VMEM((SUBSTEPS, nb, 4, 2 * RIM, ox), BF16),
        pltpu.VMEM((SUBSTEPS, nb, 4, 2 * RIM, ox), BF16),
        pltpu.VMEM((SUBSTEPS, nb, 16, ox), F32),
        pltpu.VMEM((SUBSTEPS, nb, 16, ox), F32),
        pltpu.VMEM((4, nb, zb, ox // LANES, oy, LANES), F32),
        pltpu.VMEM((ntr, ROWS, 2 * ox), F32),
        pltpu.VMEM((ntr + 1, ox // LANES, 2 * RIM, LANES), F32),
        pltpu.VMEM((ntr, zb, ox // LANES, oy, LANES), F32),
        pltpu.VMEM((ntr, oy, ox), F32),
        pltpu.VMEM((4, oy, ox), I32),
        pltpu.VMEM((2, 8, ox), I32),
        pltpu.VMEM((2, oy, LANES), I32),
        pltpu.VMEM((ox, 2 * ox), BF16),
        pltpu.VMEM((3, 16, 2 * ox), BF16),
        pltpu.VMEM((ox, 2 * ox), BF16),
        pltpu.VMEM((16, 2 * ox), BF16),
        pltpu.VMEM((4, 16, ox), BF16),
        pltpu.VMEM((slots, slots * oy), BF16),
        pltpu.VMEM((slots * oy, slots), BF16),
        pltpu.VMEM((cells, near * slots), BF16),
        pltpu.VMEM((8, cells), F32),
        pltpu.VMEM((near, 8, slots), F32),
        pltpu.VMEM((near, 8, slots), F32),
        pltpu.VMEM((peers, 8, slots), F32),
        pltpu.VMEM((near, 8, slots), F32),
        pltpu.VMEM((oy, ox), I32),
        pltpu.VMEM(atm_flux.shape, BF16),
        pltpu.VMEM(slot_cell.shape, I32),
        pltpu.SMEM(peer_list.shape, I32),
        pltpu.SMEM(peer_count.shape, I32),
        pltpu.SMEM(send_count.shape, I32),
        dma((6,)),
        dma((ox // LANES, nb)),
        dma((ox // LANES, nb)),
        dma((ox // LANES, nb)),
        dma((nb,)),
        dma,
        dma,
        dma((SUBSTEPS, 2, nb)),
        dma((SUBSTEPS, 2, nb)),
        dma((SUBSTEPS, 2, nb)),
        dma((SUBSTEPS, 2, nb)),
        dma((4,)),
        dma((4,)),
        dma((near,)),
        dma((near,)),
        dma((near,)),
        dma((near,)),
    ]
    results = pl.pallas_call(
        functools.partial(kernel, nty, ntx),
        out_shape=(
            pltpu.VMEM(tracers.shape, F32),
            pltpu.VMEM(atm_flux.shape[1:], F32),
        ),
        in_specs=[hbm] * 11,
        out_specs=(vmem, vmem),
        scratch_shapes=scratch,
        compiler_params=pltpu.CompilerParams(
            collective_id=0, has_side_effects=True, vmem_limit_bytes=62464 * 1024
        ),
        cost_estimate=pl.CostEstimate(flops=10**9, bytes_accessed=26 * 10**6, transcendentals=0),
        name="interval",
    )(
        tracers,
        courant,
        mix_inverse,
        to_ocean,
        to_atmos,
        depth_levels,
        atm_flux,
        slot_cell,
        peer_list,
        peer_count,
        send_count,
    )
    anywhere = pl.BlockSpec(memory_space=pl.ANY)
    return pl.pallas_call(
        export,
        out_shape=(
            jax.ShapeDtypeStruct(tracers.shape, F32),
            jax.ShapeDtypeStruct(atm_flux.shape[1:], F32),
        ),
        in_specs=[pl.BlockSpec(memory_space=pl.ANY)] * 2,
        out_specs=(anywhere, anywhere),
        scratch_shapes=[dma((ntr + 1,))],
        compiler_params=pltpu.CompilerParams(has_side_effects=True, vmem_limit_bytes=1024 * 1024),
        name="export",
    )(*results)


def solution(mesh):
    in_specs = (
        P(None, None, "ty", "tx"),
        P(None, None, "ty", "tx"),
        P("ty", "tx"),
        P(None, None, None, "ty", "tx"),
        P(None, None, "ty", "tx"),
        P(None, None, "ty", "tx"),
        P(None, "ty", "tx"),
        P("ty", "tx", None),
        P("ty", "tx", None),
        P("ty", "tx", None),
        P("ty", "tx", None, None),
    )
    out_specs = (P(None, None, "ty", "tx"), P("ty", "tx"))
    part = functools.partial(body, mesh.shape["ty"], mesh.shape["tx"])
    return jax.shard_map(part, mesh=mesh, in_specs=in_specs, out_specs=out_specs, check_vma=False)
```
